256 devices in a mesh: ctx: 64 (over x_hi, y, z), head: 4 (over x_lo, core).
Axes of the slice: x: 4 (x_hi: 2, x_lo: 2; x = x_hi * 2 + x_lo), y: 4, z: 8, core: 2. Of those that a mesh axis runs over, the one named last changes fastest.
Arguments:
- queries: bfloat16 [16384, 6144], P(('ctx', 'head')), may hold values from -42 to 42
- key_head_columns: bfloat16 [16384, 512], P(('ctx', 'head')), may hold values from -4 to 4
- value_head_columns: bfloat16 [16384, 512], P(('ctx', 'head')), may hold values from -6 to 6
- output_gradient: bfloat16 [16384, 6144], P(('ctx', 'head')), may hold values from -6 to 6
- file_starts: int32 [33], replicated, may hold values from 0 to 16320, as said below
- file_imports: int32 [33, 4], replicated, may hold values from -1 to 32, as said below
- header_lens: int32 [33], replicated, may hold values from 16 to 64
Outputs:
- grad_queries: float32 [16384, 6144], P(('ctx', 'head'))
- key_gradient: float32 [16384, 512], P(('ctx', 'head'))
- value_gradient: float32 [16384, 512], P(('ctx', 'head'))
The draws below stay inside these ranges and needn't reach their ends.
Inputs may be any that keep to these rules, and one draw needn't show every extreme that they name: `file_starts`: Increasing; the first is 0 and the last is 16320; each is a multiple of 64; no two lie in the same aligned block of 256 tokens; each file has 64 tokens or more. `file_imports`: each row lists distinct files other than its own, then -1 in the unused places; file 0 imports nothing.
All inputs are finite; a program needn't handle non-finite values.
Results may differ from the reference program's by a relative error of at most 0.004.
Values may be sent and summed in bfloat16 or wider, within the bound.
A program may use at most 64 MiB of HBM per device.

```python
import math
import jax
import jax.numpy as jnp
from jax import lax

QUERY_HEADS = 48
KEY_VALUE_HEADS = 4
HEAD_WIDTH = 128
TOK_DEV = 256
WIN = 1024
HDR = 64
IMPORTS = 4
PACKED_TOKENS = 16384
FILES = 33


def shared_pair(key):
    base = jax.random.fold_in(key, 11)
    leading_key = jax.random.fold_in(base, 1)
    second_key = jax.random.fold_in(base, 2)
    unpadded_keys = jnp.clip(jax.random.normal(leading_key, (PACKED_TOKENS, KEY_VALUE_HEADS * HEAD_WIDTH), jnp.float32), -4.0, 4.0)
    query_raw = jnp.clip(jax.random.normal(second_key, (PACKED_TOKENS, QUERY_HEADS * HEAD_WIDTH), jnp.float32), -4.0, 4.0)
    return (query_raw, unpadded_keys)


def draw_queries(key, part):
    return shared_pair(key)[0].astype(jnp.bfloat16)


def draw_key_head_columns(key, part):
    return shared_pair(key)[1].astype(jnp.bfloat16)


def draw_file_starts(key, part):
    base = jax.random.fold_in(key, 21)
    shards = PACKED_TOKENS // TOK_DEV
    order = jax.random.permutation(jax.random.fold_in(base, 1), shards - 2) + 1
    chosen = jnp.sort(order[:FILES - 2])
    within = jax.random.randint(jax.random.fold_in(base, 2), (FILES - 2,), 0, TOK_DEV // HDR) * HDR
    middle = (chosen * TOK_DEV + within).astype(jnp.int32)
    last_start = jnp.full((1,), PACKED_TOKENS - HDR, jnp.int32)
    return jnp.concatenate([jnp.zeros((1,), jnp.int32), middle, last_start]).astype(jnp.int32)


def draw_file_imports(key, part):
    base = jax.random.fold_in(key, 31)
    files = jnp.arange(FILES, dtype=jnp.int32)
    favour = jax.random.randint(jax.random.fold_in(base, 1), (FILES,), 0, 8)
    noise = jax.random.randint(jax.random.fold_in(base, 2), (FILES, FILES), 0, 32)
    scores = (noise + favour[None, :] * favour[None, :]) * FILES + files[None, :]
    scores = jnp.where(files[:, None] == files[None, :], -1, scores)
    scores = jnp.where((files[:, None] == FILES - 2) & (files[None, :] == FILES - 1), 1000 * FILES, scores)
    picked = lax.top_k(scores, IMPORTS)[1].astype(jnp.int32)
    counts = jax.random.randint(jax.random.fold_in(base, 3), (FILES,), 0, IMPORTS + 1)
    counts = jnp.where(files == 0, 0, counts)
    counts = jnp.where(files == FILES - 2, jnp.maximum(counts, 1), counts)
    counts = jnp.where(files == FILES - 1, IMPORTS, counts)
    places = jnp.arange(IMPORTS, dtype=jnp.int32)
    return jnp.where(places[None, :] < counts[:, None], picked, -1).astype(jnp.int32)


def place_ends(result, rng, smallest, high):
    index_at = [jax.random.randint(jax.random.fold_in(rng, axis), (), 0, length) for axis, length in enumerate(result.shape)]
    main_axis = result.shape.index(max(result.shape))
    neighbour = index_at[:main_axis] + [(index_at[main_axis] + 1) % result.shape[main_axis]] + index_at[main_axis + 1:]
    return result.at[tuple(index_at)].set(smallest).at[tuple(neighbour)].set(high)


def block_scale(rng, shape, cuts, smallest, high):
    factor_of = 1.0
    for axis_at, blocks in cuts:
        draws = jax.random.uniform(jax.random.fold_in(jax.random.fold_in(rng, 6), axis_at), (blocks,), jnp.float32, smallest / len(cuts), high / len(cuts))
        factor_of = factor_of * jnp.repeat(jnp.exp(draws), shape[axis_at] // blocks).reshape((-1,) + (1,) * (len(shape) - 1 - axis_at))
    return factor_of


def gaussian(key, extent, width, most, cuts=(), kind=jnp.bfloat16):
    gain = block_scale(key, extent, cuts, -0.22, 0.18) if cuts else 1.0
    values = jax.random.normal(key, extent, jnp.float32) * width * gain
    return jnp.minimum(jnp.maximum(values, -most), most).astype(kind)


def setup_inputs(seed: int = 0) -> dict:
    seeds = jax.random.split(jax.random.key(seed), 8)
    queries = draw_queries(jax.random.fold_in(seeds[7], 71), 0)
    key_head_columns = draw_key_head_columns(jax.random.fold_in(seeds[7], 71), 0)
    value_head_columns = gaussian(seeds[2], (PACKED_TOKENS, KEY_VALUE_HEADS * HEAD_WIDTH), 1.0, 6.0, ((0, 256),))
    output_gradient = gaussian(seeds[3], (PACKED_TOKENS, QUERY_HEADS * HEAD_WIDTH), 1.0, 6.0, ((0, 256),))
    file_starts = draw_file_starts(jax.random.fold_in(seeds[7], 71), 0)
    file_imports = draw_file_imports(jax.random.fold_in(seeds[7], 71), 0)
    header_lens = place_ends(jax.random.randint(seeds[6], (FILES,), HDR // 4, HDR + 1), jax.random.fold_in(seeds[6], 1), HDR // 4, HDR).astype(jnp.int32)
    return dict(queries=queries, key_head_columns=key_head_columns, value_head_columns=value_head_columns, output_gradient=output_gradient, file_starts=file_starts, file_imports=file_imports, header_lens=header_lens)


def local_files(file_starts, file_imports, header_lens, offset_base, span_rows):
    places = offset_base + jnp.arange(span_rows, dtype=jnp.int32)
    before = file_starts[None, :] <= places[:, None]
    file_of = lax.optimization_barrier(jnp.sum(before.astype(jnp.int32), axis=1)).astype(jnp.int32) - 1
    file_begin = lax.optimization_barrier(jnp.max(jnp.where(before, file_starts[None, :], 0), axis=1)).astype(jnp.int32)
    lower_file = file_of[0]
    upper_file = file_of[span_rows - 1]
    per_file = file_imports.shape[1]
    lower_list = lax.dynamic_slice_in_dim(file_imports, lower_file.astype(jnp.int32), 1, 0)[0]
    upper_list = lax.dynamic_slice_in_dim(file_imports, upper_file.astype(jnp.int32), 1, 0)[0]
    targets = jnp.concatenate([lower_list, upper_list])
    source_file = jnp.concatenate([jnp.full((per_file,), lower_file, jnp.int32), jnp.full((per_file,), upper_file, jnp.int32)])
    usable = (targets >= 0) & ((jnp.arange(2 * per_file, dtype=jnp.int32) < per_file) | (upper_file != lower_file))
    matches = jnp.arange(file_starts.shape[0], dtype=jnp.int32)[None, :] == targets[:, None]
    target_start = lax.optimization_barrier(jnp.sum(jnp.where(matches, file_starts[None, :], 0), axis=1)).astype(jnp.int32)
    target_len = lax.optimization_barrier(jnp.sum(jnp.where(matches, header_lens[None, :], 0), axis=1)).astype(jnp.int32)
    return (places, file_of, file_begin, source_file, usable, target_start, target_len)

def visibility(places, file_of, file_begin, key_places, source_file, usable, target_len):
    window_ok = (key_places[None, :] <= places[:, None]) & (key_places[None, :] > places[:, None] - WIN) & (key_places[None, :] >= file_begin[:, None])
    offsets = jnp.arange(usable.shape[0] * HDR, dtype=jnp.int32) % HDR
    header_ok = jnp.repeat(usable, HDR) & (offsets < jnp.repeat(target_len, HDR))
    header_vis = header_ok[None, :] & (file_of[:, None] == jnp.repeat(source_file, HDR)[None, :])
    return jnp.concatenate([window_ok, header_vis], axis=1)

def reference(queries, key_head_columns, value_head_columns, output_gradient, file_starts, file_imports, header_lens):
    queries_per_group = QUERY_HEADS // KEY_VALUE_HEADS
    scaling = 1.0 / math.sqrt(HEAD_WIDTH)
    reach = WIN // TOK_DEV
    shards = PACKED_TOKENS // TOK_DEV
    front_padding = reach * TOK_DEV
    keys_rank_three = key_head_columns.reshape(PACKED_TOKENS, KEY_VALUE_HEADS, HEAD_WIDTH)
    values_rank_three = value_head_columns.reshape(PACKED_TOKENS, KEY_VALUE_HEADS, HEAD_WIDTH)
    padded_keys = jnp.concatenate([jnp.zeros((front_padding, KEY_VALUE_HEADS, HEAD_WIDTH), key_head_columns.dtype), keys_rank_three], axis=0)
    padded_values = jnp.concatenate([jnp.zeros((front_padding, KEY_VALUE_HEADS, HEAD_WIDTH), value_head_columns.dtype), values_rank_three], axis=0)
    query_rank_four = queries.reshape(PACKED_TOKENS, KEY_VALUE_HEADS, queries_per_group, HEAD_WIDTH)
    gradient_rank_four = output_gradient.reshape(PACKED_TOKENS, KEY_VALUE_HEADS, queries_per_group, HEAD_WIDTH)
    block_count = 2 * IMPORTS

    def one_shard(carry, shard_index):
        key_gradient_sum, value_gradient_sum = carry
        offset_base = (shard_index * TOK_DEV).astype(jnp.int32)
        places, file_of, file_begin, source_file, usable, target_start, target_len = local_files(file_starts, file_imports, header_lens, offset_base, TOK_DEV)
        key_places = offset_base - front_padding + jnp.arange(front_padding + TOK_DEV, dtype=jnp.int32)
        key_window = lax.dynamic_slice_in_dim(padded_keys, offset_base, front_padding + TOK_DEV, 0)
        value_window = lax.dynamic_slice_in_dim(padded_values, offset_base, front_padding + TOK_DEV, 0)
        key_header = jnp.concatenate([lax.dynamic_slice_in_dim(keys_rank_three, target_start[index], HDR, 0) for index in range(block_count)], axis=0)
        value_header = jnp.concatenate([lax.dynamic_slice_in_dim(values_rank_three, target_start[index], HDR, 0) for index in range(block_count)], axis=0)
        key_all = jnp.concatenate([key_window, key_header], axis=0).astype(jnp.float32)
        value_all = jnp.concatenate([value_window, value_header], axis=0).astype(jnp.float32)
        visible = visibility(places, file_of, file_begin, key_places, source_file, usable, target_len)
        query_here = lax.dynamic_slice_in_dim(query_rank_four, offset_base, TOK_DEV, 0).astype(jnp.float32)
        grad_here = lax.dynamic_slice_in_dim(gradient_rank_four, offset_base, TOK_DEV, 0).astype(jnp.float32)
        scores = jnp.einsum('tagd,kad->agtk', query_here, key_all) * scaling
        scores = jnp.where(visible[None, None], scores, -jnp.inf)
        ceiling = lax.optimization_barrier(jnp.max(scores, axis=-1, keepdims=True))
        log_total = ceiling + jnp.log(lax.optimization_barrier(jnp.sum(jnp.exp(scores - ceiling), axis=-1, keepdims=True)))
        weights = jnp.exp(scores - log_total)
        grad_weights = jnp.einsum('tagd,kad->agtk', grad_here, value_all)
        centre = lax.optimization_barrier(jnp.sum(weights * grad_weights, axis=-1, keepdims=True))
        grad_scores = lax.optimization_barrier((weights * (grad_weights - centre)).astype(jnp.bfloat16)).astype(jnp.float32)
        weights_low = lax.optimization_barrier(weights.astype(jnp.bfloat16)).astype(jnp.float32)
        grad_query = jnp.einsum('agtk,kad->tagd', grad_scores, key_all) * scaling
        key_part = jnp.einsum('agtk,tagd->kad', grad_scores, query_here) * scaling
        value_part = jnp.einsum('agtk,tagd->kad', weights_low, grad_here)
        window_len = front_padding + TOK_DEV
        current = lax.dynamic_slice_in_dim(key_gradient_sum, offset_base, window_len, 0)
        key_gradient_sum = lax.dynamic_update_slice_in_dim(key_gradient_sum, current + key_part[:window_len], offset_base, 0)
        current = lax.dynamic_slice_in_dim(value_gradient_sum, offset_base, window_len, 0)
        value_gradient_sum = lax.dynamic_update_slice_in_dim(value_gradient_sum, current + value_part[:window_len], offset_base, 0)
        for index in range(block_count):
            at_row = (front_padding + target_start[index]).astype(jnp.int32)
            lower = window_len + index * HDR
            current = lax.dynamic_slice_in_dim(key_gradient_sum, at_row, HDR, 0)
            key_gradient_sum = lax.dynamic_update_slice_in_dim(key_gradient_sum, current + key_part[lower:lower + HDR], at_row, 0)
            current = lax.dynamic_slice_in_dim(value_gradient_sum, at_row, HDR, 0)
            value_gradient_sum = lax.dynamic_update_slice_in_dim(value_gradient_sum, current + value_part[lower:lower + HDR], at_row, 0)
        return ((key_gradient_sum, value_gradient_sum), grad_query.reshape(TOK_DEV, QUERY_HEADS * HEAD_WIDTH))
    empty_gradient = jnp.zeros((front_padding + PACKED_TOKENS, KEY_VALUE_HEADS, HEAD_WIDTH), jnp.float32)
    (key_gradient_sum, value_gradient_sum), grad_query = lax.scan(one_shard, (empty_gradient, empty_gradient), jnp.arange(shards, dtype=jnp.int32))
    grad_queries = grad_query.reshape(PACKED_TOKENS, QUERY_HEADS * HEAD_WIDTH)
    key_gradient = key_gradient_sum[front_padding:].reshape(PACKED_TOKENS, KEY_VALUE_HEADS * HEAD_WIDTH)
    value_gradient = value_gradient_sum[front_padding:].reshape(PACKED_TOKENS, KEY_VALUE_HEADS * HEAD_WIDTH)
    return (grad_queries, key_gradient, value_gradient)
```

```python
import functools
import math

import jax
import jax.numpy as jnp
from jax import lax
from jax.experimental import pallas as pl
from jax.experimental.pallas import tpu as pltpu
from jax.sharding import Mesh
from jax.sharding import PartitionSpec as P

WIN = 1024
HDR = 64
TOK = 256
BLK = 64
D = 128
HEADS = 12
GROUPS = 4
REACH = WIN // TOK
QB = TOK // BLK
IMPORTS = 4
NX, NY, NZ = 2, 4, 8
NCTX = NX * NY * NZ
WROWS = WIN + BLK
HROWS = IMPORTS * HDR
ROWS = WROWS + HROWS
CHUNK_HEADS = 4
CHUNKS = HEADS // CHUNK_HEADS
CW = CHUNK_HEADS * BLK
COLS = HEADS * BLK
SCALE = 1.0 / math.sqrt(D)
LOG2E = 1.4426950408889634
HIDDEN = -1e30
MESH = pl.DeviceIdType.MESH
F32 = jnp.float32
BF16 = jnp.bfloat16
AXES = ("ctx_0", "ctx_1", "ctx_2", "head_0", "head_1")


def position():
    return tuple(lax.axis_index(a) for a in AXES)


def ctx_of(xh, y, z):
    return xh * (NY * NZ) + y * NZ + z


def ctx_shifted(xh, y, z, step):
    c = lax.rem(ctx_of(xh, y, z) + (NCTX + step), NCTX)
    return {
        "ctx_0": lax.div(c, NY * NZ),
        "ctx_1": lax.rem(lax.div(c, NZ), NY),
        "ctx_2": lax.rem(c, NZ),
    }


def head_peer(xl, co, d):
    pxl = 1 - xl if d & 2 else xl
    pco = 1 - co if d & 1 else co
    return {"head_0": pxl, "head_1": pco}, pxl * 2 + pco


def greet(peers):
    barrier = pltpu.get_barrier_semaphore()
    for peer in peers:
        pl.semaphore_signal(barrier, inc=1, device_id=peer, device_id_type=MESH)
    pl.semaphore_wait(barrier, len(peers))


def remote(src, dst, send, recv, peer):
    return pltpu.make_async_remote_copy(
        src_ref=src, dst_ref=dst, send_sem=send, recv_sem=recv, device_id=peer, device_id_type=MESH
    )


def all_peers(xh, y, z, xl, co):
    peers = [head_peer(xl, co, d)[0] for d in (1, 2, 3)]
    peers += [{"ctx_2": lax.rem(z + d, NZ)} for d in range(1, NZ)]
    peers += [{"ctx_1": lax.rem(y + d, NY)} for d in range(1, NY)]
    peers += [{"ctx_0": 1 - xh}]
    peers += [ctx_shifted(xh, y, z, 1), ctx_shifted(xh, y, z, -1)]
    return peers


def rows(start, size):
    return pl.ds(pl.multiple_of(start, size), size)


def entry_kernel(
    starts, q, k, v, do,
    q_out, do_out, kvwin, slots,
    hsend, hrecv, qsend, qrecv, local, wsend, wrecv, zsend, zrecv, xsend, xrecv, ysend, yrecv,
):
    xh, y, z, xl, co = position()
    me = xl * 2 + co
    width = HEADS * D
    greet(all_peers(xh, y, z, xl, co))
    own = REACH * TOK
    kv_copies, q_copies = [], []
    for d in (1, 2, 3):
        peer, a = head_peer(xl, co, d)
        for n, src in enumerate((k, v)):
            kv_copies.append(remote(
                src.at[:, rows(a * D, D)],
                kvwin.at[rows(own + me * BLK, BLK), pl.ds(n * D, D)],
                hsend.at[d - 1, n], hrecv.at[d - 1, n], peer,
            ))
            kv_copies[-1].start()
    for d in (2, 3, 1):
        peer, a = head_peer(xl, co, d)
        for n, (src, dst) in enumerate(((q, q_out), (do, do_out))):
            q_copies.append(remote(
                src.at[:, rows(a * width, width)], dst.at[rows(me * BLK, BLK), :],
                qsend.at[d - 1, n], qrecv.at[d - 1, n], peer,
            ))
            q_copies[-1].start()
    own_copies = []
    for n, (src, dst) in enumerate(((q, q_out), (do, do_out))):
        own_copies.append(pltpu.make_async_copy(
            src.at[:, rows(me * width, width)], dst.at[rows(me * BLK, BLK), :], local.at[n]
        ))
        own_copies[-1].start()
    for n, src in enumerate((k, v)):
        kvwin[rows(own + me * BLK, BLK), pl.ds(n * D, D)] = src[:, rows(me * D, D)]
    base = ctx_of(xh, y, z) * TOK
    offset = jnp.int32(0)
    for f in range(starts.shape[0]):
        at = starts[f] - base
        offset = offset + jnp.where((at >= 0) & (at < TOK), at, 0)
    for copy in kv_copies:
        copy.wait_recv()

    forward = ctx_shifted(xh, y, z, 1)

    def window_copy(step):
        return remote(
            kvwin.at[pl.ds((REACH + 1 - step) * TOK, TOK), :],
            kvwin.at[pl.ds((REACH - step) * TOK, TOK), :],
            wsend.at[step - 1], wrecv.at[step - 1], forward,
        )

    mine = (y * NX + xh) * NZ + z
    header = jnp.zeros((HDR, 2 * D), F32)
    for b in range(QB):
        keep = jnp.where(offset == b * BLK, 1.0, 0.0)
        header = header + kvwin[own + b * BLK:own + (b + 1) * BLK, :].astype(F32) * keep
    slots[rows(mine * HDR, HDR), :] = header.astype(BF16)
    z_copies = []
    for d in (1, 7, 2, 6, 3, 5, 4):
        z_copies.append(remote(
            slots.at[rows(mine * HDR, HDR), :], slots.at[rows(mine * HDR, HDR), :],
            zsend.at[d - 1], zrecv.at[d - 1], {"ctx_2": lax.rem(z + d, NZ)},
        ))
        z_copies[-1].start()
    w_copies = [window_copy(s) for s in range(1, REACH + 1)]
    w_copies[0].start()
    for copy in z_copies:
        copy.wait_recv()
    line = rows((y * NX + xh) * NZ * HDR, NZ * HDR)
    x_copy = remote(slots.at[line, :], slots.at[line, :], xsend, xrecv, {"ctx_0": 1 - xh})
    x_copy.start()
    w_copies[0].wait_recv()
    w_copies[1].start()
    x_copy.wait_recv()
    plane = rows(y * NX * NZ * HDR, NX * NZ * HDR)
    y_copies = []
    for d in (1, 3, 2):
        y_copies.append(remote(
            slots.at[plane, :], slots.at[plane, :],
            ysend.at[d - 1], yrecv.at[d - 1], {"ctx_1": lax.rem(y + d, NY)},
        ))
        y_copies[-1].start()
    w_copies[1].wait_recv()
    w_copies[2].start()
    w_copies[2].wait_recv()
    w_copies[3].start()
    w_copies[3].wait_recv()
    for copy in q_copies + y_copies:
        copy.wait_recv()
    for copy in own_copies:
        copy.wait()
    for copy in kv_copies + q_copies + z_copies + w_copies + [x_copy] + y_copies:
        copy.wait_send()


def entry(starts, q, k, v, do):
    dma = pltpu.SemaphoreType.DMA
    hbm = pl.BlockSpec(memory_space=pl.ANY)
    vmem = pl.BlockSpec(memory_space=pltpu.VMEM)
    smem = pl.BlockSpec(memory_space=pltpu.SMEM)
    return pl.pallas_call(
        entry_kernel,
        out_shape=(
            jax.ShapeDtypeStruct((TOK, HEADS * D), BF16),
            jax.ShapeDtypeStruct((TOK, HEADS * D), BF16),
            jax.ShapeDtypeStruct(((REACH + 1) * TOK, 2 * D), BF16),
            jax.ShapeDtypeStruct((NCTX * HDR, 2 * D), BF16),
        ),
        in_specs=[smem, hbm, vmem, vmem, hbm],
        out_specs=(hbm, hbm, vmem, vmem),
        scratch_shapes=[
            dma((3, 2)), dma((3, 2)), dma((3, 2)), dma((3, 2)), dma((2,)),
            dma((REACH,)), dma((REACH,)), dma((NZ - 1,)), dma((NZ - 1,)),
            dma, dma, dma((NY - 1,)), dma((NY - 1,)),
        ],
        compiler_params=pltpu.CompilerParams(
            collective_id=0, has_side_effects=True, vmem_limit_bytes=32 * 2**20
        ),
        name="entry",
    )(starts, q, k, v, do)


def fold8(x, op):
    out = x[0:8]
    for r in range(8, x.shape[0], 8):
        out = op(out, x[r:r + 8])
    return out


def file_at(starts, place):
    count = jnp.int32(-1)
    for f in range(starts.shape[0]):
        count = count + jnp.where(starts[f] <= place, 1, 0)
    return count


def slot_of(start):
    c = lax.div(start, TOK)
    xh = lax.div(c, NY * NZ)
    y = lax.rem(lax.div(c, NZ), NY)
    z = lax.rem(c, NZ)
    return (y * NX + xh) * NZ + z


def compute_kernel(
    starts, imports, lens, q, do, kvwin, slots,
    dq_out, dkv, table,
    kc, vc, bias, qs, dos, s_ref, dp_ref, p_ref, ds_ref, hacc,
):
    xh, y, z, _, _ = position()
    base = ctx_of(xh, y, z) * TOK
    lower = file_at(starts, base)
    upper = file_at(starts, base + TOK - 1)
    dkv[...] = jnp.zeros_like(dkv)
    hacc[...] = jnp.zeros_like(hacc)
    table[...] = jnp.zeros_like(table)
    step = 64

    def one_block(qb, carry):
        place = base + qb * BLK
        file = file_at(starts, place)
        begin = starts[file]
        kc[0:WROWS, :] = kvwin[rows_at(qb * BLK, WROWS, BLK), 0:D]
        vc[0:WROWS, :] = kvwin[rows_at(qb * BLK, WROWS, BLK), D:2 * D]
        key_place = lax.broadcasted_iota(jnp.int32, (WROWS, D), 0) + (place - WIN)
        bias[0:WROWS, :] = jnp.where(key_place >= begin, 0.0, HIDDEN)
        offsets = lax.broadcasted_iota(jnp.int32, (HDR, D), 0)
        for m in range(IMPORTS):
            g = imports[file, m]
            known = jnp.maximum(g, 0)
            length = jnp.where(g >= 0, lens[known], 0)
            at = rows(slot_of(starts[known]) * HDR, HDR)
            here = pl.ds(WROWS + m * HDR, HDR)
            kc[here, :] = slots[at, 0:D]
            vc[here, :] = slots[at, D:2 * D]
            bias[here, :] = jnp.where(offsets < length, 0.0, HIDDEN)
        for h in range(HEADS):
            qs[h * BLK:(h + 1) * BLK, :] = q[rows(qb * BLK, BLK), h * D:(h + 1) * D]
            dos[h * BLK:(h + 1) * BLK, :] = do[rows(qb * BLK, BLK), h * D:(h + 1) * D]

        t = lax.broadcasted_iota(jnp.int32, (BLK, CW), 0)
        p_at = lax.broadcasted_iota(jnp.int32, (BLK, CW), 1) % BLK
        nt = (((1,), (1,)), ((), ()))
        for chunk in range(CHUNKS):
            cols = slice(chunk * CW, (chunk + 1) * CW)
            s_ref[...] = lax.dot_general(kc[...], qs[cols, :], nt, preferred_element_type=F32)
            dp_ref[...] = lax.dot_general(vc[...], dos[cols, :], nt, preferred_element_type=F32)
            top = None
            for r in range(0, ROWS, step):
                b = bias[r:r + step, :]
                s = s_ref[r:r + step, :] + jnp.concatenate([b] * (CW // D), axis=1)
                if r == 0:
                    s = jnp.where(t > p_at, s, HIDDEN)
                if r == WIN:
                    s = jnp.where(t <= p_at, s, HIDDEN)
                s_ref[r:r + step, :] = s
                part = fold8(s, jnp.maximum)
                top = part if top is None else jnp.maximum(top, part)
            top = jnp.max(top, axis=0, keepdims=True)
            total = jnp.zeros((8, CW), F32)
            centre = jnp.zeros((8, CW), F32)
            for r in range(0, ROWS, step):
                e = jnp.exp2((s_ref[r:r + step, :] - top) * (SCALE * LOG2E))
                s_ref[r:r + step, :] = e
                total = total + fold8(e, jnp.add)
                centre = centre + fold8(e * dp_ref[r:r + step, :], jnp.add)
            inverse = 1.0 / jnp.sum(total, axis=0, keepdims=True)
            centre = jnp.sum(centre, axis=0, keepdims=True) * inverse
            for r in range(0, ROWS, step):
                w = s_ref[r:r + step, :] * inverse
                p_ref[r:r + step, cols] = w.astype(BF16)
                ds_ref[r:r + step, cols] = (w * (dp_ref[r:r + step, :] - centre)).astype(BF16)
        dv = jnp.dot(p_ref[...], dos[...], preferred_element_type=F32)
        dk = jnp.dot(ds_ref[...], qs[...], preferred_element_type=F32) * SCALE
        window = rows_at(qb * BLK, WROWS, BLK)
        dkv[window, 0:D] += dk[0:WROWS]
        dkv[window, D:2 * D] += dv[0:WROWS]
        which = jnp.where(file == lower, 0, 1)
        hdr = rows(which * HROWS, HROWS)
        hacc[hdr, 0:D] += dk[WROWS:]
        hacc[hdr, D:2 * D] += dv[WROWS:]
        dqt = lax.dot_general(
            kc[...], ds_ref[...], (((0,), (0,)), ((), ())), preferred_element_type=F32
        )
        dq = (dqt.T * SCALE).astype(BF16)
        for h in range(HEADS):
            dq_out[rows(qb * BLK, BLK), h * D:(h + 1) * D] = dq[h * BLK:(h + 1) * BLK]
        return carry

    lax.fori_loop(0, QB, one_block, 0)
    for which, file in ((0, lower), (1, upper)):
        for m in range(IMPORTS):
            g = imports[file, m]
            usable = g >= 0 if which == 0 else (g >= 0) & (upper != lower)

            @pl.when(usable)
            def _():
                at = rows(slot_of(starts[jnp.maximum(g, 0)]) * HDR, HDR)
                part = hacc[pl.ds((which * IMPORTS + m) * HDR, HDR), :]
                table[at, :] = (table[at, :].astype(F32) + part).astype(BF16)


def rows_at(start, size, multiple):
    return pl.ds(pl.multiple_of(start, multiple), size)


def compute(starts, imports, lens, q, do, kvwin, slots):
    vmem = pl.BlockSpec(memory_space=pltpu.VMEM)
    smem = pl.BlockSpec(memory_space=pltpu.SMEM)
    return pl.pallas_call(
        compute_kernel,
        out_shape=(
            jax.ShapeDtypeStruct((TOK, HEADS * D), BF16),
            jax.ShapeDtypeStruct(((REACH + 1) * TOK, 2 * D), F32),
            jax.ShapeDtypeStruct((NCTX * HDR, 2 * D), BF16),
        ),
        in_specs=[smem, smem, smem, vmem, vmem, vmem, vmem],
        out_specs=(vmem, vmem, vmem),
        scratch_shapes=[
            pltpu.VMEM((ROWS, D), BF16), pltpu.VMEM((ROWS, D), BF16), pltpu.VMEM((ROWS, D), F32),
            pltpu.VMEM((COLS, D), BF16), pltpu.VMEM((COLS, D), BF16),
            pltpu.VMEM((ROWS, CW), F32), pltpu.VMEM((ROWS, CW), F32),
            pltpu.VMEM((ROWS, COLS), BF16), pltpu.VMEM((ROWS, COLS), BF16),
            pltpu.VMEM((2 * HROWS, 2 * D), F32),
        ],
        compiler_params=pltpu.CompilerParams(vmem_limit_bytes=48 * 2**20),
        name="attend",
    )(starts, imports, lens, q, do, kvwin, slots)


def exit_kernel(
    starts, dq, dkv, table,
    dq_out, dk_out, dv_out,
    ry, tx, rx, acc, tz, rz, wout, win, coll,
    ysend, yrecv, qsend, qrecv, local, wsend, wrecv, xsend, xrecv, zsend, zrecv, hsend, hrecv,
):
    xh, y, z, xl, co = position()
    me = xl * 2 + co
    width = HEADS * D
    greet(all_peers(xh, y, z, xl, co))
    plane = NX * NZ * HDR
    line = NZ * HDR
    y_copies = []
    for d in (1, 3, 2):
        to = lax.rem(y + d, NY)
        y_copies.append(remote(
            table.at[rows(to * plane, plane), :], ry.at[d - 1],
            ysend.at[d - 1], yrecv.at[d - 1], {"ctx_1": to},
        ))
        y_copies[-1].start()
    back = ctx_shifted(xh, y, z, -1)
    w_copies = [
        remote(wout.at[s], win.at[s], wsend.at[s], wrecv.at[s], back) for s in range(REACH)
    ]
    wout[0] = dkv[0:TOK, :].astype(BF16)
    w_copies[0].start()
    q_copies = []
    for d in (2, 3, 1):
        peer, a = head_peer(xl, co, d)
        q_copies.append(remote(
            dq.at[rows(a * BLK, BLK), :], dq_out.at[:, rows(me * width, width)],
            qsend.at[d - 1], qrecv.at[d - 1], peer,
        ))
        q_copies[-1].start()
    own = pltpu.make_async_copy(
        dq.at[rows(me * BLK, BLK), :], dq_out.at[:, rows(me * width, width)], local
    )
    own.start()
    for s in range(1, REACH):
        w_copies[s - 1].wait_recv()
        wout[s] = (win[s - 1].astype(F32) + dkv[s * TOK:(s + 1) * TOK, :]).astype(BF16)
        w_copies[s].start()
    for copy in y_copies:
        copy.wait_recv()

    def plane_sum(block):
        at = rows(block * line, line)
        total = table[rows(y * plane + block * line, line), :].astype(F32)
        for d in range(NY - 1):
            total = total + ry[d, at, :].astype(F32)
        return total

    tx[...] = plane_sum(1 - xh).astype(BF16)
    x_copy = remote(tx, rx, xsend, xrecv, {"ctx_0": 1 - xh})
    x_copy.start()
    acc[...] = plane_sum(xh)
    x_copy.wait_recv()
    acc[...] += rx[...].astype(F32)
    tz[...] = acc[...].astype(BF16)
    z_copies = []
    for d in (4, 3, 5, 2, 6, 1, 7):
        to = lax.rem(z + d, NZ)
        z_copies.append(remote(
            tz.at[rows(to * HDR, HDR), :], rz.at[d - 1],
            zsend.at[d - 1], zrecv.at[d - 1], {"ctx_2": to},
        ))
        z_copies[-1].start()
    w_copies[REACH - 1].wait_recv()
    header = acc[rows(z * HDR, HDR), :]
    for copy in z_copies:
        copy.wait_recv()
    for d in range(NZ - 1):
        header = header + rz[d].astype(F32)
    base = ctx_of(xh, y, z) * TOK
    offset = jnp.int32(0)
    for f in range(starts.shape[0]):
        at = starts[f] - base
        offset = offset + jnp.where((at >= 0) & (at < TOK), at, 0)
    for b in range(QB):
        part = slice(b * BLK, (b + 1) * BLK)
        keep = jnp.where(offset == b * BLK, 1.0, 0.0)
        coll[part, :] = (
            dkv[REACH * TOK + b * BLK:REACH * TOK + (b + 1) * BLK, :]
            + win[REACH - 1, part, :].astype(F32)
            + header * keep
        )
    h_copies = []
    for d in (2, 3, 1):
        peer, a = head_peer(xl, co, d)
        for n, dst in enumerate((dk_out, dv_out)):
            h_copies.append(remote(
                coll.at[rows(a * BLK, BLK), pl.ds(n * D, D)], dst.at[:, rows(me * D, D)],
                hsend.at[d - 1, n], hrecv.at[d - 1, n], peer,
            ))
            h_copies[-1].start()
    for n, dst in enumerate((dk_out, dv_out)):
        dst[:, rows(me * D, D)] = coll[rows(me * BLK, BLK), n * D:(n + 1) * D]
    own.wait()
    for copy in q_copies + h_copies:
        copy.wait_recv()
    for copy in y_copies + w_copies + q_copies + [x_copy] + z_copies + h_copies:
        copy.wait_send()


def leave(starts, dq, dkv, table):
    dma = pltpu.SemaphoreType.DMA
    hbm = pl.BlockSpec(memory_space=pl.ANY)
    vmem = pl.BlockSpec(memory_space=pltpu.VMEM)
    smem = pl.BlockSpec(memory_space=pltpu.SMEM)
    plane = NX * NZ * HDR
    line = NZ * HDR
    return pl.pallas_call(
        exit_kernel,
        out_shape=(
            jax.ShapeDtypeStruct((BLK, GROUPS * HEADS * D), BF16),
            jax.ShapeDtypeStruct((BLK, GROUPS * D), F32),
            jax.ShapeDtypeStruct((BLK, GROUPS * D), F32),
        ),
        in_specs=[smem, hbm, vmem, vmem],
        out_specs=(hbm, vmem, vmem),
        scratch_shapes=[
            pltpu.VMEM((NY - 1, plane, 2 * D), BF16),
            pltpu.VMEM((line, 2 * D), BF16), pltpu.VMEM((line, 2 * D), BF16),
            pltpu.VMEM((line, 2 * D), F32), pltpu.VMEM((line, 2 * D), BF16),
            pltpu.VMEM((NZ - 1, HDR, 2 * D), BF16),
            pltpu.VMEM((REACH, TOK, 2 * D), BF16), pltpu.VMEM((REACH, TOK, 2 * D), BF16),
            pltpu.VMEM((TOK, 2 * D), F32),
            dma((NY - 1,)), dma((NY - 1,)), dma((3,)), dma((3,)), dma,
            dma((REACH,)), dma((REACH,)), dma, dma, dma((NZ - 1,)), dma((NZ - 1,)),
            dma((3, 2)), dma((3, 2)),
        ],
        compiler_params=pltpu.CompilerParams(
            collective_id=1, has_side_effects=True, vmem_limit_bytes=32 * 2**20
        ),
        name="leave",
    )(starts, dq, dkv, table)


def per_device(queries, keys, values, output_gradient, file_starts, file_imports, header_lens):
    q, do, kvwin, slots = entry(file_starts, queries, keys, values, output_gradient)
    dq, dkv, table = compute(file_starts, file_imports, header_lens, q, do, kvwin, slots)
    dq_low, dk, dv = leave(file_starts, dq, dkv, table)
    return dq_low.astype(F32), dk, dv


def solution(mesh):
    split = Mesh(mesh.devices.reshape(NX, NY, NZ, 2, 2), AXES)
    placed = P(AXES, None)
    return jax.shard_map(
        per_device,
        mesh=split,
        in_specs=(placed, placed, placed, placed, P(), P(), P()),
        out_specs=(placed, placed, placed),
        check_vma=False,
    )
```

```python
import functools
import math

import jax
import jax.numpy as jnp
from jax import lax
from jax.experimental import pallas as pl
from jax.experimental.pallas import tpu as pltpu
from jax.sharding import Mesh
from jax.sharding import PartitionSpec as P

WIN = 1024
HDR = 64
TOK = 256
BLK = 64
D = 128
HEADS = 12
GROUPS = 4
REACH = WIN // TOK
QB = TOK // BLK
IMPORTS = 4
NX, NY, NZ = 2, 4, 8
NCTX = NX * NY * NZ
WROWS = WIN + BLK
HROWS = IMPORTS * HDR
ROWS = WROWS + HROWS
CHUNK_HEADS = 4
CHUNKS = HEADS // CHUNK_HEADS
CW = CHUNK_HEADS * BLK
COLS = HEADS * BLK
SCALE = 1.0 / math.sqrt(D)
LOG2E = 1.4426950408889634
HIDDEN = -1e30
MESH = pl.DeviceIdType.MESH
F32 = jnp.float32
BF16 = jnp.bfloat16
AXES = ("ctx_0", "ctx_1", "ctx_2", "head_0", "head_1")


def position():
    return tuple(lax.axis_index(a) for a in AXES)


def ctx_of(xh, y, z):
    return xh * (NY * NZ) + y * NZ + z


def ctx_shifted(xh, y, z, step):
    c = lax.rem(ctx_of(xh, y, z) + (NCTX + step), NCTX)
    return {
        "ctx_0": lax.div(c, NY * NZ),
        "ctx_1": lax.rem(lax.div(c, NZ), NY),
        "ctx_2": lax.rem(c, NZ),
    }


def head_peer(xl, co, d):
    pxl = 1 - xl if d & 2 else xl
    pco = 1 - co if d & 1 else co
    return {"head_0": pxl, "head_1": pco}, pxl * 2 + pco


def greet(peers):
    barrier = pltpu.get_barrier_semaphore()
    for peer in peers:
        pl.semaphore_signal(barrier, inc=1, device_id=peer, device_id_type=MESH)
    pl.semaphore_wait(barrier, len(peers))


def remote(src, dst, send, recv, peer):
    return pltpu.make_async_remote_copy(
        src_ref=src, dst_ref=dst, send_sem=send, recv_sem=recv, device_id=peer, device_id_type=MESH
    )


def all_peers(xh, y, z, xl, co):
    peers = [head_peer(xl, co, d)[0] for d in (1, 2, 3)]
    peers += [{"ctx_2": lax.rem(z + d, NZ)} for d in range(1, NZ)]
    peers += [{"ctx_1": n} for n in y_neighbours(y)]
    peers += [{"ctx_0": 1 - xh}]
    peers += [ctx_shifted(xh, y, z, 1), ctx_shifted(xh, y, z, -1)]
    return peers


def rows(start, size):
    return pl.ds(pl.multiple_of(start, size), size)


def y_neighbours(y):
    near = y + 1 - 2 * lax.rem(y, 2)
    return near, NY - 1 - y


def file_at(starts, place):
    count = jnp.int32(-1)
    for f in range(starts.shape[0]):
        count = count + jnp.where(starts[f] <= place, 1, 0)
    return count


def header_blocks(starts, imports, c):
    lower = file_at(starts, c * TOK)
    upper = file_at(starts, c * TOK + TOK - 1)
    blocks = []
    for file in (lower, upper):
        for m in range(IMPORTS):
            g = imports[file, m]
            blocks.append((g >= 0, lax.div(starts[jnp.maximum(g, 0)], TOK)))
    return lower, upper, blocks


def own_header_offset(starts, base):
    offset = jnp.int32(0)
    for f in range(starts.shape[0]):
        at = starts[f] - base
        offset = offset + jnp.where((at >= 0) & (at < TOK), at, 0)
    return offset


def fetch(pairs, sems):
    copies = [pltpu.make_async_copy(src, dst, sems.at[n]) for n, (src, dst) in enumerate(pairs)]
    for copy in copies:
        copy.start()
    return copies


def entry_kernel(
    starts_hbm, imports_hbm, q, k, v, do,
    q_out, do_out, kvwin, slots, far,
    starts, imports, picked,
    fsem, hsend, hrecv, qsend, qrecv, local, wsend, wrecv, zsend, zrecv, xsend, xrecv,
    ysend, yrecv,
):
    xh, y, z, xl, co = position()
    me = xl * 2 + co
    c = ctx_of(xh, y, z)
    width = HEADS * D
    own = REACH * TOK
    small = fetch(((starts_hbm, starts), (imports_hbm, imports)), fsem)
    here = fetch(
        (
            (k.at[:, rows(me * D, D)], kvwin.at[rows(own + me * BLK, BLK), pl.ds(0, D)]),
            (v.at[:, rows(me * D, D)], kvwin.at[rows(own + me * BLK, BLK), pl.ds(D, D)]),
            (q.at[:, rows(me * width, width)], q_out.at[rows(me * BLK, BLK), :]),
            (do.at[:, rows(me * width, width)], do_out.at[rows(me * BLK, BLK), :]),
        ),
        local,
    )
    greet(all_peers(xh, y, z, xl, co))
    kv_copies, q_copies = [], []
    for d in (2, 3, 1):
        peer, a = head_peer(xl, co, d)
        for n, src in enumerate((k, v)):
            kv_copies.append(remote(
                src.at[:, rows(a * D, D)],
                kvwin.at[rows(own + me * BLK, BLK), pl.ds(n * D, D)],
                hsend.at[d - 1, n], hrecv.at[d - 1, n], peer,
            ))
            kv_copies[-1].start()
    for d in (2, 3, 1):
        peer, a = head_peer(xl, co, d)
        for n, (src, dst) in enumerate(((q, q_out), (do, do_out))):
            q_copies.append(remote(
                src.at[:, rows(a * width, width)], dst.at[rows(me * BLK, BLK), :],
                qsend.at[d - 1, n], qrecv.at[d - 1, n], peer,
            ))
            q_copies[-1].start()
    for copy in small:
        copy.wait()
    offset = own_header_offset(starts, c * TOK)
    for copy in here[:2]:
        copy.wait()
    for copy in kv_copies:
        copy.wait_recv()

    forward = ctx_shifted(xh, y, z, 1)
    w_copies = [
        remote(
            kvwin.at[pl.ds((REACH - s) * TOK, TOK), :],
            kvwin.at[pl.ds((REACH - 1 - s) * TOK, TOK), :],
            wsend.at[s], wrecv.at[s], forward,
        )
        for s in range(REACH)
    ]
    header = jnp.zeros((HDR, 2 * D), F32)
    for b in range(QB):
        keep = jnp.where(offset == b * BLK, 1.0, 0.0)
        header = header + kvwin[own + b * BLK:own + (b + 1) * BLK, :].astype(F32) * keep
    line = y * NZ + z
    slots[line] = header.astype(BF16)
    z_copies = []
    for d in (1, 7, 2, 6, 3, 5, 4):
        z_copies.append(remote(
            slots.at[line], slots.at[line],
            zsend.at[d - 1], zrecv.at[d - 1], {"ctx_2": lax.rem(z + d, NZ)},
        ))
        z_copies[-1].start()
    w_copies[0].start()
    for copy in z_copies:
        copy.wait_recv()
    near, other = y_neighbours(y)
    y_copies = []
    for n, to in enumerate((near, other)):
        y_copies.append(remote(
            slots.at[rows(y * NZ, NZ)], slots.at[rows(y * NZ, NZ)],
            ysend.at[n], yrecv.at[n], {"ctx_1": to},
        ))
        y_copies[-1].start()
    w_copies[0].wait_recv()
    w_copies[1].start()
    for n, (came, to) in enumerate(((near, other), (other, near))):
        y_copies[n].wait_recv()
        part = slots.at[rows(came * NZ, NZ), :, pl.ds(n * D, D)]
        y_copies.append(remote(part, part, ysend.at[2 + n], yrecv.at[2 + n], {"ctx_1": to}))
        y_copies[-1].start()
    w_copies[1].wait_recv()
    w_copies[2].start()
    _, _, wanted = header_blocks(starts, imports, ctx_of(1 - xh, y, z))
    for copy in y_copies[2:]:
        copy.wait_recv()
    for m, (_, shard) in enumerate(wanted):
        picked[m] = slots[lax.rem(shard, NY * NZ)]
    x_copy = remote(picked, far, xsend, xrecv, {"ctx_0": 1 - xh})
    x_copy.start()
    w_copies[2].wait_recv()
    w_copies[3].start()
    w_copies[3].wait_recv()
    x_copy.wait_recv()
    for copy in q_copies:
        copy.wait_recv()
    for copy in here[2:]:
        copy.wait()
    for copy in kv_copies + q_copies + z_copies + w_copies + y_copies + [x_copy]:
        copy.wait_send()


def entry(starts, imports, q, k, v, do):
    dma = pltpu.SemaphoreType.DMA
    hbm = pl.BlockSpec(memory_space=pl.ANY)
    vmem = pl.BlockSpec(memory_space=pltpu.VMEM)
    return pl.pallas_call(
        entry_kernel,
        out_shape=(
            jax.ShapeDtypeStruct((TOK, HEADS * D), BF16),
            jax.ShapeDtypeStruct((TOK, HEADS * D), BF16),
            jax.ShapeDtypeStruct(((REACH + 1) * TOK, 2 * D), BF16),
            jax.ShapeDtypeStruct((NY * NZ, HDR, 2 * D), BF16),
            jax.ShapeDtypeStruct((2 * IMPORTS, HDR, 2 * D), BF16),
        ),
        in_specs=[hbm] * 6,
        out_specs=(hbm, hbm, vmem, vmem, vmem),
        scratch_shapes=[
            pltpu.SMEM(starts.shape, jnp.int32), pltpu.SMEM(imports.shape, jnp.int32),
            pltpu.VMEM((2 * IMPORTS, HDR, 2 * D), BF16),
            dma((2,)), dma((3, 2)), dma((3, 2)), dma((3, 2)), dma((3, 2)), dma((4,)),
            dma((REACH,)), dma((REACH,)), dma((NZ - 1,)), dma((NZ - 1,)),
            dma, dma, dma((4,)), dma((4,)),
        ],
        compiler_params=pltpu.CompilerParams(
            collective_id=0, has_side_effects=True, vmem_limit_bytes=32 * 2**20
        ),
        name="entry",
    )(starts, imports, q, k, v, do)


def fold8(x, op):
    out = x[0:8]
    for r in range(8, x.shape[0], 8):
        out = op(out, x[r:r + 8])
    return out


def compute_kernel(
    starts, imports, lens, q, do, kvwin, slots, far,
    dq_out, dkv, packed,
    kc, vc, bias, qs, dos, s_ref, dp_ref, p_ref, ds_ref, hacc,
):
    xh, y, z, _, _ = position()
    base = ctx_of(xh, y, z) * TOK
    lower = file_at(starts, base)
    dkv[...] = jnp.zeros_like(dkv)
    hacc[...] = jnp.zeros_like(hacc)
    step = 64

    def one_block(qb, carry):
        place = base + qb * BLK
        file = file_at(starts, place)
        begin = starts[file]
        kc[0:WROWS, :] = kvwin[rows_at(qb * BLK, WROWS, BLK), 0:D]
        vc[0:WROWS, :] = kvwin[rows_at(qb * BLK, WROWS, BLK), D:2 * D]
        key_place = lax.broadcasted_iota(jnp.int32, (WROWS, D), 0) + (place - WIN)
        bias[0:WROWS, :] = jnp.where(key_place >= begin, 0.0, HIDDEN)
        offsets = lax.broadcasted_iota(jnp.int32, (HDR, D), 0)
        for m in range(IMPORTS):
            g = imports[file, m]
            known = jnp.maximum(g, 0)
            length = jnp.where(g >= 0, lens[known], 0)
            shard = lax.div(starts[known], TOK)
            at = lax.rem(shard, NY * NZ)
            which = jnp.where(file == lower, 0, IMPORTS) + m
            same = jnp.full((HDR, 2 * D), lax.div(shard, NY * NZ)) == xh
            rows_kv = jnp.where(same, slots[at].astype(F32), far[which].astype(F32)).astype(BF16)
            here = pl.ds(WROWS + m * HDR, HDR)
            kc[here, :] = rows_kv[:, 0:D]
            vc[here, :] = rows_kv[:, D:2 * D]
            bias[here, :] = jnp.where(offsets < length, 0.0, HIDDEN)
        for h in range(HEADS):
            qs[h * BLK:(h + 1) * BLK, :] = q[rows(qb * BLK, BLK), h * D:(h + 1) * D]
            dos[h * BLK:(h + 1) * BLK, :] = do[rows(qb * BLK, BLK), h * D:(h + 1) * D]

        t = lax.broadcasted_iota(jnp.int32, (BLK, CW), 0)
        p_at = lax.broadcasted_iota(jnp.int32, (BLK, CW), 1) % BLK
        nt = (((1,), (1,)), ((), ()))
        for chunk in range(CHUNKS):
            cols = slice(chunk * CW, (chunk + 1) * CW)
            s_ref[...] = lax.dot_general(kc[...], qs[cols, :], nt, preferred_element_type=F32)
            dp_ref[...] = lax.dot_general(vc[...], dos[cols, :], nt, preferred_element_type=F32)
            top = None
            for r in range(0, ROWS, step):
                b = bias[r:r + step, :]
                s = s_ref[r:r + step, :] + jnp.concatenate([b] * (CW // D), axis=1)
                if r == 0:
                    s = jnp.where(t > p_at, s, HIDDEN)
                if r == WIN:
                    s = jnp.where(t <= p_at, s, HIDDEN)
                s_ref[r:r + step, :] = s
                part = fold8(s, jnp.maximum)
                top = part if top is None else jnp.maximum(top, part)
            top = jnp.max(top, axis=0, keepdims=True)
            total = jnp.zeros((8, CW), F32)
            centre = jnp.zeros((8, CW), F32)
            for r in range(0, ROWS, step):
                e = jnp.exp2((s_ref[r:r + step, :] - top) * (SCALE * LOG2E))
                s_ref[r:r + step, :] = e
                total = total + fold8(e, jnp.add)
                centre = centre + fold8(e * dp_ref[r:r + step, :], jnp.add)
            inverse = 1.0 / jnp.sum(total, axis=0, keepdims=True)
            centre = jnp.sum(centre, axis=0, keepdims=True) * inverse
            for r in range(0, ROWS, step):
                w = s_ref[r:r + step, :] * inverse
                p_ref[r:r + step, cols] = w.astype(BF16)
                ds_ref[r:r + step, cols] = (w * (dp_ref[r:r + step, :] - centre)).astype(BF16)
        dv = jnp.dot(p_ref[...], dos[...], preferred_element_type=F32)
        dk = jnp.dot(ds_ref[...], qs[...], preferred_element_type=F32) * SCALE
        window = rows_at(qb * BLK, WROWS, BLK)
        dkv[window, 0:D] += dk[0:WROWS]
        dkv[window, D:2 * D] += dv[0:WROWS]
        which = jnp.where(file == lower, 0, 1)
        hdr = rows(which * HROWS, HROWS)
        hacc[hdr, 0:D] += dk[WROWS:]
        hacc[hdr, D:2 * D] += dv[WROWS:]
        dqt = lax.dot_general(
            kc[...], ds_ref[...], (((0,), (0,)), ((), ())), preferred_element_type=F32
        )
        dq = (dqt.T * SCALE).astype(BF16)
        for h in range(HEADS):
            dq_out[rows(qb * BLK, BLK), h * D:(h + 1) * D] = dq[h * BLK:(h + 1) * BLK]
        return carry

    lax.fori_loop(0, QB, one_block, 0)
    for m in range(2 * IMPORTS):
        packed[m] = hacc[m * HDR:(m + 1) * HDR, :].astype(BF16)


def rows_at(start, size, multiple):
    return pl.ds(pl.multiple_of(start, multiple), size)


def compute(starts, imports, lens, q, do, kvwin, slots, far):
    vmem = pl.BlockSpec(memory_space=pltpu.VMEM)
    smem = pl.BlockSpec(memory_space=pltpu.SMEM)
    return pl.pallas_call(
        compute_kernel,
        out_shape=(
            jax.ShapeDtypeStruct((TOK, HEADS * D), BF16),
            jax.ShapeDtypeStruct(((REACH + 1) * TOK, 2 * D), F32),
            jax.ShapeDtypeStruct((2 * IMPORTS, HDR, 2 * D), BF16),
        ),
        in_specs=[smem, smem, smem, vmem, vmem, vmem, vmem, vmem],
        out_specs=(vmem, vmem, vmem),
        scratch_shapes=[
            pltpu.VMEM((ROWS, D), BF16), pltpu.VMEM((ROWS, D), BF16), pltpu.VMEM((ROWS, D), F32),
            pltpu.VMEM((COLS, D), BF16), pltpu.VMEM((COLS, D), BF16),
            pltpu.VMEM((ROWS, CW), F32), pltpu.VMEM((ROWS, CW), F32),
            pltpu.VMEM((ROWS, COLS), BF16), pltpu.VMEM((ROWS, COLS), BF16),
            pltpu.VMEM((2 * HROWS, 2 * D), F32),
        ],
        compiler_params=pltpu.CompilerParams(vmem_limit_bytes=48 * 2**20),
        name="attend",
    )(starts, imports, lens, q, do, kvwin, slots, far)


def exit_kernel(
    starts_hbm, imports_hbm, dq, dkv_hbm, packed,
    dq_out, dk_out, dv_out,
    starts, imports, dkv, mine, theirs, tab, y1out, y1in, y2out, y2in, acc, tz, rz, wout, win, coll,
    fsem, ysend, yrecv, qsend, qrecv, local, wsend, wrecv, xsend, xrecv, zsend, zrecv,
    hsend, hrecv,
):
    xh, y, z, xl, co = position()
    me = xl * 2 + co
    c = ctx_of(xh, y, z)
    width = HEADS * D
    slots = 2 * IMPORTS
    first = fetch(
        (
            (starts_hbm, starts), (imports_hbm, imports), (dkv_hbm, dkv),
            (packed, mine.at[pl.ds(0, slots)]),
            (dq.at[rows(me * BLK, BLK), :], dq_out.at[:, rows(me * width, width)]),
        ),
        fsem,
    )
    mine[slots] = jnp.zeros((HDR, 2 * D), BF16)
    theirs[slots] = jnp.zeros((HDR, 2 * D), BF16)
    greet(all_peers(xh, y, z, xl, co))
    x_copy = remote(packed, theirs.at[pl.ds(0, slots)], xsend, xrecv, {"ctx_0": 1 - xh})
    x_copy.start()
    first[2].wait()
    back = ctx_shifted(xh, y, z, -1)
    w_copies = [
        remote(wout.at[s], win.at[s], wsend.at[s], wrecv.at[s], back) for s in range(REACH)
    ]
    wout[0] = dkv[0:TOK, :].astype(BF16)
    w_copies[0].start()
    for n in (0, 1, 3):
        first[n].wait()
    offset = own_header_offset(starts, c * TOK)
    places = []
    for shard_at in (c, ctx_of(1 - xh, y, z)):
        _, _, blocks = header_blocks(starts, imports, shard_at)
        places += [blocks[0:IMPORTS], blocks[IMPORTS:]]

    def find(blocks, base, shard):
        at = jnp.int32(slots)
        for m, (used, block) in enumerate(blocks):
            at = jnp.where(used & (block == shard), base + m, at)
        return at

    def collect(buffer, lists, n):
        shard = xh * (NY * NZ) + n
        return (
            buffer[find(lists[0], 0, shard)].astype(F32)
            + buffer[find(lists[1], IMPORTS, shard)].astype(F32)
        )

    def start_dq():
        copies = []
        for d in (2, 3, 1):
            peer, a = head_peer(xl, co, d)
            copies.append(remote(
                dq.at[rows(a * BLK, BLK), :], dq_out.at[:, rows(me * width, width)],
                qsend.at[d - 1], qrecv.at[d - 1], peer,
            ))
            copies[-1].start()
        return copies

    def own_part(n, carry):
        tab[n] = collect(mine, places[0:2], n)
        return carry

    def peer_part(n, carry):
        tab[n] = tab[n] + collect(theirs, places[2:4], n)
        return carry

    lax.fori_loop(0, NY * NZ, own_part, 0)
    x_copy.wait_recv()
    q_copies = start_dq()
    lax.fori_loop(0, NY * NZ, peer_part, 0)
    near, other = y_neighbours(y)
    across = 2 * lax.rem(lax.div(y, 2) + 1, 2) + lax.rem(y, 2)
    y_copies = []
    for n, to in enumerate((near, other)):
        y1out[n] = tab[rows(across * NZ, NZ), :, n * D:(n + 1) * D].astype(BF16)
        y_copies.append(remote(
            y1out.at[n], y1in.at[n], ysend.at[n], yrecv.at[n], {"ctx_1": to}
        ))
        y_copies[-1].start()
    w_copies[0].wait_recv()
    wout[1] = (win[0].astype(F32) + dkv[TOK:2 * TOK, :]).astype(BF16)
    w_copies[1].start()
    for n, to in enumerate((other, near)):
        y_copies[n].wait_recv()
        plane = rows(to * NZ, NZ)
        add = slice(n * D, (n + 1) * D)
        rest = slice((1 - n) * D, (2 - n) * D)
        y2out[n, :, :, add] = (tab[plane, :, add] + y1in[n].astype(F32)).astype(BF16)
        y2out[n, :, :, rest] = tab[plane, :, rest].astype(BF16)
        y_copies.append(remote(
            y2out.at[n], y2in.at[n], ysend.at[2 + n], yrecv.at[2 + n], {"ctx_1": to}
        ))
        y_copies[-1].start()
    w_copies[1].wait_recv()
    wout[2] = (win[1].astype(F32) + dkv[2 * TOK:3 * TOK, :]).astype(BF16)
    w_copies[2].start()
    for copy in y_copies[2:]:
        copy.wait_recv()
    acc[...] = tab[rows(y * NZ, NZ)] + y2in[0].astype(F32) + y2in[1].astype(F32)
    tz[...] = acc[...].astype(BF16)
    z_copies = []
    for d in (4, 3, 5, 2, 6, 1, 7):
        to = lax.rem(z + d, NZ)
        z_copies.append(remote(
            tz.at[to], rz.at[d - 1], zsend.at[d - 1], zrecv.at[d - 1], {"ctx_2": to}
        ))
        z_copies[-1].start()
    w_copies[2].wait_recv()
    wout[3] = (win[2].astype(F32) + dkv[3 * TOK:4 * TOK, :]).astype(BF16)
    w_copies[3].start()
    header = acc[z]
    for copy in z_copies:
        copy.wait_recv()
    for d in range(NZ - 1):
        header = header + rz[d].astype(F32)
    w_copies[3].wait_recv()
    for b in range(QB):
        part = slice(b * BLK, (b + 1) * BLK)
        keep = jnp.where(offset == b * BLK, 1.0, 0.0)
        coll[part, :] = (
            dkv[REACH * TOK + b * BLK:REACH * TOK + (b + 1) * BLK, :]
            + win[REACH - 1, part, :].astype(F32)
            + header * keep
        )
    h_copies = []
    for d in (2, 3, 1):
        peer, a = head_peer(xl, co, d)
        for n, dst in enumerate((dk_out, dv_out)):
            h_copies.append(remote(
                coll.at[rows(a * BLK, BLK), pl.ds(n * D, D)], dst.at[:, rows(me * D, D)],
                hsend.at[d - 1, n], hrecv.at[d - 1, n], peer,
            ))
            h_copies[-1].start()
    for n, dst in enumerate((dk_out, dv_out)):
        dst[:, rows(me * D, D)] = coll[rows(me * BLK, BLK), n * D:(n + 1) * D]
    first[4].wait()
    for copy in q_copies + h_copies:
        copy.wait_recv()
    for copy in y_copies + w_copies + q_copies + [x_copy] + z_copies + h_copies:
        copy.wait_send()


def leave(starts, imports, dq, dkv, packed):
    dma = pltpu.SemaphoreType.DMA
    hbm = pl.BlockSpec(memory_space=pl.ANY)
    vmem = pl.BlockSpec(memory_space=pltpu.VMEM)
    block = (HDR, 2 * D)
    return pl.pallas_call(
        exit_kernel,
        out_shape=(
            jax.ShapeDtypeStruct((BLK, GROUPS * HEADS * D), BF16),
            jax.ShapeDtypeStruct((BLK, GROUPS * D), F32),
            jax.ShapeDtypeStruct((BLK, GROUPS * D), F32),
        ),
        in_specs=[hbm] * 5,
        out_specs=(hbm, vmem, vmem),
        scratch_shapes=[
            pltpu.SMEM(starts.shape, jnp.int32), pltpu.SMEM(imports.shape, jnp.int32),
            pltpu.VMEM(((REACH + 1) * TOK, 2 * D), F32),
            pltpu.VMEM((2 * IMPORTS + 1, *block), BF16), pltpu.VMEM((2 * IMPORTS + 1, *block), BF16),
            pltpu.VMEM((NY * NZ, *block), F32),
            pltpu.VMEM((2, NZ, HDR, D), BF16), pltpu.VMEM((2, NZ, HDR, D), BF16),
            pltpu.VMEM((2, NZ, *block), BF16), pltpu.VMEM((2, NZ, *block), BF16),
            pltpu.VMEM((NZ, *block), F32), pltpu.VMEM((NZ, *block), BF16),
            pltpu.VMEM((NZ - 1, *block), BF16),
            pltpu.VMEM((REACH, TOK, 2 * D), BF16), pltpu.VMEM((REACH, TOK, 2 * D), BF16),
            pltpu.VMEM((TOK, 2 * D), F32),
            dma((5,)), dma((4,)), dma((4,)), dma((3,)), dma((3,)), dma,
            dma((REACH,)), dma((REACH,)), dma, dma, dma((NZ - 1,)), dma((NZ - 1,)),
            dma((3, 2)), dma((3, 2)),
        ],
        compiler_params=pltpu.CompilerParams(
            collective_id=1, has_side_effects=True, vmem_limit_bytes=32 * 2**20
        ),
        name="leave",
    )(starts, imports, dq, dkv, packed)


def per_device(queries, keys, values, output_gradient, file_starts, file_imports, header_lens):
    q, do, kvwin, slots, far = entry(
        file_starts, file_imports, queries, keys, values, output_gradient
    )
    dq, dkv, packed = compute(
        file_starts, file_imports, header_lens, q, do, kvwin, slots, far
    )
    dq_low, dk, dv = leave(file_starts, file_imports, dq, dkv, packed)
    return dq_low.astype(F32), dk, dv


def solution(mesh):
    split = Mesh(mesh.devices.reshape(NX, NY, NZ, 2, 2), AXES)
    placed = P(AXES, None)
    return jax.shard_map(
        per_device,
        mesh=split,
        in_specs=(placed, placed, placed, placed, P(), P(), P()),
        out_specs=(placed, placed, placed),
        check_vma=False,
    )
```

```python
import math

import jax
import jax.numpy as jnp
from jax import lax
from jax.experimental import pallas as pl
from jax.experimental.pallas import tpu as pltpu
from jax.sharding import Mesh
from jax.sharding import PartitionSpec as P

WIN = 1024
HDR = 64
TOK = 256
BLK = 64
D = 128
HEADS = 12
GROUPS = 4
REACH = WIN // TOK
QB = TOK // BLK
IMPORTS = 4
FILES = 33
VMEM_LIMIT = 60 * 2**20
NX, NY, NZ = 2, 4, 8
NCTX = NX * NY * NZ
WROWS = WIN + BLK
HROWS = IMPORTS * HDR
ROWS = WROWS + HROWS
CHUNK_HEADS = 4
CHUNKS = HEADS // CHUNK_HEADS
CW = CHUNK_HEADS * BLK
COLS = HEADS * BLK
SCALE = 1.0 / math.sqrt(D)
LOG2E = 1.4426950408889634
HIDDEN = -1e30
MESH = pl.DeviceIdType.MESH
F32 = jnp.float32
BF16 = jnp.bfloat16
AXES = ("ctx_0", "ctx_1", "ctx_2", "head_0", "head_1")


def position():
    return tuple(lax.axis_index(a) for a in AXES)


def ctx_of(xh, y, z):
    return xh * (NY * NZ) + y * NZ + z


def ctx_shifted(xh, y, z, step):
    c = lax.rem(ctx_of(xh, y, z) + (NCTX + step), NCTX)
    return {
        "ctx_0": lax.div(c, NY * NZ),
        "ctx_1": lax.rem(lax.div(c, NZ), NY),
        "ctx_2": lax.rem(c, NZ),
    }


def head_peer(xl, co, d):
    pxl = 1 - xl if d & 2 else xl
    pco = 1 - co if d & 1 else co
    return {"head_0": pxl, "head_1": pco}, pxl * 2 + pco


def greet(peers):
    barrier = pltpu.get_barrier_semaphore()
    for peer in peers:
        pl.semaphore_signal(barrier, inc=1, device_id=peer, device_id_type=MESH)
    pl.semaphore_wait(barrier, len(peers))


def remote(src, dst, send, recv, peer):
    return pltpu.make_async_remote_copy(
        src_ref=src, dst_ref=dst, send_sem=send, recv_sem=recv, device_id=peer, device_id_type=MESH
    )


def all_peers(xh, y, z, xl, co):
    peers = [head_peer(xl, co, d)[0] for d in (1, 2, 3)]
    peers += [{"ctx_2": lax.rem(z + d, NZ)} for d in range(1, NZ)]
    peers += [{"ctx_1": n} for n in y_neighbours(y)]
    peers += [{"ctx_0": 1 - xh}]
    peers += [ctx_shifted(xh, y, z, 1), ctx_shifted(xh, y, z, -1)]
    return peers


def rows(start, size):
    return pl.ds(pl.multiple_of(start, size), size)


def y_neighbours(y):
    near = y + 1 - 2 * lax.rem(y, 2)
    return near, NY - 1 - y


def file_at(starts, place):
    count = jnp.int32(-1)
    for f in range(starts.shape[0]):
        count = count + jnp.where(starts[f] <= place, 1, 0)
    return count


def header_blocks(starts, imports, c):
    lower = file_at(starts, c * TOK)
    upper = file_at(starts, c * TOK + TOK - 1)
    blocks = []
    for file in (lower, upper):
        for m in range(IMPORTS):
            g = imports[m, file]
            blocks.append((g >= 0, lax.div(starts[jnp.maximum(g, 0)], TOK)))
    return lower, upper, blocks


def own_header_offset(starts, base):
    offset = jnp.int32(0)
    for f in range(starts.shape[0]):
        at = starts[f] - base
        offset = offset + jnp.where((at >= 0) & (at < TOK), at, 0)
    return offset


def fetch(pairs, sems):
    copies = [pltpu.make_async_copy(src, dst, sems.at[n]) for n, (src, dst) in enumerate(pairs)]
    for copy in copies:
        copy.start()
    return copies


def fold8(x, op):
    out = x[0:8]
    for r in range(8, x.shape[0], 8):
        out = op(out, x[r:r + 8])
    return out


def rows_at(start, size, multiple):
    return pl.ds(pl.multiple_of(start, multiple), size)


def receive_inputs(q, k, v, do, small, tables, b, sems):
    starts, imports = tables
    xh, y, z, xl, co = position()
    me = xl * 2 + co
    c = ctx_of(xh, y, z)
    width = HEADS * D
    own = REACH * TOK
    kvwin, slots = b["kvwin"], b["slots"]
    here = fetch(
        (
            (k.at[:, rows(me * D, D)], kvwin.at[rows(own + me * BLK, BLK), pl.ds(0, D)]),
            (v.at[:, rows(me * D, D)], kvwin.at[rows(own + me * BLK, BLK), pl.ds(D, D)]),
            (q.at[:, rows(me * width, width)], b["q"].at[rows(me * BLK, BLK), :]),
            (do.at[:, rows(me * width, width)], b["do"].at[rows(me * BLK, BLK), :]),
        ),
        sems["here"],
    )
    greet(all_peers(xh, y, z, xl, co))
    kv_copies, q_copies = [], []
    for d in (2, 3, 1):
        peer, a = head_peer(xl, co, d)
        for n, src in enumerate((k, v)):
            kv_copies.append(remote(
                src.at[:, rows(a * D, D)],
                kvwin.at[rows(own + me * BLK, BLK), pl.ds(n * D, D)],
                sems["hsend"].at[d - 1, n], sems["hrecv"].at[d - 1, n], peer,
            ))
            kv_copies[-1].start()
    for d in (2, 3, 1):
        peer, a = head_peer(xl, co, d)
        for n, (src, dst) in enumerate(((q, b["q"]), (do, b["do"]))):
            q_copies.append(remote(
                src.at[:, rows(a * width, width)], dst.at[rows(me * BLK, BLK), :],
                sems["qsend"].at[d - 1, n], sems["qrecv"].at[d - 1, n], peer,
            ))
            q_copies[-1].start()
    for copy in small:
        copy.wait()
    offset = own_header_offset(starts, c * TOK)
    for copy in here[:2]:
        copy.wait()
    for copy in kv_copies:
        copy.wait_recv()

    forward = ctx_shifted(xh, y, z, 1)
    w_copies = [
        remote(
            kvwin.at[pl.ds((REACH - s) * TOK, TOK), :],
            kvwin.at[pl.ds((REACH - 1 - s) * TOK, TOK), :],
            sems["wsend"].at[s], sems["wrecv"].at[s], forward,
        )
        for s in range(REACH)
    ]
    w_copies[0].start()
    header = jnp.zeros((HDR, 2 * D), F32)
    for n in range(QB):
        keep = jnp.where(offset == n * BLK, 1.0, 0.0)
        header = header + kvwin[own + n * BLK:own + (n + 1) * BLK, :].astype(F32) * keep
    line = y * NZ + z
    slots[line] = header.astype(BF16)
    z_copies = []
    for d in (1, 7, 2, 6, 3, 5, 4):
        z_copies.append(remote(
            slots.at[line], slots.at[line],
            sems["zsend"].at[d - 1], sems["zrecv"].at[d - 1], {"ctx_2": lax.rem(z + d, NZ)},
        ))
        z_copies[-1].start()
    w_copies[0].wait_recv()
    w_copies[1].start()
    for copy in z_copies:
        copy.wait_recv()
    near, other = y_neighbours(y)
    y_copies = []
    for n, to in enumerate((near, other)):
        y_copies.append(remote(
            slots.at[rows(y * NZ, NZ)], slots.at[rows(y * NZ, NZ)],
            sems["ysend"].at[n], sems["yrecv"].at[n], {"ctx_1": to},
        ))
        y_copies[-1].start()
    w_copies[1].wait_recv()
    w_copies[2].start()
    for n, (came, to) in enumerate(((near, other), (other, near))):
        y_copies[n].wait_recv()
        part = slots.at[rows(came * NZ, NZ), :, pl.ds(n * D, D)]
        y_copies.append(
            remote(part, part, sems["ysend"].at[2 + n], sems["yrecv"].at[2 + n], {"ctx_1": to})
        )
        y_copies[-1].start()
    w_copies[2].wait_recv()
    w_copies[3].start()
    _, _, wanted = header_blocks(starts, imports, ctx_of(1 - xh, y, z))
    for copy in y_copies[2:]:
        copy.wait_recv()
    for m, (_, shard) in enumerate(wanted):
        b["picked"][m] = slots[lax.rem(shard, NY * NZ)]
    x_copy = remote(b["picked"], b["far"], sems["xsend"], sems["xrecv"], {"ctx_0": 1 - xh})
    x_copy.start()
    for copy in q_copies:
        copy.wait_recv()
    for copy in here[2:]:
        copy.wait()
    w_copies[3].wait_recv()
    x_copy.wait_recv()
    return kv_copies + q_copies + z_copies + w_copies + y_copies + [x_copy]


def attend_block(qb, starts, imports, lens, b):
    xh, y, z, _, _ = position()
    base = ctx_of(xh, y, z) * TOK
    place = base + qb * BLK
    lower = file_at(starts, base)
    file = file_at(starts, place)
    begin = starts[file]
    kc, vc, bias, s_ref, dp_ref = b["kc"], b["vc"], b["bias"], b["s"], b["dp"]
    p_ref, ds_ref, qs, dos = b["p"].at[qb], b["ds"].at[qb], b["qs"].at[qb], b["dos"].at[qb]
    step = 64
    kc[0:WROWS, :] = b["kvwin"][rows_at(qb * BLK, WROWS, BLK), 0:D]
    vc[0:WROWS, :] = b["kvwin"][rows_at(qb * BLK, WROWS, BLK), D:2 * D]
    key_place = lax.broadcasted_iota(jnp.int32, (WROWS, D), 0) + (place - WIN)
    bias[0:WROWS, :] = jnp.where(key_place >= begin, 0.0, HIDDEN)
    offsets = lax.broadcasted_iota(jnp.int32, (HDR, D), 0)
    for m in range(IMPORTS):
        g = imports[m, file]
        known = jnp.maximum(g, 0)
        length = jnp.where(g >= 0, lens[known], 0)
        here = pl.ds(WROWS + m * HDR, HDR)
        shard = lax.div(starts[known], TOK)
        at = lax.rem(shard, NY * NZ)
        which = jnp.where(file == lower, 0, IMPORTS) + m
        same = jnp.full((HDR, 2 * D), lax.div(shard, NY * NZ)) == xh
        rows_kv = jnp.where(
            same, b["slots"][at].astype(F32), b["far"][which].astype(F32)
        ).astype(BF16)
        kc[here, :] = rows_kv[:, 0:D]
        vc[here, :] = rows_kv[:, D:2 * D]
        bias[here, :] = jnp.where(offsets < length, 0.0, HIDDEN)
    for h in range(HEADS):
        qs[h * BLK:(h + 1) * BLK, :] = b["q"][rows(qb * BLK, BLK), h * D:(h + 1) * D]
        dos[h * BLK:(h + 1) * BLK, :] = b["do"][rows(qb * BLK, BLK), h * D:(h + 1) * D]

    t = lax.broadcasted_iota(jnp.int32, (BLK, CW), 0)
    p_at = lax.broadcasted_iota(jnp.int32, (BLK, CW), 1) % BLK
    nt = (((1,), (1,)), ((), ()))
    for chunk in range(CHUNKS):
        cols = slice(chunk * CW, (chunk + 1) * CW)
        s_ref[...] = lax.dot_general(kc[...], qs[cols, :], nt, preferred_element_type=F32)
        dp_ref[...] = lax.dot_general(vc[...], dos[cols, :], nt, preferred_element_type=F32)
        top = None
        for r in range(0, ROWS, step):
            s = s_ref[r:r + step, :] + jnp.concatenate([bias[r:r + step, :]] * (CW // D), axis=1)
            if r == 0:
                s = jnp.where(t > p_at, s, HIDDEN)
            if r == WIN:
                s = jnp.where(t <= p_at, s, HIDDEN)
            s_ref[r:r + step, :] = s
            part = fold8(s, jnp.maximum)
            top = part if top is None else jnp.maximum(top, part)
        top = jnp.max(top, axis=0, keepdims=True)
        total = jnp.zeros((8, CW), F32)
        centre = jnp.zeros((8, CW), F32)
        for r in range(0, ROWS, step):
            e = jnp.exp2((s_ref[r:r + step, :] - top) * (SCALE * LOG2E))
            s_ref[r:r + step, :] = e
            total = total + fold8(e, jnp.add)
            centre = centre + fold8(e * dp_ref[r:r + step, :], jnp.add)
        inverse = 1.0 / jnp.sum(total, axis=0, keepdims=True)
        centre = jnp.sum(centre, axis=0, keepdims=True) * inverse
        for r in range(0, ROWS, step):
            w = s_ref[r:r + step, :] * inverse
            p_ref[r:r + step, cols] = w.astype(BF16)
            ds_ref[r:r + step, cols] = (w * (dp_ref[r:r + step, :] - centre)).astype(BF16)
    dqt = lax.dot_general(
        kc[...], ds_ref[...], (((0,), (0,)), ((), ())), preferred_element_type=F32
    )
    dq = (dqt.T * SCALE).astype(BF16)
    for h in range(HEADS):
        b["dq"][qb, :, h * D:(h + 1) * D] = dq[h * BLK:(h + 1) * BLK]
    dv = jnp.dot(p_ref[WROWS:, :], dos[...], preferred_element_type=F32)
    dk = jnp.dot(ds_ref[WROWS:, :], qs[...], preferred_element_type=F32) * SCALE
    first = jnp.where(file == lower, 1.0, 0.0)
    for n, share in enumerate((first, 1.0 - first)):
        part = slice(n * HROWS, (n + 1) * HROWS)
        b["hacc"][part, 0:D] += dk * share
        b["hacc"][part, D:2 * D] += dv * share


def fused_kernel(starts_hbm, imports_hbm, lens_hbm, q, k, v, do, dq_out, dk_out, dv_out, *scratch):
    b = dict(zip(BUFFERS, scratch))
    sems = dict(zip(SEMAPHORES, scratch[len(BUFFERS):]))
    starts, imports, lens = b["starts"], b["imports"], b["lens"]
    xh, y, z, xl, co = position()
    me = xl * 2 + co
    c = ctx_of(xh, y, z)
    width = HEADS * D
    slots = 2 * IMPORTS
    dkv, tab, hacc = b["dkv"], b["tab"], b["hacc"]
    mine, theirs = b["mine"], b["theirs"]
    small = fetch(
        ((starts_hbm, starts), (imports_hbm, imports), (lens_hbm, lens)), sems["small"]
    )
    mine[slots] = jnp.zeros((HDR, 2 * D), BF16)
    theirs[slots] = jnp.zeros((HDR, 2 * D), BF16)
    dkv[...] = jnp.zeros_like(dkv)
    hacc[...] = jnp.zeros_like(hacc)
    sent = receive_inputs(q, k, v, do, small, (starts, imports), b, sems)
    offset = own_header_offset(starts, c * TOK)

    def dq_copy(to):
        return remote(
            b["dq"].at[to], dq_out.at[:, rows(me * width, width)],
            sems["dsend"].at[to], sems["drecv"].at[me],
            {"head_0": lax.div(to, 2), "head_1": lax.rem(to, 2)},
        )

    own_dq = pltpu.make_async_copy(
        b["dq"].at[me], dq_out.at[:, rows(me * width, width)], sems["dlocal"]
    )

    def one_block(i, carry):
        turn = jnp.where(i == 3, 0, jnp.where(i == 2, 1, i + 2))
        qb = lax.rem(me + turn, QB)
        attend_block(qb, starts, imports, lens, b)

        @pl.when(i < 3)
        def _():
            dq_copy(qb).start()

        return carry

    lax.fori_loop(0, QB, one_block, 0)
    own_dq.start()
    for m in range(slots):
        mine[m] = hacc[m * HDR:(m + 1) * HDR, :].astype(BF16)
    x_copy = remote(
        mine.at[pl.ds(0, slots)], theirs.at[pl.ds(0, slots)],
        sems["x2send"], sems["x2recv"], {"ctx_0": 1 - xh},
    )
    x_copy.start()

    def window_gradients(qb, carry):
        window = rows_at(qb * BLK, WROWS, BLK)
        dkv[window, 0:D] += jnp.dot(
            b["ds"][qb, 0:WROWS, :], b["qs"][qb], preferred_element_type=F32
        ) * SCALE
        dkv[window, D:2 * D] += jnp.dot(
            b["p"][qb, 0:WROWS, :], b["dos"][qb], preferred_element_type=F32
        )
        return carry

    lax.fori_loop(0, QB, window_gradients, 0)
    back = ctx_shifted(xh, y, z, -1)
    wout, win = b["wout"], b["win"]
    w_copies = [
        remote(wout.at[s], win.at[s], sems["v2send"].at[s], sems["v2recv"].at[s], back)
        for s in range(REACH)
    ]
    wout[0] = dkv[0:TOK, :].astype(BF16)
    w_copies[0].start()

    def pass_on(s):
        w_copies[s - 1].wait_recv()
        wout[s] = (win[s - 1].astype(F32) + dkv[s * TOK:(s + 1) * TOK, :]).astype(BF16)
        w_copies[s].start()

    places = []
    for shard_at in (c, ctx_of(1 - xh, y, z)):
        _, _, blocks = header_blocks(starts, imports, shard_at)
        places += [blocks[0:IMPORTS], blocks[IMPORTS:]]

    def find(blocks, first, shard):
        at = jnp.int32(slots)
        for m, (used, block) in enumerate(blocks):
            at = jnp.where(used & (block == shard), first + m, at)
        return at

    x_copy.wait_recv()

    def one_slot(n, carry):
        shard = xh * (NY * NZ) + n
        total = None
        for buffer, lists in ((mine, places[0:2]), (theirs, places[2:4])):
            for side in range(2):
                part = buffer[find(lists[side], side * IMPORTS, shard)].astype(F32)
                total = part if total is None else total + part
        tab[n] = total
        return carry

    lax.fori_loop(0, NY * NZ, one_slot, 0)
    near, other = y_neighbours(y)
    across = 2 * lax.rem(lax.div(y, 2) + 1, 2) + lax.rem(y, 2)
    y1out, y1in, y2out, y2in = b["y1out"], b["y1in"], b["y2out"], b["y2in"]
    y_copies = []
    for n, to in enumerate((near, other)):
        y1out[n] = tab[rows(across * NZ, NZ), :, n * D:(n + 1) * D].astype(BF16)
        y_copies.append(remote(
            y1out.at[n], y1in.at[n], sems["y2send"].at[n], sems["y2recv"].at[n], {"ctx_1": to}
        ))
        y_copies[-1].start()
    pass_on(1)
    for n, to in enumerate((other, near)):
        y_copies[n].wait_recv()
        plane = rows(to * NZ, NZ)
        add = slice(n * D, (n + 1) * D)
        rest = slice((1 - n) * D, (2 - n) * D)
        y2out[n, :, :, add] = (tab[plane, :, add] + y1in[n].astype(F32)).astype(BF16)
        y2out[n, :, :, rest] = tab[plane, :, rest].astype(BF16)
        y_copies.append(remote(
            y2out.at[n], y2in.at[n], sems["y2send"].at[2 + n], sems["y2recv"].at[2 + n],
            {"ctx_1": to},
        ))
        y_copies[-1].start()
    pass_on(2)
    for copy in y_copies[2:]:
        copy.wait_recv()
    acc, tz, rz, coll = b["acc"], b["tz"], b["rz"], b["coll"]
    acc[...] = tab[rows(y * NZ, NZ)] + y2in[0].astype(F32) + y2in[1].astype(F32)
    tz[...] = acc[...].astype(BF16)
    z_copies = []
    for d in (4, 3, 5, 2, 6, 1, 7):
        to = lax.rem(z + d, NZ)
        z_copies.append(remote(
            tz.at[to], rz.at[d - 1], sems["z2send"].at[d - 1], sems["z2recv"].at[d - 1],
            {"ctx_2": to},
        ))
        z_copies[-1].start()
    pass_on(3)
    header = acc[z]
    for copy in z_copies:
        copy.wait_recv()
    for d in range(NZ - 1):
        header = header + rz[d].astype(F32)
    w_copies[3].wait_recv()
    for n in range(QB):
        part = slice(n * BLK, (n + 1) * BLK)
        keep = jnp.where(offset == n * BLK, 1.0, 0.0)
        coll[part, :] = (
            dkv[REACH * TOK + n * BLK:REACH * TOK + (n + 1) * BLK, :]
            + win[REACH - 1, part, :].astype(F32)
            + header * keep
        )
    h_copies = []
    for d in (2, 3, 1):
        peer, a = head_peer(xl, co, d)
        for n, dst in enumerate((dk_out, dv_out)):
            h_copies.append(remote(
                coll.at[rows(a * BLK, BLK), pl.ds(n * D, D)], dst.at[:, rows(me * D, D)],
                sems["h2send"].at[d - 1, n], sems["h2recv"].at[d - 1, n], peer,
            ))
            h_copies[-1].start()
    for n, dst in enumerate((dk_out, dv_out)):
        dst[:, rows(me * D, D)] = coll[rows(me * BLK, BLK), n * D:(n + 1) * D]
    own_dq.wait()
    for d in (1, 2, 3):
        _, a = head_peer(xl, co, d)
        remote(
            b["dq"].at[a], dq_out.at[:, rows(a * width, width)],
            sems["dsend"].at[a], sems["drecv"].at[a],
            {"head_0": lax.div(a, 2), "head_1": lax.rem(a, 2)},
        ).wait()
    for copy in h_copies:
        copy.wait_recv()
    for copy in sent + y_copies + w_copies + [x_copy] + z_copies + h_copies:
        copy.wait_send()


def memory():
    vmem, smem = pltpu.VMEM, pltpu.SMEM
    dma = pltpu.SemaphoreType.DMA
    block = (HDR, 2 * D)
    buffers = dict(
        starts=smem((FILES,), jnp.int32), imports=smem((IMPORTS, FILES), jnp.int32),
        lens=smem((FILES,), jnp.int32),
        q=vmem((TOK, HEADS * D), BF16), do=vmem((TOK, HEADS * D), BF16),
        kvwin=vmem(((REACH + 1) * TOK, 2 * D), BF16),
        slots=vmem((NY * NZ, *block), BF16),
        picked=vmem((2 * IMPORTS, *block), BF16), far=vmem((2 * IMPORTS, *block), BF16),
        kc=vmem((ROWS, D), BF16), vc=vmem((ROWS, D), BF16), bias=vmem((ROWS, D), F32),
        qs=vmem((QB, COLS, D), BF16), dos=vmem((QB, COLS, D), BF16),
        s=vmem((ROWS, CW), F32), dp=vmem((ROWS, CW), F32),
        p=vmem((QB, ROWS, COLS), BF16), ds=vmem((QB, ROWS, COLS), BF16),
        hacc=vmem((2 * HROWS, 2 * D), F32),
        dq=vmem((QB, BLK, HEADS * D), BF16),
        dkv=vmem(((REACH + 1) * TOK, 2 * D), F32),
        mine=vmem((2 * IMPORTS + 1, *block), BF16), theirs=vmem((2 * IMPORTS + 1, *block), BF16),
        tab=vmem((NY * NZ, *block), F32),
        y1out=vmem((2, NZ, HDR, D), BF16), y1in=vmem((2, NZ, HDR, D), BF16),
        y2out=vmem((2, NZ, *block), BF16), y2in=vmem((2, NZ, *block), BF16),
        acc=vmem((NZ, *block), F32), tz=vmem((NZ, *block), BF16),
        rz=vmem((NZ - 1, *block), BF16),
        wout=vmem((REACH, TOK, 2 * D), BF16), win=vmem((REACH, TOK, 2 * D), BF16),
        coll=vmem((TOK, 2 * D), F32),
    )
    one, four, window, line, pairs = dma, dma((4,)), dma((REACH,)), dma((NZ - 1,)), dma((3, 2))
    semaphores = dict(
        small=dma((3,)), here=four, hsend=pairs, hrecv=pairs, qsend=pairs, qrecv=pairs,
        wsend=window, wrecv=window, zsend=line, zrecv=line, xsend=one, xrecv=one,
        ysend=four, yrecv=four, dsend=four, drecv=four, dlocal=one,
        v2send=window, v2recv=window, z2send=line, z2recv=line, x2send=one, x2recv=one,
        y2send=four, y2recv=four, h2send=pairs, h2recv=pairs,
    )
    return buffers, semaphores


BUFFERS, SEMAPHORES = (tuple(d) for d in memory())


def per_device(queries, keys, values, output_gradient, file_starts, file_imports, header_lens):
    hbm = pl.BlockSpec(memory_space=pl.ANY)
    vmem = pl.BlockSpec(memory_space=pltpu.VMEM)
    buffers, semaphores = memory()
    dq, dk, dv = pl.pallas_call(
        fused_kernel,
        out_shape=(
            jax.ShapeDtypeStruct((BLK, GROUPS * HEADS * D), BF16),
            jax.ShapeDtypeStruct((BLK, GROUPS * D), F32),
            jax.ShapeDtypeStruct((BLK, GROUPS * D), F32),
        ),
        in_specs=[hbm] * 7,
        out_specs=(hbm, vmem, vmem),
        scratch_shapes=[*buffers.values(), *semaphores.values()],
        compiler_params=pltpu.CompilerParams(
            collective_id=0, has_side_effects=True, vmem_limit_bytes=VMEM_LIMIT
        ),
        name="attention_backward",
    )(
        file_starts, file_imports.T, header_lens, queries, keys, values, output_gradient
    )
    return dq.astype(F32), dk, dv


def solution(mesh):
    split = Mesh(mesh.devices.reshape(NX, NY, NZ, 2, 2), AXES)
    placed = P(AXES, None)
    return jax.shard_map(
        per_device,
        mesh=split,
        in_specs=(placed, placed, placed, placed, P(), P(), P()),
        out_specs=(placed, placed, placed),
        check_vma=False,
    )
```

```python
import math

import jax
import jax.numpy as jnp
from jax import lax
from jax.experimental import pallas as pl
from jax.experimental.pallas import tpu as pltpu
from jax.sharding import Mesh
from jax.sharding import PartitionSpec as P

WIN = 1024
HDR = 64
TOK = 256
BLK = 64
D = 128
HEADS = 12
GROUPS = 4
REACH = WIN // TOK
QB = TOK // BLK
IMPORTS = 4
FILES = 33
VMEM_LIMIT = 60 * 2**20
NX, NY, NZ = 2, 4, 8
NCTX = NX * NY * NZ
WROWS = WIN + BLK
HROWS = IMPORTS * HDR
ROWS = WROWS + HROWS
CHUNK_HEADS = 4
CHUNKS = HEADS // CHUNK_HEADS
CW = CHUNK_HEADS * BLK
COLS = HEADS * BLK
SCALE = 1.0 / math.sqrt(D)
LOG2E = 1.4426950408889634
HIDDEN = -1e30
MESH = pl.DeviceIdType.MESH
F32 = jnp.float32
BF16 = jnp.bfloat16
AXES = ("ctx_0", "ctx_1", "ctx_2", "head_0", "head_1")


def position():
    return tuple(lax.axis_index(a) for a in AXES)


def ctx_of(xh, y, z):
    return xh * (NY * NZ) + y * NZ + z


def ctx_shifted(xh, y, z, step):
    c = lax.rem(ctx_of(xh, y, z) + (NCTX + step), NCTX)
    return {
        "ctx_0": lax.div(c, NY * NZ),
        "ctx_1": lax.rem(lax.div(c, NZ), NY),
        "ctx_2": lax.rem(c, NZ),
    }


def head_peer(xl, co, d):
    pxl = 1 - xl if d & 2 else xl
    pco = 1 - co if d & 1 else co
    return {"head_0": pxl, "head_1": pco}, pxl * 2 + pco


def greet(peers):
    barrier = pltpu.get_barrier_semaphore()
    for peer in peers:
        pl.semaphore_signal(barrier, inc=1, device_id=peer, device_id_type=MESH)
    pl.semaphore_wait(barrier, len(peers))


def remote(src, dst, send, recv, peer):
    return pltpu.make_async_remote_copy(
        src_ref=src, dst_ref=dst, send_sem=send, recv_sem=recv, device_id=peer, device_id_type=MESH
    )


def all_peers(xh, y, z, xl, co):
    peers = [head_peer(xl, co, d)[0] for d in (1, 2, 3)]
    peers += [{"ctx_2": lax.rem(z + d, NZ)} for d in range(1, NZ)]
    peers += [{"ctx_1": n} for n in y_neighbours(y)]
    peers += [{"ctx_0": 1 - xh}]
    peers += [ctx_shifted(xh, y, z, 1), ctx_shifted(xh, y, z, -1)]
    return peers


def rows(start, size):
    return pl.ds(pl.multiple_of(start, size), size)


def y_neighbours(y):
    near = y + 1 - 2 * lax.rem(y, 2)
    return near, NY - 1 - y


def file_at(starts, place):
    count = jnp.int32(-1)
    for f in range(starts.shape[0]):
        count = count + jnp.where(starts[f] <= place, 1, 0)
    return count


def header_blocks(starts, imports, c):
    lower = file_at(starts, c * TOK)
    upper = file_at(starts, c * TOK + TOK - 1)
    blocks = []
    for file in (lower, upper):
        for m in range(IMPORTS):
            g = imports[m, file]
            blocks.append((g >= 0, lax.div(starts[jnp.maximum(g, 0)], TOK)))
    return lower, upper, blocks


def own_header_offset(starts, base):
    offset = jnp.int32(0)
    for f in range(starts.shape[0]):
        at = starts[f] - base
        offset = offset + jnp.where((at >= 0) & (at < TOK), at, 0)
    return offset


def fetch(pairs, sems):
    copies = [pltpu.make_async_copy(src, dst, sems.at[n]) for n, (src, dst) in enumerate(pairs)]
    for copy in copies:
        copy.start()
    return copies


def fold8(x, op):
    out = x[0:8]
    for r in range(8, x.shape[0], 8):
        out = op(out, x[r:r + 8])
    return out


def rows_at(start, size, multiple):
    return pl.ds(pl.multiple_of(start, multiple), size)


def receive_inputs(q, k, v, do, small, tables, b, sems):
    starts, imports = tables
    xh, y, z, xl, co = position()
    me = xl * 2 + co
    c = ctx_of(xh, y, z)
    width = HEADS * D
    own = REACH * TOK
    kvwin, slots = b["kvwin"], (b["slots_k"], b["slots_v"])
    here = fetch(
        (
            (k.at[:, rows(me * D, D)], kvwin.at[rows(own + me * BLK, BLK), pl.ds(0, D)]),
            (v.at[:, rows(me * D, D)], kvwin.at[rows(own + me * BLK, BLK), pl.ds(D, D)]),
            (q.at[:, rows(me * width, width)], b["q"].at[rows(me * BLK, BLK), :]),
            (do.at[:, rows(me * width, width)], b["do"].at[rows(me * BLK, BLK), :]),
        ),
        sems["here"],
    )
    greet(all_peers(xh, y, z, xl, co))
    kv_copies, q_copies = [], []
    for d in (2, 3, 1):
        peer, a = head_peer(xl, co, d)
        for n, src in enumerate((k, v)):
            kv_copies.append(remote(
                src.at[:, rows(a * D, D)],
                kvwin.at[rows(own + me * BLK, BLK), pl.ds(n * D, D)],
                sems["hsend"].at[d - 1, n], sems["hrecv"].at[d - 1, n], peer,
            ))
            kv_copies[-1].start()
    for d in (2, 3, 1):
        peer, a = head_peer(xl, co, d)
        for n, (src, dst) in enumerate(((q, b["q"]), (do, b["do"]))):
            q_copies.append(remote(
                src.at[:, rows(a * width, width)], dst.at[rows(me * BLK, BLK), :],
                sems["qsend"].at[d - 1, n], sems["qrecv"].at[d - 1, n], peer,
            ))
            q_copies[-1].start()
    for copy in small:
        copy.wait()
    offset = own_header_offset(starts, c * TOK)
    for copy in here[:2]:
        copy.wait()
    for copy in kv_copies:
        copy.wait_recv()

    forward = ctx_shifted(xh, y, z, 1)
    w_copies = [
        remote(
            kvwin.at[pl.ds((REACH - s) * TOK, TOK), :],
            kvwin.at[pl.ds((REACH - 1 - s) * TOK, TOK), :],
            sems["wsend"].at[s], sems["wrecv"].at[s], forward,
        )
        for s in range(REACH)
    ]
    w_copies[0].start()
    header = jnp.zeros((HDR, 2 * D), F32)
    for n in range(QB):
        keep = jnp.where(offset == n * BLK, 1.0, 0.0)
        header = header + kvwin[own + n * BLK:own + (n + 1) * BLK, :].astype(F32) * keep
    line = y * NZ + z
    for n in range(2):
        slots[n][line] = header[:, n * D:(n + 1) * D].astype(BF16)
    z_copies = ([], [])
    for n in range(2):
        for d in (1, 7, 2, 6, 3, 5, 4):
            part = slots[n].at[line]
            z_copies[n].append(remote(
                part, part, sems["zsend"].at[n, d - 1], sems["zrecv"].at[n, d - 1],
                {"ctx_2": lax.rem(z + d, NZ)},
            ))
            z_copies[n][-1].start()
    near, other = y_neighbours(y)
    near_copies, far_copies, x_copies = ([], []), ([], []), []

    def to_neighbours(n):
        for copy in z_copies[n]:
            copy.wait_recv()
        for d, to in enumerate((near, other)):
            part = slots[n].at[rows(y * NZ, NZ)]
            near_copies[n].append(remote(
                part, part, sems["ysend"].at[n, d], sems["yrecv"].at[n, d], {"ctx_1": to}
            ))
            near_copies[n][-1].start()

    def to_opposite(n):
        for d, (came, to) in enumerate(((near, other), (other, near))):
            near_copies[n][d].wait_recv()
            part = slots[n].at[rows(came * NZ + d * (NZ // 2), NZ // 2)]
            far_copies[n].append(remote(
                part, part, sems["ysend"].at[n, 2 + d], sems["yrecv"].at[n, 2 + d],
                {"ctx_1": to},
            ))
            far_copies[n][-1].start()

    def to_other_half(n):
        for copy in far_copies[n]:
            copy.wait_recv()
        for m, (_, shard) in enumerate(wanted):
            b["picked"][n, m] = slots[n][lax.rem(shard, NY * NZ)]
        x_copies.append(remote(
            b["picked"].at[n], b["far"].at[n], sems["xsend"].at[n], sems["xrecv"].at[n],
            {"ctx_0": 1 - xh},
        ))
        x_copies[-1].start()

    _, _, wanted = header_blocks(starts, imports, ctx_of(1 - xh, y, z))
    to_neighbours(0)
    w_copies[0].wait_recv()
    w_copies[1].start()
    to_neighbours(1)
    to_opposite(0)
    to_opposite(1)
    w_copies[1].wait_recv()
    w_copies[2].start()
    to_other_half(0)
    to_other_half(1)
    w_copies[2].wait_recv()
    w_copies[3].start()
    for copy in q_copies:
        copy.wait_recv()
    for copy in here[2:]:
        copy.wait()
    w_copies[3].wait_recv()
    for copy in x_copies:
        copy.wait_recv()
    y_copies = near_copies[0] + near_copies[1] + far_copies[0] + far_copies[1]
    return kv_copies + q_copies + z_copies[0] + z_copies[1] + w_copies + y_copies + x_copies


def attend_block(qb, starts, imports, lens, b):
    xh, y, z, _, _ = position()
    base = ctx_of(xh, y, z) * TOK
    place = base + qb * BLK
    lower = file_at(starts, base)
    file = file_at(starts, place)
    begin = starts[file]
    kc, vc, bias, s_ref, dp_ref = b["kc"], b["vc"], b["bias"], b["s"], b["dp"]
    p_ref, ds_ref, qs, dos = b["p"].at[qb], b["ds"].at[qb], b["qs"].at[qb], b["dos"].at[qb]
    step = 64
    kc[0:WROWS, :] = b["kvwin"][rows_at(qb * BLK, WROWS, BLK), 0:D]
    vc[0:WROWS, :] = b["kvwin"][rows_at(qb * BLK, WROWS, BLK), D:2 * D]
    key_place = lax.broadcasted_iota(jnp.int32, (WROWS, D), 0) + (place - WIN)
    bias[0:WROWS, :] = jnp.where(key_place >= begin, 0.0, HIDDEN)
    offsets = lax.broadcasted_iota(jnp.int32, (HDR, D), 0)
    for m in range(IMPORTS):
        g = imports[m, file]
        known = jnp.maximum(g, 0)
        length = jnp.where(g >= 0, lens[known], 0)
        here = pl.ds(WROWS + m * HDR, HDR)
        shard = lax.div(starts[known], TOK)
        at = lax.rem(shard, NY * NZ)
        which = jnp.where(file == lower, 0, IMPORTS) + m
        same = jnp.full((HDR, D), lax.div(shard, NY * NZ)) == xh
        for n, (dst, slots) in enumerate(((kc, b["slots_k"]), (vc, b["slots_v"]))):
            near = slots[at].astype(F32)
            dst[here, :] = jnp.where(same, near, b["far"][n, which].astype(F32)).astype(BF16)
        bias[here, :] = jnp.where(offsets < length, 0.0, HIDDEN)
    for h in range(HEADS):
        qs[h * BLK:(h + 1) * BLK, :] = b["q"][rows(qb * BLK, BLK), h * D:(h + 1) * D]
        dos[h * BLK:(h + 1) * BLK, :] = b["do"][rows(qb * BLK, BLK), h * D:(h + 1) * D]

    t = lax.broadcasted_iota(jnp.int32, (BLK, CW), 0)
    p_at = lax.broadcasted_iota(jnp.int32, (BLK, CW), 1) % BLK
    nt = (((1,), (1,)), ((), ()))
    for chunk in range(CHUNKS):
        cols = slice(chunk * CW, (chunk + 1) * CW)
        s_ref[...] = lax.dot_general(kc[...], qs[cols, :], nt, preferred_element_type=F32)
        dp_ref[...] = lax.dot_general(vc[...], dos[cols, :], nt, preferred_element_type=F32)
        top = None
        for r in range(0, ROWS, step):
            s = s_ref[r:r + step, :] + jnp.concatenate([bias[r:r + step, :]] * (CW // D), axis=1)
            if r == 0:
                s = jnp.where(t > p_at, s, HIDDEN)
            if r == WIN:
                s = jnp.where(t <= p_at, s, HIDDEN)
            s_ref[r:r + step, :] = s
            part = fold8(s, jnp.maximum)
            top = part if top is None else jnp.maximum(top, part)
        top = jnp.max(top, axis=0, keepdims=True)
        total = jnp.zeros((8, CW), F32)
        centre = jnp.zeros((8, CW), F32)
        for r in range(0, ROWS, step):
            e = jnp.exp2((s_ref[r:r + step, :] - top) * (SCALE * LOG2E))
            s_ref[r:r + step, :] = e
            total = total + fold8(e, jnp.add)
            centre = centre + fold8(e * dp_ref[r:r + step, :], jnp.add)
        inverse = 1.0 / jnp.sum(total, axis=0, keepdims=True)
        centre = jnp.sum(centre, axis=0, keepdims=True) * inverse
        for r in range(0, ROWS, step):
            w = s_ref[r:r + step, :] * inverse
            p_ref[r:r + step, cols] = w.astype(BF16)
            ds_ref[r:r + step, cols] = (w * (dp_ref[r:r + step, :] - centre)).astype(BF16)
    dqt = lax.dot_general(
        kc[...], ds_ref[...], (((0,), (0,)), ((), ())), preferred_element_type=F32
    )
    dq = (dqt.T * SCALE).astype(BF16)
    for h in range(HEADS):
        b["dq"][qb, :, h * D:(h + 1) * D] = dq[h * BLK:(h + 1) * BLK]
    dv = jnp.dot(p_ref[WROWS:, :], dos[...], preferred_element_type=F32)
    dk = jnp.dot(ds_ref[WROWS:, :], qs[...], preferred_element_type=F32) * SCALE
    first = jnp.where(file == lower, 1.0, 0.0)
    for n, share in enumerate((first, 1.0 - first)):
        part = slice(n * HROWS, (n + 1) * HROWS)
        b["hacc"][part, 0:D] += dk * share
        b["hacc"][part, D:2 * D] += dv * share


def fused_kernel(starts_hbm, imports_hbm, lens_hbm, q, k, v, do, dq_out, dk_out, dv_out, *scratch):
    b = dict(zip(BUFFERS, scratch))
    sems = dict(zip(SEMAPHORES, scratch[len(BUFFERS):]))
    starts, imports, lens = b["starts"], b["imports"], b["lens"]
    xh, y, z, xl, co = position()
    me = xl * 2 + co
    c = ctx_of(xh, y, z)
    width = HEADS * D
    slots = 2 * IMPORTS
    dkv, tab, hacc = b["dkv"], b["tab"], b["hacc"]
    mine, theirs = b["mine"], (b["theirs_k"], b["theirs_v"])
    small = fetch(
        ((starts_hbm, starts), (imports_hbm, imports), (lens_hbm, lens)), sems["small"]
    )
    for n in range(2):
        mine[n, slots] = jnp.zeros((HDR, D), BF16)
        theirs[n][slots] = jnp.zeros((HDR, D), BF16)
    dkv[...] = jnp.zeros_like(dkv)
    hacc[...] = jnp.zeros_like(hacc)
    sent = receive_inputs(q, k, v, do, small, (starts, imports), b, sems)
    offset = own_header_offset(starts, c * TOK)

    def dq_copy(to):
        return remote(
            b["dq"].at[to], dq_out.at[:, rows(me * width, width)],
            sems["dsend"].at[to], sems["drecv"].at[me],
            {"head_0": lax.div(to, 2), "head_1": lax.rem(to, 2)},
        )

    own_dq = pltpu.make_async_copy(
        b["dq"].at[me], dq_out.at[:, rows(me * width, width)], sems["dlocal"]
    )

    def one_block(i, carry):
        turn = jnp.where(i == 3, 0, jnp.where(i == 2, 1, i + 2))
        qb = lax.rem(me + turn, QB)
        attend_block(qb, starts, imports, lens, b)

        @pl.when(i < 3)
        def _():
            dq_copy(qb).start()

        return carry

    lax.fori_loop(0, QB, one_block, 0)
    own_dq.start()
    halves = (slice(0, D), slice(D, 2 * D))
    x_copies = []
    for n, half in enumerate(halves):
        for m in range(slots):
            mine[n, m] = hacc[m * HDR:(m + 1) * HDR, half].astype(BF16)
        x_copies.append(remote(
            mine.at[n, pl.ds(0, slots)], theirs[n].at[pl.ds(0, slots)],
            sems["x2send"].at[n], sems["x2recv"].at[n], {"ctx_0": 1 - xh},
        ))
        x_copies[-1].start()

    def window_gradients(qb, carry):
        window = rows_at(qb * BLK, WROWS, BLK)
        dkv[window, 0:D] += jnp.dot(
            b["ds"][qb, 0:WROWS, :], b["qs"][qb], preferred_element_type=F32
        ) * SCALE
        dkv[window, D:2 * D] += jnp.dot(
            b["p"][qb, 0:WROWS, :], b["dos"][qb], preferred_element_type=F32
        )
        return carry

    lax.fori_loop(0, QB, window_gradients, 0)
    back = ctx_shifted(xh, y, z, -1)
    wout, win = b["wout"], b["win"]
    w_copies = [
        remote(wout.at[s], win.at[s], sems["v2send"].at[s], sems["v2recv"].at[s], back)
        for s in range(REACH)
    ]
    wout[0] = dkv[0:TOK, :].astype(BF16)
    w_copies[0].start()

    def pass_on(s):
        w_copies[s - 1].wait_recv()
        wout[s] = (win[s - 1].astype(F32) + dkv[s * TOK:(s + 1) * TOK, :]).astype(BF16)
        w_copies[s].start()

    places = []
    for shard_at in (c, ctx_of(1 - xh, y, z)):
        _, _, blocks = header_blocks(starts, imports, shard_at)
        places += [blocks[0:IMPORTS], blocks[IMPORTS:]]

    def find(blocks, first, shard):
        at = jnp.int32(slots)
        for m, (used, block) in enumerate(blocks):
            at = jnp.where(used & (block == shard), first + m, at)
        return at

    near, other = y_neighbours(y)
    across = 2 * lax.rem(lax.div(y, 2) + 1, 2) + lax.rem(y, 2)
    y1out, y1in, y2out, y2in = b["y1out"], b["y1in"], b["y2out"], b["y2in"]
    acc, tz, rz, coll = b["acc"], b["tz"], b["rz"], b["coll"]
    near_copies, far_copies, z_copies = ([], []), ([], []), ([], [])
    middle = NZ // 2

    def to_opposite(n):
        x_copies[n].wait_recv()

        def one_slot(i, carry):
            shard = xh * (NY * NZ) + i
            total = None
            for buffer, lists in ((mine.at[n], places[0:2]), (theirs[n], places[2:4])):
                for side in range(2):
                    part = buffer[find(lists[side], side * IMPORTS, shard)].astype(F32)
                    total = part if total is None else total + part
            tab[n, i] = total
            return carry

        lax.fori_loop(0, NY * NZ, one_slot, 0)
        for d, to in enumerate((near, other)):
            y1out[n, d] = tab[n, rows(across * NZ + d * middle, middle)].astype(BF16)
            far_copies[n].append(remote(
                y1out.at[n, d], y1in.at[n, d],
                sems["y2send"].at[n, d], sems["y2recv"].at[n, d], {"ctx_1": to},
            ))
            far_copies[n][-1].start()

    def to_neighbours(n):
        for d, to in enumerate((other, near)):
            far_copies[n][d].wait_recv()
            add, rest = d * middle, (1 - d) * middle
            y2out[n, d, pl.ds(add, middle)] = (
                tab[n, rows(to * NZ + add, middle)] + y1in[n, d].astype(F32)
            ).astype(BF16)
            y2out[n, d, pl.ds(rest, middle)] = tab[n, rows(to * NZ + rest, middle)].astype(BF16)
            near_copies[n].append(remote(
                y2out.at[n, d], y2in.at[n, d],
                sems["y2send"].at[n, 2 + d], sems["y2recv"].at[n, 2 + d], {"ctx_1": to},
            ))
            near_copies[n][-1].start()

    def to_owners(n):
        for copy in near_copies[n]:
            copy.wait_recv()
        acc[n] = (
            tab[n, rows(y * NZ, NZ)] + y2in[n, 0].astype(F32) + y2in[n, 1].astype(F32)
        )
        tz[n] = acc[n].astype(BF16)
        for d in (4, 3, 5, 2, 6, 1, 7):
            to = lax.rem(z + d, NZ)
            z_copies[n].append(remote(
                tz.at[n, to], rz.at[n, d - 1],
                sems["z2send"].at[n, d - 1], sems["z2recv"].at[n, d - 1], {"ctx_2": to},
            ))
            z_copies[n][-1].start()

    to_opposite(0)
    pass_on(1)
    to_opposite(1)
    to_neighbours(0)
    pass_on(2)
    to_neighbours(1)
    to_owners(0)
    pass_on(3)
    to_owners(1)
    headers = []
    for n in range(2):
        header = acc[n, z]
        for copy in z_copies[n]:
            copy.wait_recv()
        for d in range(NZ - 1):
            header = header + rz[n, d].astype(F32)
        headers.append(header)
    w_copies[3].wait_recv()
    for n in range(QB):
        part = slice(n * BLK, (n + 1) * BLK)
        keep = jnp.where(offset == n * BLK, 1.0, 0.0)
        for half, header in zip(halves, headers):
            coll[part, half] = (
                dkv[REACH * TOK + n * BLK:REACH * TOK + (n + 1) * BLK, half]
                + win[REACH - 1, part, half].astype(F32)
                + header * keep
            )
    h_copies = []
    for d in (2, 3, 1):
        peer, a = head_peer(xl, co, d)
        for n, dst in enumerate((dk_out, dv_out)):
            h_copies.append(remote(
                coll.at[rows(a * BLK, BLK), pl.ds(n * D, D)], dst.at[:, rows(me * D, D)],
                sems["h2send"].at[d - 1, n], sems["h2recv"].at[d - 1, n], peer,
            ))
            h_copies[-1].start()
    for n, dst in enumerate((dk_out, dv_out)):
        dst[:, rows(me * D, D)] = coll[rows(me * BLK, BLK), n * D:(n + 1) * D]
    own_dq.wait()
    for d in (1, 2, 3):
        _, a = head_peer(xl, co, d)
        remote(
            b["dq"].at[a], dq_out.at[:, rows(a * width, width)],
            sems["dsend"].at[a], sems["drecv"].at[a],
            {"head_0": lax.div(a, 2), "head_1": lax.rem(a, 2)},
        ).wait()
    for copy in h_copies:
        copy.wait_recv()
    for pair in (near_copies, far_copies, z_copies):
        sent = sent + pair[0] + pair[1]
    for copy in sent + w_copies + x_copies + h_copies:
        copy.wait_send()


def memory():
    vmem, smem = pltpu.VMEM, pltpu.SMEM
    dma = pltpu.SemaphoreType.DMA
    half = (HDR, D)
    buffers = dict(
        starts=smem((FILES,), jnp.int32), imports=smem((IMPORTS, FILES), jnp.int32),
        lens=smem((FILES,), jnp.int32),
        q=vmem((TOK, HEADS * D), BF16), do=vmem((TOK, HEADS * D), BF16),
        kvwin=vmem(((REACH + 1) * TOK, 2 * D), BF16),
        slots_k=vmem((NY * NZ, *half), BF16), slots_v=vmem((NY * NZ, *half), BF16),
        picked=vmem((2, 2 * IMPORTS, HDR, D), BF16), far=vmem((2, 2 * IMPORTS, HDR, D), BF16),
        kc=vmem((ROWS, D), BF16), vc=vmem((ROWS, D), BF16), bias=vmem((ROWS, D), F32),
        qs=vmem((QB, COLS, D), BF16), dos=vmem((QB, COLS, D), BF16),
        s=vmem((ROWS, CW), F32), dp=vmem((ROWS, CW), F32),
        p=vmem((QB, ROWS, COLS), BF16), ds=vmem((QB, ROWS, COLS), BF16),
        hacc=vmem((2 * HROWS, 2 * D), F32),
        dq=vmem((QB, BLK, HEADS * D), BF16),
        dkv=vmem(((REACH + 1) * TOK, 2 * D), F32),
        mine=vmem((2, 2 * IMPORTS + 1, *half), BF16),
        theirs_k=vmem((2 * IMPORTS + 1, *half), BF16),
        theirs_v=vmem((2 * IMPORTS + 1, *half), BF16),
        tab=vmem((2, NY * NZ, *half), F32),
        y1out=vmem((2, 2, NZ // 2, *half), BF16), y1in=vmem((2, 2, NZ // 2, *half), BF16),
        y2out=vmem((2, 2, NZ, *half), BF16), y2in=vmem((2, 2, NZ, *half), BF16),
        acc=vmem((2, NZ, *half), F32), tz=vmem((2, NZ, *half), BF16),
        rz=vmem((2, NZ - 1, *half), BF16),
        wout=vmem((REACH, TOK, 2 * D), BF16), win=vmem((REACH, TOK, 2 * D), BF16),
        coll=vmem((TOK, 2 * D), F32),
    )
    four, window, line, pairs = dma((4,)), dma((REACH,)), dma((2, NZ - 1)), dma((3, 2))
    two, steps = dma((2,)), dma((2, 4))
    semaphores = dict(
        small=dma((3,)), here=four, hsend=pairs, hrecv=pairs, qsend=pairs, qrecv=pairs,
        wsend=window, wrecv=window, zsend=line, zrecv=line, xsend=two, xrecv=two,
        ysend=steps, yrecv=steps, dsend=four, drecv=four, dlocal=dma,
        v2send=window, v2recv=window, z2send=line, z2recv=line, x2send=two, x2recv=two,
        y2send=steps, y2recv=steps, h2send=pairs, h2recv=pairs,
    )
    return buffers, semaphores


BUFFERS, SEMAPHORES = (tuple(d) for d in memory())


def per_device(queries, keys, values, output_gradient, file_starts, file_imports, header_lens):
    hbm = pl.BlockSpec(memory_space=pl.ANY)
    vmem = pl.BlockSpec(memory_space=pltpu.VMEM)
    buffers, semaphores = memory()
    dq, dk, dv = pl.pallas_call(
        fused_kernel,
        out_shape=(
            jax.ShapeDtypeStruct((BLK, GROUPS * HEADS * D), BF16),
            jax.ShapeDtypeStruct((BLK, GROUPS * D), F32),
            jax.ShapeDtypeStruct((BLK, GROUPS * D), F32),
        ),
        in_specs=[hbm] * 7,
        out_specs=(hbm, vmem, vmem),
        scratch_shapes=[*buffers.values(), *semaphores.values()],
        compiler_params=pltpu.CompilerParams(
            collective_id=0, has_side_effects=True, vmem_limit_bytes=VMEM_LIMIT
        ),
        name="attention_backward",
    )(
        file_starts, file_imports.T, header_lens, queries, keys, values, output_gradient
    )
    return dq.astype(F32), dk, dv


def solution(mesh):
    split = Mesh(mesh.devices.reshape(NX, NY, NZ, 2, 2), AXES)
    placed = P(AXES, None)
    return jax.shard_map(
        per_device,
        mesh=split,
        in_specs=(placed, placed, placed, placed, P(), P(), P()),
        out_specs=(placed, placed, placed),
        check_vma=False,
    )
```

```python
import math

import jax
import jax.numpy as jnp
from jax import lax
from jax.experimental import pallas as pl
from jax.experimental.pallas import tpu as pltpu
from jax.sharding import Mesh
from jax.sharding import PartitionSpec as P

WIN = 1024
HDR = 64
TOK = 256
BLK = 64
D = 128
HEADS = 12
GROUPS = 4
REACH = WIN // TOK
QB = TOK // BLK
IMPORTS = 4
FILES = 33
VMEM_LIMIT = 60 * 2**20
NX, NY, NZ = 2, 4, 8
NCTX = NX * NY * NZ
WROWS = WIN + BLK
HROWS = IMPORTS * HDR
ROWS = WROWS + HROWS
CHUNK_HEADS = 4
CHUNKS = HEADS // CHUNK_HEADS
CW = CHUNK_HEADS * BLK
COLS = HEADS * BLK
SCALE = 1.0 / math.sqrt(D)
LOG2E = 1.4426950408889634
HIDDEN = -1e30
MESH = pl.DeviceIdType.MESH
F32 = jnp.float32
BF16 = jnp.bfloat16
AXES = ("ctx_0", "ctx_1", "ctx_2", "head_0", "head_1")


def position():
    return tuple(lax.axis_index(a) for a in AXES)


def ctx_of(xh, y, z):
    return xh * (NY * NZ) + y * NZ + z


def ctx_shifted(xh, y, z, step):
    c = lax.rem(ctx_of(xh, y, z) + (NCTX + step), NCTX)
    return {
        "ctx_0": lax.div(c, NY * NZ),
        "ctx_1": lax.rem(lax.div(c, NZ), NY),
        "ctx_2": lax.rem(c, NZ),
    }


def head_peer(xl, co, d):
    pxl = 1 - xl if d & 2 else xl
    pco = 1 - co if d & 1 else co
    return {"head_0": pxl, "head_1": pco}, pxl * 2 + pco


def greet(peers):
    barrier = pltpu.get_barrier_semaphore()
    for peer in peers:
        pl.semaphore_signal(barrier, inc=1, device_id=peer, device_id_type=MESH)
    pl.semaphore_wait(barrier, len(peers))


def remote(src, dst, send, recv, peer):
    return pltpu.make_async_remote_copy(
        src_ref=src, dst_ref=dst, send_sem=send, recv_sem=recv, device_id=peer, device_id_type=MESH
    )


def all_peers(xh, y, z, xl, co):
    peers = [head_peer(xl, co, d)[0] for d in (1, 2, 3)]
    peers += [{"ctx_2": lax.rem(z + d, NZ)} for d in range(1, NZ)]
    peers += [{"ctx_1": n} for n in y_neighbours(y)]
    peers += [{"ctx_0": 1 - xh}]
    peers += [ctx_shifted(xh, y, z, 1), ctx_shifted(xh, y, z, -1)]
    return peers


def rows(start, size):
    return pl.ds(pl.multiple_of(start, size), size)


def y_neighbours(y):
    near = y + 1 - 2 * lax.rem(y, 2)
    return near, NY - 1 - y


def file_at(starts, place):
    count = jnp.int32(-1)
    for f in range(starts.shape[0]):
        count = count + jnp.where(starts[f] <= place, 1, 0)
    return count


def header_blocks(starts, imports, c):
    lower = file_at(starts, c * TOK)
    upper = file_at(starts, c * TOK + TOK - 1)
    blocks = []
    for file in (lower, upper):
        for m in range(IMPORTS):
            g = imports[m, file]
            blocks.append((g >= 0, lax.div(starts[jnp.maximum(g, 0)], TOK)))
    return lower, upper, blocks


def own_header_offset(starts, base):
    offset = jnp.int32(0)
    for f in range(starts.shape[0]):
        at = starts[f] - base
        offset = offset + jnp.where((at >= 0) & (at < TOK), at, 0)
    return offset


def fetch(pairs, sems):
    copies = [pltpu.make_async_copy(src, dst, sems.at[n]) for n, (src, dst) in enumerate(pairs)]
    for copy in copies:
        copy.start()
    return copies


def fold8(x, op):
    out = x[0:8]
    for r in range(8, x.shape[0], 8):
        out = op(out, x[r:r + 8])
    return out


def rows_at(start, size, multiple):
    return pl.ds(pl.multiple_of(start, multiple), size)


def receive_inputs(q, k, v, do, small, tables, b, sems):
    starts, imports = tables
    xh, y, z, xl, co = position()
    me = xl * 2 + co
    c = ctx_of(xh, y, z)
    width = HEADS * D
    own = REACH * TOK
    kvwin, slots = b["kvwin"], (b["slots_k"], b["slots_v"])
    here = fetch(
        (
            (k.at[:, rows(me * D, D)], kvwin.at[rows(own + me * BLK, BLK), pl.ds(0, D)]),
            (v.at[:, rows(me * D, D)], kvwin.at[rows(own + me * BLK, BLK), pl.ds(D, D)]),
            (q.at[:, rows(me * width, width)], b["q"].at[rows(me * BLK, BLK), :]),
            (do.at[:, rows(me * width, width)], b["do"].at[rows(me * BLK, BLK), :]),
        ),
        sems["here"],
    )
    greet(all_peers(xh, y, z, xl, co))
    kv_copies, q_copies = [], []
    for d in (2, 3, 1):
        peer, a = head_peer(xl, co, d)
        for n, src in enumerate((k, v)):
            kv_copies.append(remote(
                src.at[:, rows(a * D, D)],
                kvwin.at[rows(own + me * BLK, BLK), pl.ds(n * D, D)],
                sems["hsend"].at[d - 1, n], sems["hrecv"].at[d - 1, n], peer,
            ))
            kv_copies[-1].start()
    for d in (2, 3, 1):
        peer, a = head_peer(xl, co, d)
        for n, (src, dst) in enumerate(((q, b["q"]), (do, b["do"]))):
            q_copies.append(remote(
                src.at[:, rows(a * width, width)], dst.at[rows(me * BLK, BLK), :],
                sems["qsend"].at[d - 1, n], sems["qrecv"].at[d - 1, n], peer,
            ))
            q_copies[-1].start()
    for copy in small:
        copy.wait()
    offset = own_header_offset(starts, c * TOK)
    for copy in here[:2]:
        copy.wait()
    for copy in kv_copies:
        copy.wait_recv()

    forward = ctx_shifted(xh, y, z, 1)
    w_copies = [
        remote(
            kvwin.at[pl.ds((REACH - s) * TOK, TOK), :],
            kvwin.at[pl.ds((REACH - 1 - s) * TOK, TOK), :],
            sems["wsend"].at[s], sems["wrecv"].at[s], forward,
        )
        for s in range(REACH)
    ]
    w_copies[0].start()
    header = jnp.zeros((HDR, 2 * D), F32)
    for n in range(QB):
        keep = jnp.where(offset == n * BLK, 1.0, 0.0)
        header = header + kvwin[own + n * BLK:own + (n + 1) * BLK, :].astype(F32) * keep
    line = y * NZ + z
    for n in range(2):
        slots[n][line] = header[:, n * D:(n + 1) * D].astype(BF16)
    z_copies = ([], [])
    for n in range(2):
        for d in (1, 7, 2, 6, 3, 5, 4):
            part = slots[n].at[line]
            z_copies[n].append(remote(
                part, part, sems["zsend"].at[n, d - 1], sems["zrecv"].at[n, d - 1],
                {"ctx_2": lax.rem(z + d, NZ)},
            ))
            z_copies[n][-1].start()
    near, other = y_neighbours(y)
    near_copies, far_copies, x_copies = ([], []), ([], []), []

    def to_neighbours(n):
        for copy in z_copies[n]:
            copy.wait_recv()
        for d, to in enumerate((near, other)):
            part = slots[n].at[rows(y * NZ, NZ)]
            near_copies[n].append(remote(
                part, part, sems["ysend"].at[n, d], sems["yrecv"].at[n, d], {"ctx_1": to}
            ))
            near_copies[n][-1].start()

    def to_opposite(n):
        for d, (came, to) in enumerate(((near, other), (other, near))):
            near_copies[n][d].wait_recv()
            part = slots[n].at[rows(came * NZ + d * (NZ // 2), NZ // 2)]
            far_copies[n].append(remote(
                part, part, sems["ysend"].at[n, 2 + d], sems["yrecv"].at[n, 2 + d],
                {"ctx_1": to},
            ))
            far_copies[n][-1].start()

    def to_other_half(n):
        for copy in far_copies[n]:
            copy.wait_recv()
        for m, (_, shard) in enumerate(wanted):
            b["picked"][n, m] = slots[n][lax.rem(shard, NY * NZ)]
        x_copies.append(remote(
            b["picked"].at[n], b["far"].at[n], sems["xsend"].at[n], sems["xrecv"].at[n],
            {"ctx_0": 1 - xh},
        ))
        x_copies[-1].start()

    _, _, wanted = header_blocks(starts, imports, ctx_of(1 - xh, y, z))
    to_neighbours(0)
    w_copies[0].wait_recv()
    w_copies[1].start()
    to_neighbours(1)
    to_opposite(0)
    to_opposite(1)
    w_copies[1].wait_recv()
    w_copies[2].start()
    to_other_half(0)
    to_other_half(1)
    w_copies[2].wait_recv()
    w_copies[3].start()
    for copy in q_copies:
        copy.wait_recv()
    for copy in here[2:]:
        copy.wait()
    w_copies[3].wait_recv()
    for copy in x_copies:
        copy.wait_recv()
    y_copies = near_copies[0] + near_copies[1] + far_copies[0] + far_copies[1]
    return kv_copies + q_copies + z_copies[0] + z_copies[1] + w_copies + y_copies + x_copies


def attend_block(qb, starts, imports, lens, b):
    xh, y, z, _, _ = position()
    base = ctx_of(xh, y, z) * TOK
    place = base + qb * BLK
    lower = file_at(starts, base)
    file = file_at(starts, place)
    begin = starts[file]
    kc, vc, bias = b["kc"].at[qb], b["vc"], b["bias"]
    qs, dos = b["qs"].at[qb], b["dos"].at[qb]
    p_ref, ds_ref = b["hp"], b["hds"].at[qb]
    step = 64
    kc[0:WROWS, :] = b["kvwin"][rows_at(qb * BLK, WROWS, BLK), 0:D]
    vc[0:WROWS, :] = b["kvwin"][rows_at(qb * BLK, WROWS, BLK), D:2 * D]
    key_place = lax.broadcasted_iota(jnp.int32, (WROWS, D), 0) + (place - WIN)
    bias[0:WROWS, :] = jnp.where(key_place >= begin, 0.0, HIDDEN)
    offsets = lax.broadcasted_iota(jnp.int32, (HDR, D), 0)
    for m in range(IMPORTS):
        g = imports[m, file]
        known = jnp.maximum(g, 0)
        length = jnp.where(g >= 0, lens[known], 0)
        here = pl.ds(WROWS + m * HDR, HDR)
        shard = lax.div(starts[known], TOK)
        at = lax.rem(shard, NY * NZ)
        which = jnp.where(file == lower, 0, IMPORTS) + m
        same = jnp.full((HDR, D), lax.div(shard, NY * NZ)) == xh
        for n, (dst, slots) in enumerate(((kc, b["slots_k"]), (vc, b["slots_v"]))):
            near = slots[at].astype(F32)
            dst[here, :] = jnp.where(same, near, b["far"][n, which].astype(F32)).astype(BF16)
        bias[here, :] = jnp.where(offsets < length, 0.0, HIDDEN)
    for h in range(HEADS):
        qs[h * BLK:(h + 1) * BLK, :] = b["q"][rows(qb * BLK, BLK), h * D:(h + 1) * D]
        dos[h * BLK:(h + 1) * BLK, :] = b["do"][rows(qb * BLK, BLK), h * D:(h + 1) * D]

    t = lax.broadcasted_iota(jnp.int32, (BLK, CW), 0)
    p_at = lax.broadcasted_iota(jnp.int32, (BLK, CW), 1) % BLK
    nt = (((1,), (1,)), ((), ()))
    for chunk in range(CHUNKS):
        cols = slice(chunk * CW, (chunk + 1) * CW)
        s_ref, dp_ref = b["s"].at[qb, chunk], b["dp"].at[qb, chunk]
        s_ref[...] = lax.dot_general(kc[...], qs[cols, :], nt, preferred_element_type=F32)
        dp_ref[...] = lax.dot_general(vc[...], dos[cols, :], nt, preferred_element_type=F32)
        top = None
        for r in range(0, ROWS, step):
            s = s_ref[r:r + step, :] + jnp.concatenate([bias[r:r + step, :]] * (CW // D), axis=1)
            if r == 0:
                s = jnp.where(t > p_at, s, HIDDEN)
            if r == WIN:
                s = jnp.where(t <= p_at, s, HIDDEN)
            s_ref[r:r + step, :] = s
            part = fold8(s, jnp.maximum)
            top = part if top is None else jnp.maximum(top, part)
        top = jnp.max(top, axis=0, keepdims=True)
        total = jnp.zeros((8, CW), F32)
        centre = jnp.zeros((8, CW), F32)
        for r in range(0, ROWS, step):
            e = jnp.exp2((s_ref[r:r + step, :] - top) * (SCALE * LOG2E))
            s_ref[r:r + step, :] = e
            total = total + fold8(e, jnp.add)
            centre = centre + fold8(e * dp_ref[r:r + step, :], jnp.add)
        inverse = 1.0 / jnp.sum(total, axis=0, keepdims=True)
        centre = jnp.sum(centre, axis=0, keepdims=True) * inverse
        b["stat"][qb, chunk, 0:1, :] = inverse
        b["stat"][qb, chunk, 1:2, :] = centre
        for r in range(WROWS, ROWS, step):
            w = s_ref[r:r + step, :] * inverse
            here = slice(r - WROWS, r - WROWS + step)
            p_ref[here, cols] = w.astype(BF16)
            ds_ref[here, cols] = (w * (dp_ref[r:r + step, :] - centre)).astype(BF16)
    dv = jnp.dot(p_ref[...], dos[...], preferred_element_type=F32)
    dk = jnp.dot(ds_ref[...], qs[...], preferred_element_type=F32) * SCALE
    first = jnp.where(file == lower, 1.0, 0.0)
    for n, share in enumerate((first, 1.0 - first)):
        part = slice(n * HROWS, (n + 1) * HROWS)
        b["hacc"][part, 0:D] += dk * share
        b["hacc"][part, D:2 * D] += dv * share


def window_block(qb, b):
    kc, p_ref, ds_ref, hds = b["kc"].at[qb], b["p"], b["ds"], b["hds"].at[qb]
    step = 64
    for chunk in range(CHUNKS):
        cols = slice(chunk * CW, (chunk + 1) * CW)
        s_ref, dp_ref = b["s"].at[qb, chunk], b["dp"].at[qb, chunk]
        inverse = b["stat"][qb, chunk, 0:1, :]
        centre = b["stat"][qb, chunk, 1:2, :]
        for r in range(0, WROWS, step):
            w = s_ref[r:r + step, :] * inverse
            p_ref[r:r + step, cols] = w.astype(BF16)
            ds_ref[r:r + step, cols] = (w * (dp_ref[r:r + step, :] - centre)).astype(BF16)
    tn = (((0,), (0,)), ((), ()))
    dqt = lax.dot_general(kc[0:WROWS, :], ds_ref[...], tn, preferred_element_type=F32)
    dqt = dqt + lax.dot_general(kc[WROWS:, :], hds[...], tn, preferred_element_type=F32)
    dq = (dqt.T * SCALE).astype(BF16)
    for h in range(HEADS):
        b["dq"][qb, :, h * D:(h + 1) * D] = dq[h * BLK:(h + 1) * BLK]
    window = rows_at(qb * BLK, WROWS, BLK)
    dkv = b["dkv"]
    dkv[window, 0:D] += jnp.dot(ds_ref[...], b["qs"][qb], preferred_element_type=F32) * SCALE
    dkv[window, D:2 * D] += jnp.dot(p_ref[...], b["dos"][qb], preferred_element_type=F32)


def fused_kernel(starts_hbm, imports_hbm, lens_hbm, q, k, v, do, dq_out, dk_out, dv_out, *scratch):
    b = dict(zip(BUFFERS, scratch))
    sems = dict(zip(SEMAPHORES, scratch[len(BUFFERS):]))
    starts, imports, lens = b["starts"], b["imports"], b["lens"]
    xh, y, z, xl, co = position()
    me = xl * 2 + co
    c = ctx_of(xh, y, z)
    width = HEADS * D
    slots = 2 * IMPORTS
    dkv, tab, hacc = b["dkv"], b["tab"], b["hacc"]
    mine, theirs = b["mine"], (b["theirs_k"], b["theirs_v"])
    small = fetch(
        ((starts_hbm, starts), (imports_hbm, imports), (lens_hbm, lens)), sems["small"]
    )
    for n in range(2):
        mine[n, slots] = jnp.zeros((HDR, D), BF16)
        theirs[n][slots] = jnp.zeros((HDR, D), BF16)
    dkv[...] = jnp.zeros_like(dkv)
    hacc[...] = jnp.zeros_like(hacc)
    sent = receive_inputs(q, k, v, do, small, (starts, imports), b, sems)
    offset = own_header_offset(starts, c * TOK)

    def dq_copy(to):
        return remote(
            b["dq"].at[to], dq_out.at[:, rows(me * width, width)],
            sems["dsend"].at[to], sems["drecv"].at[me],
            {"head_0": lax.div(to, 2), "head_1": lax.rem(to, 2)},
        )

    own_dq = pltpu.make_async_copy(
        b["dq"].at[me], dq_out.at[:, rows(me * width, width)], sems["dlocal"]
    )

    def block_of(i):
        turn = jnp.where(i == 3, 0, jnp.where(i == 2, 1, i + 2))
        return lax.rem(me + turn, QB)

    def first_half(i, carry):
        attend_block(i, starts, imports, lens, b)
        return carry

    def second_half(i, carry):
        qb = block_of(i)
        window_block(qb, b)

        @pl.when(i < 3)
        def _():
            dq_copy(qb).start()

        return carry

    lax.fori_loop(0, QB, first_half, 0)
    halves = (slice(0, D), slice(D, 2 * D))
    x_copies = []
    for n, half in enumerate(halves):
        for m in range(slots):
            mine[n, m] = hacc[m * HDR:(m + 1) * HDR, half].astype(BF16)
        x_copies.append(remote(
            mine.at[n, pl.ds(0, slots)], theirs[n].at[pl.ds(0, slots)],
            sems["x2send"].at[n], sems["x2recv"].at[n], {"ctx_0": 1 - xh},
        ))
        x_copies[-1].start()

    back = ctx_shifted(xh, y, z, -1)
    wout, win = b["wout"], b["win"]
    w_copies = [
        remote(wout.at[s], win.at[s], sems["v2send"].at[s], sems["v2recv"].at[s], back)
        for s in range(REACH)
    ]

    def pass_on(s):
        w_copies[s - 1].wait_recv()
        wout[s] = (win[s - 1].astype(F32) + dkv[s * TOK:(s + 1) * TOK, :]).astype(BF16)
        w_copies[s].start()

    places = []
    for shard_at in (c, ctx_of(1 - xh, y, z)):
        _, _, blocks = header_blocks(starts, imports, shard_at)
        places += [blocks[0:IMPORTS], blocks[IMPORTS:]]

    def find(blocks, first, shard):
        at = jnp.int32(slots)
        for m, (used, block) in enumerate(blocks):
            at = jnp.where(used & (block == shard), first + m, at)
        return at

    near, other = y_neighbours(y)
    across = 2 * lax.rem(lax.div(y, 2) + 1, 2) + lax.rem(y, 2)
    y1out, y1in, y2out, y2in = b["y1out"], b["y1in"], b["y2out"], b["y2in"]
    acc, tz, rz, coll = b["acc"], b["tz"], b["rz"], b["coll"]
    near_copies, far_copies, z_copies = ([], []), ([], []), ([], [])
    middle = NZ // 2

    def to_opposite(n):
        x_copies[n].wait_recv()

        def one_slot(i, carry):
            shard = xh * (NY * NZ) + i
            total = None
            for buffer, lists in ((mine.at[n], places[0:2]), (theirs[n], places[2:4])):
                for side in range(2):
                    part = buffer[find(lists[side], side * IMPORTS, shard)].astype(F32)
                    total = part if total is None else total + part
            tab[n, i] = total
            return carry

        lax.fori_loop(0, NY * NZ, one_slot, 0)
        for d, to in enumerate((near, other)):
            y1out[n, d] = tab[n, rows(across * NZ + d * middle, middle)].astype(BF16)
            far_copies[n].append(remote(
                y1out.at[n, d], y1in.at[n, d],
                sems["y2send"].at[n, d], sems["y2recv"].at[n, d], {"ctx_1": to},
            ))
            far_copies[n][-1].start()

    def to_neighbours(n):
        for d, to in enumerate((other, near)):
            far_copies[n][d].wait_recv()
            add, rest = d * middle, (1 - d) * middle
            y2out[n, d, pl.ds(add, middle)] = (
                tab[n, rows(to * NZ + add, middle)] + y1in[n, d].astype(F32)
            ).astype(BF16)
            y2out[n, d, pl.ds(rest, middle)] = tab[n, rows(to * NZ + rest, middle)].astype(BF16)
            near_copies[n].append(remote(
                y2out.at[n, d], y2in.at[n, d],
                sems["y2send"].at[n, 2 + d], sems["y2recv"].at[n, 2 + d], {"ctx_1": to},
            ))
            near_copies[n][-1].start()

    def to_owners(n):
        for copy in near_copies[n]:
            copy.wait_recv()
        acc[n] = (
            tab[n, rows(y * NZ, NZ)] + y2in[n, 0].astype(F32) + y2in[n, 1].astype(F32)
        )
        tz[n] = acc[n].astype(BF16)
        for d in (4, 3, 5, 2, 6, 1, 7):
            to = lax.rem(z + d, NZ)
            z_copies[n].append(remote(
                tz.at[n, to], rz.at[n, d - 1],
                sems["z2send"].at[n, d - 1], sems["z2recv"].at[n, d - 1], {"ctx_2": to},
            ))
            z_copies[n][-1].start()

    lax.fori_loop(0, QB, second_half, 0)
    own_dq.start()
    wout[0] = dkv[0:TOK, :].astype(BF16)
    w_copies[0].start()
    to_opposite(0)
    to_opposite(1)
    to_neighbours(0)
    pass_on(1)
    to_neighbours(1)
    to_owners(0)
    pass_on(2)
    to_owners(1)
    pass_on(3)
    headers = []
    for n in range(2):
        header = acc[n, z]
        for copy in z_copies[n]:
            copy.wait_recv()
        for d in range(NZ - 1):
            header = header + rz[n, d].astype(F32)
        headers.append(header)
    w_copies[3].wait_recv()
    for n in range(QB):
        part = slice(n * BLK, (n + 1) * BLK)
        keep = jnp.where(offset == n * BLK, 1.0, 0.0)
        for half, header in zip(halves, headers):
            coll[part, half] = (
                dkv[REACH * TOK + n * BLK:REACH * TOK + (n + 1) * BLK, half]
                + win[REACH - 1, part, half].astype(F32)
                + header * keep
            )
    h_copies = []
    for d in (2, 3, 1):
        peer, a = head_peer(xl, co, d)
        for n, dst in enumerate((dk_out, dv_out)):
            h_copies.append(remote(
                coll.at[rows(a * BLK, BLK), pl.ds(n * D, D)], dst.at[:, rows(me * D, D)],
                sems["h2send"].at[d - 1, n], sems["h2recv"].at[d - 1, n], peer,
            ))
            h_copies[-1].start()
    for n, dst in enumerate((dk_out, dv_out)):
        dst[:, rows(me * D, D)] = coll[rows(me * BLK, BLK), n * D:(n + 1) * D]
    own_dq.wait()
    for d in (1, 2, 3):
        _, a = head_peer(xl, co, d)
        remote(
            b["dq"].at[a], dq_out.at[:, rows(a * width, width)],
            sems["dsend"].at[a], sems["drecv"].at[a],
            {"head_0": lax.div(a, 2), "head_1": lax.rem(a, 2)},
        ).wait()
    for copy in h_copies:
        copy.wait_recv()
    for pair in (near_copies, far_copies, z_copies):
        sent = sent + pair[0] + pair[1]
    for copy in sent + w_copies + x_copies + h_copies:
        copy.wait_send()


def memory():
    vmem, smem = pltpu.VMEM, pltpu.SMEM
    dma = pltpu.SemaphoreType.DMA
    half = (HDR, D)
    buffers = dict(
        starts=smem((FILES,), jnp.int32), imports=smem((IMPORTS, FILES), jnp.int32),
        lens=smem((FILES,), jnp.int32),
        q=vmem((TOK, HEADS * D), BF16), do=vmem((TOK, HEADS * D), BF16),
        kvwin=vmem(((REACH + 1) * TOK, 2 * D), BF16),
        slots_k=vmem((NY * NZ, *half), BF16), slots_v=vmem((NY * NZ, *half), BF16),
        picked=vmem((2, 2 * IMPORTS, HDR, D), BF16), far=vmem((2, 2 * IMPORTS, HDR, D), BF16),
        kc=vmem((QB, ROWS, D), BF16), vc=vmem((ROWS, D), BF16), bias=vmem((ROWS, D), F32),
        qs=vmem((QB, COLS, D), BF16), dos=vmem((QB, COLS, D), BF16),
        s=vmem((QB, CHUNKS, ROWS, CW), F32), dp=vmem((QB, CHUNKS, ROWS, CW), F32),
        stat=vmem((QB, CHUNKS, 8, CW), F32),
        p=vmem((WROWS, COLS), BF16), ds=vmem((WROWS, COLS), BF16),
        hp=vmem((HROWS, COLS), BF16), hds=vmem((QB, HROWS, COLS), BF16),
        hacc=vmem((2 * HROWS, 2 * D), F32),
        dq=vmem((QB, BLK, HEADS * D), BF16),
        dkv=vmem(((REACH + 1) * TOK, 2 * D), F32),
        mine=vmem((2, 2 * IMPORTS + 1, *half), BF16),
        theirs_k=vmem((2 * IMPORTS + 1, *half), BF16),
        theirs_v=vmem((2 * IMPORTS + 1, *half), BF16),
        tab=vmem((2, NY * NZ, *half), F32),
        y1out=vmem((2, 2, NZ // 2, *half), BF16), y1in=vmem((2, 2, NZ // 2, *half), BF16),
        y2out=vmem((2, 2, NZ, *half), BF16), y2in=vmem((2, 2, NZ, *half), BF16),
        acc=vmem((2, NZ, *half), F32), tz=vmem((2, NZ, *half), BF16),
        rz=vmem((2, NZ - 1, *half), BF16),
        wout=vmem((REACH, TOK, 2 * D), BF16), win=vmem((REACH, TOK, 2 * D), BF16),
        coll=vmem((TOK, 2 * D), F32),
    )
    four, window, line, pairs = dma((4,)), dma((REACH,)), dma((2, NZ - 1)), dma((3, 2))
    two, steps = dma((2,)), dma((2, 4))
    semaphores = dict(
        small=dma((3,)), here=four, hsend=pairs, hrecv=pairs, qsend=pairs, qrecv=pairs,
        wsend=window, wrecv=window, zsend=line, zrecv=line, xsend=two, xrecv=two,
        ysend=steps, yrecv=steps, dsend=four, drecv=four, dlocal=dma,
        v2send=window, v2recv=window, z2send=line, z2recv=line, x2send=two, x2recv=two,
        y2send=steps, y2recv=steps, h2send=pairs, h2recv=pairs,
    )
    return buffers, semaphores


BUFFERS, SEMAPHORES = (tuple(d) for d in memory())


def per_device(queries, keys, values, output_gradient, file_starts, file_imports, header_lens):
    hbm = pl.BlockSpec(memory_space=pl.ANY)
    vmem = pl.BlockSpec(memory_space=pltpu.VMEM)
    buffers, semaphores = memory()
    dq, dk, dv = pl.pallas_call(
        fused_kernel,
        out_shape=(
            jax.ShapeDtypeStruct((BLK, GROUPS * HEADS * D), BF16),
            jax.ShapeDtypeStruct((BLK, GROUPS * D), F32),
            jax.ShapeDtypeStruct((BLK, GROUPS * D), F32),
        ),
        in_specs=[hbm] * 7,
        out_specs=(hbm, vmem, vmem),
        scratch_shapes=[*buffers.values(), *semaphores.values()],
        compiler_params=pltpu.CompilerParams(
            collective_id=0, has_side_effects=True, vmem_limit_bytes=VMEM_LIMIT
        ),
        name="attention_backward",
    )(
        file_starts, file_imports.T, header_lens, queries, keys, values, output_gradient
    )
    return dq.astype(F32), dk, dv


def solution(mesh):
    split = Mesh(mesh.devices.reshape(NX, NY, NZ, 2, 2), AXES)
    placed = P(AXES, None)
    return jax.shard_map(
        per_device,
        mesh=split,
        in_specs=(placed, placed, placed, placed, P(), P(), P()),
        out_specs=(placed, placed, placed),
        check_vma=False,
    )
```

```python
import math

import jax
import jax.numpy as jnp
from jax import lax
from jax.experimental import pallas as pl
from jax.experimental.pallas import tpu as pltpu
from jax.sharding import Mesh
from jax.sharding import PartitionSpec as P

WIN = 1024
HDR = 64
TOK = 256
BLK = 64
D = 128
HEADS = 12
GROUPS = 4
REACH = WIN // TOK
QB = TOK // BLK
IMPORTS = 4
FILES = 33
VMEM_LIMIT = 60 * 2**20
NX, NY, NZ = 2, 4, 8
NCTX = NX * NY * NZ
WROWS = WIN + BLK
HROWS = IMPORTS * HDR
ROWS = WROWS + HROWS
CHUNK_HEADS = 4
CHUNKS = HEADS // CHUNK_HEADS
CW = CHUNK_HEADS * BLK
COLS = HEADS * BLK
SCALE = 1.0 / math.sqrt(D)
LOG2E = 1.4426950408889634
HIDDEN = -1e30
MESH = pl.DeviceIdType.MESH
F32 = jnp.float32
BF16 = jnp.bfloat16
AXES = ("ctx_0", "ctx_1", "ctx_2", "head_0", "head_1")


def position():
    return tuple(lax.axis_index(a) for a in AXES)


def ctx_of(xh, y, z):
    return xh * (NY * NZ) + y * NZ + z


def ctx_shifted(xh, y, z, step):
    c = lax.rem(ctx_of(xh, y, z) + (NCTX + step), NCTX)
    return {
        "ctx_0": lax.div(c, NY * NZ),
        "ctx_1": lax.rem(lax.div(c, NZ), NY),
        "ctx_2": lax.rem(c, NZ),
    }


def head_peer(xl, co, d):
    pxl = 1 - xl if d & 2 else xl
    pco = 1 - co if d & 1 else co
    return {"head_0": pxl, "head_1": pco}, pxl * 2 + pco


def greet(peers):
    barrier = pltpu.get_barrier_semaphore()
    for peer in peers:
        pl.semaphore_signal(barrier, inc=1, device_id=peer, device_id_type=MESH)
    pl.semaphore_wait(barrier, len(peers))


def remote(src, dst, send, recv, peer):
    return pltpu.make_async_remote_copy(
        src_ref=src, dst_ref=dst, send_sem=send, recv_sem=recv, device_id=peer, device_id_type=MESH
    )


def all_peers(xh, y, z, xl, co):
    peers = [head_peer(xl, co, d)[0] for d in (1, 2, 3)]
    peers += [{"ctx_2": lax.rem(z + d, NZ)} for d in range(1, NZ)]
    peers += [{"ctx_1": n} for n in y_neighbours(y)]
    peers += [{"ctx_0": 1 - xh}]
    peers += [ctx_shifted(xh, y, z, 1), ctx_shifted(xh, y, z, -1)]
    return peers


def rows(start, size):
    return pl.ds(pl.multiple_of(start, size), size)


def y_neighbours(y):
    near = y + 1 - 2 * lax.rem(y, 2)
    return near, NY - 1 - y


def file_at(starts, place):
    count = jnp.int32(-1)
    for f in range(starts.shape[0]):
        count = count + jnp.where(starts[f] <= place, 1, 0)
    return count


def header_blocks(starts, imports, c):
    lower = file_at(starts, c * TOK)
    upper = file_at(starts, c * TOK + TOK - 1)
    blocks = []
    for file in (lower, upper):
        for m in range(IMPORTS):
            g = imports[m, file]
            blocks.append((g >= 0, lax.div(starts[jnp.maximum(g, 0)], TOK)))
    return lower, upper, blocks


def own_header_offset(starts, base):
    offset = jnp.int32(0)
    for f in range(starts.shape[0]):
        at = starts[f] - base
        offset = offset + jnp.where((at >= 0) & (at < TOK), at, 0)
    return offset


def fetch(pairs, sems):
    copies = [pltpu.make_async_copy(src, dst, sems.at[n]) for n, (src, dst) in enumerate(pairs)]
    for copy in copies:
        copy.start()
    return copies


def fold8(x, op):
    out = x[0:8]
    for r in range(8, x.shape[0], 8):
        out = op(out, x[r:r + 8])
    return out


def rows_at(start, size, multiple):
    return pl.ds(pl.multiple_of(start, multiple), size)


def receive_inputs(q, k, v, do, small, tables, b, sems):
    starts, imports = tables
    xh, y, z, xl, co = position()
    me = xl * 2 + co
    c = ctx_of(xh, y, z)
    width = HEADS * D
    own = REACH * TOK
    kvwin, slots = b["kvwin"], (b["slots_k"], b["slots_v"])
    here = fetch(
        (
            (k.at[:, rows(me * D, D)], kvwin.at[rows(own + me * BLK, BLK), pl.ds(0, D)]),
            (v.at[:, rows(me * D, D)], kvwin.at[rows(own + me * BLK, BLK), pl.ds(D, D)]),
            (q.at[:, rows(me * width, width)], b["q"].at[rows(me * BLK, BLK), :]),
            (do.at[:, rows(me * width, width)], b["do"].at[rows(me * BLK, BLK), :]),
        ),
        sems["here"],
    )
    greet(all_peers(xh, y, z, xl, co))
    kv_copies, q_copies = [], []
    for d in (2, 3, 1):
        peer, a = head_peer(xl, co, d)
        for n, src in enumerate((k, v)):
            kv_copies.append(remote(
                src.at[:, rows(a * D, D)],
                kvwin.at[rows(own + me * BLK, BLK), pl.ds(n * D, D)],
                sems["hsend"].at[d - 1, n], sems["hrecv"].at[d - 1, n], peer,
            ))
            kv_copies[-1].start()
    for d in (2, 3, 1):
        peer, a = head_peer(xl, co, d)
        for n, (src, dst) in enumerate(((q, b["q"]), (do, b["do"]))):
            q_copies.append(remote(
                src.at[:, rows(a * width, width)], dst.at[rows(me * BLK, BLK), :],
                sems["qsend"].at[d - 1, n], sems["qrecv"].at[d - 1, n], peer,
            ))
            q_copies[-1].start()
    for copy in small:
        copy.wait()
    offset = own_header_offset(starts, c * TOK)
    for copy in here[:2]:
        copy.wait()
    for copy in kv_copies:
        copy.wait_recv()

    forward = ctx_shifted(xh, y, z, 1)
    w_copies = [
        remote(
            kvwin.at[pl.ds((REACH - s) * TOK, TOK), :],
            kvwin.at[pl.ds((REACH - 1 - s) * TOK, TOK), :],
            sems["wsend"].at[s], sems["wrecv"].at[s], forward,
        )
        for s in range(REACH)
    ]
    w_copies[0].start()
    header = jnp.zeros((HDR, 2 * D), F32)
    for n in range(QB):
        keep = jnp.where(offset == n * BLK, 1.0, 0.0)
        header = header + kvwin[own + n * BLK:own + (n + 1) * BLK, :].astype(F32) * keep
    line = y * NZ + z
    for n in range(2):
        slots[n][line] = header[:, n * D:(n + 1) * D].astype(BF16)
    z_copies = ([], [])
    for n in range(2):
        for d in (1, 7, 2, 6, 3, 5, 4):
            part = slots[n].at[line]
            z_copies[n].append(remote(
                part, part, sems["zsend"].at[n, d - 1], sems["zrecv"].at[n, d - 1],
                {"ctx_2": lax.rem(z + d, NZ)},
            ))
            z_copies[n][-1].start()
    near, other = y_neighbours(y)
    near_copies, far_copies, x_copies = ([], []), ([], []), []

    def to_neighbours(n):
        for copy in z_copies[n]:
            copy.wait_recv()
        for d, to in enumerate((near, other)):
            part = slots[n].at[rows(y * NZ, NZ)]
            near_copies[n].append(remote(
                part, part, sems["ysend"].at[n, d], sems["yrecv"].at[n, d], {"ctx_1": to}
            ))
            near_copies[n][-1].start()

    def to_opposite(n):
        for d, (came, to) in enumerate(((near, other), (other, near))):
            near_copies[n][d].wait_recv()
            part = slots[n].at[rows(came * NZ + d * (NZ // 2), NZ // 2)]
            far_copies[n].append(remote(
                part, part, sems["ysend"].at[n, 2 + d], sems["yrecv"].at[n, 2 + d],
                {"ctx_1": to},
            ))
            far_copies[n][-1].start()

    def to_other_half(n):
        for copy in far_copies[n]:
            copy.wait_recv()
        for m, (_, shard) in enumerate(wanted):
            b["picked"][n, m] = slots[n][lax.rem(shard, NY * NZ)]
        x_copies.append(remote(
            b["picked"].at[n], b["far"].at[n], sems["xsend"].at[n], sems["xrecv"].at[n],
            {"ctx_0": 1 - xh},
        ))
        x_copies[-1].start()

    _, _, wanted = header_blocks(starts, imports, ctx_of(1 - xh, y, z))
    to_neighbours(0)
    w_copies[0].wait_recv()
    w_copies[1].start()
    to_neighbours(1)
    to_opposite(0)
    to_opposite(1)
    w_copies[1].wait_recv()
    w_copies[2].start()
    to_other_half(0)
    to_other_half(1)
    w_copies[2].wait_recv()
    w_copies[3].start()
    for copy in q_copies:
        copy.wait_recv()
    for copy in here[2:]:
        copy.wait()
    w_copies[3].wait_recv()
    for copy in x_copies:
        copy.wait_recv()
    y_copies = near_copies[0] + near_copies[1] + far_copies[0] + far_copies[1]
    return kv_copies + q_copies + z_copies[0] + z_copies[1] + w_copies + y_copies + x_copies


def attend_block(qb, starts, imports, lens, b):
    xh, y, z, _, _ = position()
    base = ctx_of(xh, y, z) * TOK
    place = base + qb * BLK
    lower = file_at(starts, base)
    file = file_at(starts, place)
    begin = starts[file]
    kc, vc, bias = b["kc"].at[qb], b["vc"], b["bias"]
    qs, dos = b["qs"].at[qb], b["dos"].at[qb]
    p_ref, ds_ref = b["hp"], b["hds"].at[qb]
    step = 64
    kc[0:WROWS, :] = b["kvwin"][rows_at(qb * BLK, WROWS, BLK), 0:D]
    vc[0:WROWS, :] = b["kvwin"][rows_at(qb * BLK, WROWS, BLK), D:2 * D]
    key_place = lax.broadcasted_iota(jnp.int32, (WROWS, D), 0) + (place - WIN)
    bias[0:WROWS, :] = jnp.where(key_place >= begin, 0.0, HIDDEN)
    offsets = lax.broadcasted_iota(jnp.int32, (HDR, D), 0)
    for m in range(IMPORTS):
        g = imports[m, file]
        known = jnp.maximum(g, 0)
        length = jnp.where(g >= 0, lens[known], 0)
        here = pl.ds(WROWS + m * HDR, HDR)
        shard = lax.div(starts[known], TOK)
        at = lax.rem(shard, NY * NZ)
        which = jnp.where(file == lower, 0, IMPORTS) + m
        same = jnp.full((HDR, D), lax.div(shard, NY * NZ)) == xh
        for n, (dst, slots) in enumerate(((kc, b["slots_k"]), (vc, b["slots_v"]))):
            near = slots[at].astype(F32)
            dst[here, :] = jnp.where(same, near, b["far"][n, which].astype(F32)).astype(BF16)
        bias[here, :] = jnp.where(offsets < length, 0.0, HIDDEN)
    for h in range(HEADS):
        qs[h * BLK:(h + 1) * BLK, :] = b["q"][rows(qb * BLK, BLK), h * D:(h + 1) * D]
        dos[h * BLK:(h + 1) * BLK, :] = b["do"][rows(qb * BLK, BLK), h * D:(h + 1) * D]

    t = lax.broadcasted_iota(jnp.int32, (BLK, CW), 0)
    p_at = lax.broadcasted_iota(jnp.int32, (BLK, CW), 1) % BLK
    nt = (((1,), (1,)), ((), ()))
    for chunk in range(CHUNKS):
        cols = slice(chunk * CW, (chunk + 1) * CW)
        s_ref, dp_ref = b["s"].at[qb, chunk], b["dp"].at[qb, chunk]
        s_ref[...] = lax.dot_general(kc[...], qs[cols, :], nt, preferred_element_type=F32)
        dp_ref[...] = lax.dot_general(vc[...], dos[cols, :], nt, preferred_element_type=F32)
        top = None
        for r in range(0, ROWS, step):
            s = s_ref[r:r + step, :] + jnp.concatenate([bias[r:r + step, :]] * (CW // D), axis=1)
            if r == 0:
                s = jnp.where(t > p_at, s, HIDDEN)
            if r == WIN:
                s = jnp.where(t <= p_at, s, HIDDEN)
            s_ref[r:r + step, :] = s
            part = fold8(s, jnp.maximum)
            top = part if top is None else jnp.maximum(top, part)
        top = jnp.max(top, axis=0, keepdims=True)
        total = jnp.zeros((8, CW), F32)
        centre = jnp.zeros((8, CW), F32)
        for r in range(0, ROWS, step):
            e = jnp.exp2((s_ref[r:r + step, :] - top) * (SCALE * LOG2E))
            s_ref[r:r + step, :] = e
            total = total + fold8(e, jnp.add)
            centre = centre + fold8(e * dp_ref[r:r + step, :], jnp.add)
        inverse = 1.0 / jnp.sum(total, axis=0, keepdims=True)
        centre = jnp.sum(centre, axis=0, keepdims=True) * inverse
        b["stat"][qb, chunk, 0:1, :] = inverse
        b["stat"][qb, chunk, 1:2, :] = centre
        for r in range(WROWS, ROWS, step):
            w = s_ref[r:r + step, :] * inverse
            here = slice(r - WROWS, r - WROWS + step)
            p_ref[here, cols] = w.astype(BF16)
            ds_ref[here, cols] = (w * (dp_ref[r:r + step, :] - centre)).astype(BF16)
    dv = jnp.dot(p_ref[...], dos[...], preferred_element_type=F32)
    dk = jnp.dot(ds_ref[...], qs[...], preferred_element_type=F32) * SCALE
    first = jnp.where(file == lower, 1.0, 0.0)
    for n, share in enumerate((first, 1.0 - first)):
        part = slice(n * HROWS, (n + 1) * HROWS)
        b["hacc"][part, 0:D] += dk * share
        b["hacc"][part, D:2 * D] += dv * share


def window_block(qb, b):
    p_ref, ds_ref = b["p"], b["ds"].at[qb]
    step = 64
    for chunk in range(CHUNKS):
        cols = slice(chunk * CW, (chunk + 1) * CW)
        s_ref, dp_ref = b["s"].at[qb, chunk], b["dp"].at[qb, chunk]
        inverse = b["stat"][qb, chunk, 0:1, :]
        centre = b["stat"][qb, chunk, 1:2, :]
        for r in range(0, WROWS, step):
            w = s_ref[r:r + step, :] * inverse
            p_ref[r:r + step, cols] = w.astype(BF16)
            ds_ref[r:r + step, cols] = (w * (dp_ref[r:r + step, :] - centre)).astype(BF16)
    window = rows_at(qb * BLK, WROWS, BLK)
    dkv = b["dkv"]
    dkv[window, 0:D] += jnp.dot(ds_ref[...], b["qs"][qb], preferred_element_type=F32) * SCALE
    dkv[window, D:2 * D] += jnp.dot(p_ref[...], b["dos"][qb], preferred_element_type=F32)


def query_block(qb, b):
    kc, ds_ref, hds = b["kc"].at[qb], b["ds"].at[qb], b["hds"].at[qb]
    tn = (((0,), (0,)), ((), ()))
    dqt = lax.dot_general(kc[0:WROWS, :], ds_ref[...], tn, preferred_element_type=F32)
    dqt = dqt + lax.dot_general(kc[WROWS:, :], hds[...], tn, preferred_element_type=F32)
    dq = (dqt.T * SCALE).astype(BF16)
    for h in range(HEADS):
        b["dq"][qb, :, h * D:(h + 1) * D] = dq[h * BLK:(h + 1) * BLK]


def fused_kernel(starts_hbm, imports_hbm, lens_hbm, q, k, v, do, dq_out, dk_out, dv_out, *scratch):
    b = dict(zip(BUFFERS, scratch))
    sems = dict(zip(SEMAPHORES, scratch[len(BUFFERS):]))
    starts, imports, lens = b["starts"], b["imports"], b["lens"]
    xh, y, z, xl, co = position()
    me = xl * 2 + co
    c = ctx_of(xh, y, z)
    width = HEADS * D
    slots = 2 * IMPORTS
    dkv, tab, hacc = b["dkv"], b["tab"], b["hacc"]
    mine, theirs = b["mine"], (b["theirs_k"], b["theirs_v"])
    small = fetch(
        ((starts_hbm, starts), (imports_hbm, imports), (lens_hbm, lens)), sems["small"]
    )
    for n in range(2):
        mine[n, slots] = jnp.zeros((HDR, D), BF16)
        theirs[n][slots] = jnp.zeros((HDR, D), BF16)
    dkv[...] = jnp.zeros_like(dkv)
    hacc[...] = jnp.zeros_like(hacc)
    sent = receive_inputs(q, k, v, do, small, (starts, imports), b, sems)
    offset = own_header_offset(starts, c * TOK)

    def dq_copy(to):
        return remote(
            b["dq"].at[to], dq_out.at[:, rows(me * width, width)],
            sems["dsend"].at[to], sems["drecv"].at[me],
            {"head_0": lax.div(to, 2), "head_1": lax.rem(to, 2)},
        )

    own_dq = pltpu.make_async_copy(
        b["dq"].at[me], dq_out.at[:, rows(me * width, width)], sems["dlocal"]
    )

    def block_of(i):
        turn = jnp.where(i == 3, 0, jnp.where(i == 2, 1, i + 2))
        return lax.rem(me + turn, QB)

    def first_half(i, carry):
        attend_block(i, starts, imports, lens, b)
        return carry

    def second_half(i, carry):
        window_block(i, b)
        return carry

    def third_part(i, carry):
        qb = block_of(i)
        query_block(qb, b)

        @pl.when(i < 3)
        def _():
            dq_copy(qb).start()

        return carry

    lax.fori_loop(0, QB, first_half, 0)
    halves = (slice(0, D), slice(D, 2 * D))
    x_copies = []
    for n, half in enumerate(halves):
        for m in range(slots):
            mine[n, m] = hacc[m * HDR:(m + 1) * HDR, half].astype(BF16)
        x_copies.append(remote(
            mine.at[n, pl.ds(0, slots)], theirs[n].at[pl.ds(0, slots)],
            sems["x2send"].at[n], sems["x2recv"].at[n], {"ctx_0": 1 - xh},
        ))
        x_copies[-1].start()

    back = ctx_shifted(xh, y, z, -1)
    wout, win = b["wout"], b["win"]
    w_copies = [
        remote(wout.at[s], win.at[s], sems["v2send"].at[s], sems["v2recv"].at[s], back)
        for s in range(REACH)
    ]

    def pass_on(s):
        w_copies[s - 1].wait_recv()
        wout[s] = (win[s - 1].astype(F32) + dkv[s * TOK:(s + 1) * TOK, :]).astype(BF16)
        w_copies[s].start()

    places = []
    for shard_at in (c, ctx_of(1 - xh, y, z)):
        _, _, blocks = header_blocks(starts, imports, shard_at)
        places += [blocks[0:IMPORTS], blocks[IMPORTS:]]

    def find(blocks, first, shard):
        at = jnp.int32(slots)
        for m, (used, block) in enumerate(blocks):
            at = jnp.where(used & (block == shard), first + m, at)
        return at

    near, other = y_neighbours(y)
    across = 2 * lax.rem(lax.div(y, 2) + 1, 2) + lax.rem(y, 2)
    y1out, y1in, y2out, y2in = b["y1out"], b["y1in"], b["y2out"], b["y2in"]
    acc, tz, rz, coll = b["acc"], b["tz"], b["rz"], b["coll"]
    near_copies, far_copies, z_copies = ([], []), ([], []), ([], [])
    middle = NZ // 2

    def to_opposite(n):
        x_copies[n].wait_recv()

        def one_slot(i, carry):
            shard = xh * (NY * NZ) + i
            total = None
            for buffer, lists in ((mine.at[n], places[0:2]), (theirs[n], places[2:4])):
                for side in range(2):
                    part = buffer[find(lists[side], side * IMPORTS, shard)].astype(F32)
                    total = part if total is None else total + part
            tab[n, i] = total
            return carry

        lax.fori_loop(0, NY * NZ, one_slot, 0)
        for d, to in enumerate((near, other)):
            y1out[n, d] = tab[n, rows(across * NZ + d * middle, middle)].astype(BF16)
            far_copies[n].append(remote(
                y1out.at[n, d], y1in.at[n, d],
                sems["y2send"].at[n, d], sems["y2recv"].at[n, d], {"ctx_1": to},
            ))
            far_copies[n][-1].start()

    def to_neighbours(n):
        for d, to in enumerate((other, near)):
            far_copies[n][d].wait_recv()
            add, rest = d * middle, (1 - d) * middle
            y2out[n, d, pl.ds(add, middle)] = (
                tab[n, rows(to * NZ + add, middle)] + y1in[n, d].astype(F32)
            ).astype(BF16)
            y2out[n, d, pl.ds(rest, middle)] = tab[n, rows(to * NZ + rest, middle)].astype(BF16)
            near_copies[n].append(remote(
                y2out.at[n, d], y2in.at[n, d],
                sems["y2send"].at[n, 2 + d], sems["y2recv"].at[n, 2 + d], {"ctx_1": to},
            ))
            near_copies[n][-1].start()

    def to_owners(n):
        for copy in near_copies[n]:
            copy.wait_recv()
        acc[n] = (
            tab[n, rows(y * NZ, NZ)] + y2in[n, 0].astype(F32) + y2in[n, 1].astype(F32)
        )
        tz[n] = acc[n].astype(BF16)
        for d in (4, 3, 5, 2, 6, 1, 7):
            to = lax.rem(z + d, NZ)
            z_copies[n].append(remote(
                tz.at[n, to], rz.at[n, d - 1],
                sems["z2send"].at[n, d - 1], sems["z2recv"].at[n, d - 1], {"ctx_2": to},
            ))
            z_copies[n][-1].start()

    lax.fori_loop(0, QB, second_half, 0)
    wout[0] = dkv[0:TOK, :].astype(BF16)
    w_copies[0].start()
    to_opposite(0)
    to_opposite(1)
    lax.fori_loop(0, QB // 2, third_part, 0)
    to_neighbours(0)
    pass_on(1)
    to_neighbours(1)
    lax.fori_loop(QB // 2, QB, third_part, 0)
    own_dq.start()
    to_owners(0)
    pass_on(2)
    to_owners(1)
    pass_on(3)
    headers = []
    for n in range(2):
        header = acc[n, z]
        for copy in z_copies[n]:
            copy.wait_recv()
        for d in range(NZ - 1):
            header = header + rz[n, d].astype(F32)
        headers.append(header)
    w_copies[3].wait_recv()
    for n in range(QB):
        part = slice(n * BLK, (n + 1) * BLK)
        keep = jnp.where(offset == n * BLK, 1.0, 0.0)
        for half, header in zip(halves, headers):
            coll[part, half] = (
                dkv[REACH * TOK + n * BLK:REACH * TOK + (n + 1) * BLK, half]
                + win[REACH - 1, part, half].astype(F32)
                + header * keep
            )
    h_copies = []
    for d in (2, 3, 1):
        peer, a = head_peer(xl, co, d)
        for n, dst in enumerate((dk_out, dv_out)):
            h_copies.append(remote(
                coll.at[rows(a * BLK, BLK), pl.ds(n * D, D)], dst.at[:, rows(me * D, D)],
                sems["h2send"].at[d - 1, n], sems["h2recv"].at[d - 1, n], peer,
            ))
            h_copies[-1].start()
    for n, dst in enumerate((dk_out, dv_out)):
        dst[:, rows(me * D, D)] = coll[rows(me * BLK, BLK), n * D:(n + 1) * D]
    own_dq.wait()
    for d in (1, 2, 3):
        _, a = head_peer(xl, co, d)
        remote(
            b["dq"].at[a], dq_out.at[:, rows(a * width, width)],
            sems["dsend"].at[a], sems["drecv"].at[a],
            {"head_0": lax.div(a, 2), "head_1": lax.rem(a, 2)},
        ).wait()
    for copy in h_copies:
        copy.wait_recv()
    for pair in (near_copies, far_copies, z_copies):
        sent = sent + pair[0] + pair[1]
    for copy in sent + w_copies + x_copies + h_copies:
        copy.wait_send()


def memory():
    vmem, smem = pltpu.VMEM, pltpu.SMEM
    dma = pltpu.SemaphoreType.DMA
    half = (HDR, D)
    buffers = dict(
        starts=smem((FILES,), jnp.int32), imports=smem((IMPORTS, FILES), jnp.int32),
        lens=smem((FILES,), jnp.int32),
        q=vmem((TOK, HEADS * D), BF16), do=vmem((TOK, HEADS * D), BF16),
        kvwin=vmem(((REACH + 1) * TOK, 2 * D), BF16),
        slots_k=vmem((NY * NZ, *half), BF16), slots_v=vmem((NY * NZ, *half), BF16),
        picked=vmem((2, 2 * IMPORTS, HDR, D), BF16), far=vmem((2, 2 * IMPORTS, HDR, D), BF16),
        kc=vmem((QB, ROWS, D), BF16), vc=vmem((ROWS, D), BF16), bias=vmem((ROWS, D), F32),
        qs=vmem((QB, COLS, D), BF16), dos=vmem((QB, COLS, D), BF16),
        s=vmem((QB, CHUNKS, ROWS, CW), F32), dp=vmem((QB, CHUNKS, ROWS, CW), F32),
        stat=vmem((QB, CHUNKS, 8, CW), F32),
        p=vmem((WROWS, COLS), BF16), ds=vmem((QB, WROWS, COLS), BF16),
        hp=vmem((HROWS, COLS), BF16), hds=vmem((QB, HROWS, COLS), BF16),
        hacc=vmem((2 * HROWS, 2 * D), F32),
        dq=vmem((QB, BLK, HEADS * D), BF16),
        dkv=vmem(((REACH + 1) * TOK, 2 * D), F32),
        mine=vmem((2, 2 * IMPORTS + 1, *half), BF16),
        theirs_k=vmem((2 * IMPORTS + 1, *half), BF16),
        theirs_v=vmem((2 * IMPORTS + 1, *half), BF16),
        tab=vmem((2, NY * NZ, *half), F32),
        y1out=vmem((2, 2, NZ // 2, *half), BF16), y1in=vmem((2, 2, NZ // 2, *half), BF16),
        y2out=vmem((2, 2, NZ, *half), BF16), y2in=vmem((2, 2, NZ, *half), BF16),
        acc=vmem((2, NZ, *half), F32), tz=vmem((2, NZ, *half), BF16),
        rz=vmem((2, NZ - 1, *half), BF16),
        wout=vmem((REACH, TOK, 2 * D), BF16), win=vmem((REACH, TOK, 2 * D), BF16),
        coll=vmem((TOK, 2 * D), F32),
    )
    four, window, line, pairs = dma((4,)), dma((REACH,)), dma((2, NZ - 1)), dma((3, 2))
    two, steps = dma((2,)), dma((2, 4))
    semaphores = dict(
        small=dma((3,)), here=four, hsend=pairs, hrecv=pairs, qsend=pairs, qrecv=pairs,
        wsend=window, wrecv=window, zsend=line, zrecv=line, xsend=two, xrecv=two,
        ysend=steps, yrecv=steps, dsend=four, drecv=four, dlocal=dma,
        v2send=window, v2recv=window, z2send=line, z2recv=line, x2send=two, x2recv=two,
        y2send=steps, y2recv=steps, h2send=pairs, h2recv=pairs,
    )
    return buffers, semaphores


BUFFERS, SEMAPHORES = (tuple(d) for d in memory())


def per_device(queries, keys, values, output_gradient, file_starts, file_imports, header_lens):
    hbm = pl.BlockSpec(memory_space=pl.ANY)
    vmem = pl.BlockSpec(memory_space=pltpu.VMEM)
    buffers, semaphores = memory()
    dq, dk, dv = pl.pallas_call(
        fused_kernel,
        out_shape=(
            jax.ShapeDtypeStruct((BLK, GROUPS * HEADS * D), BF16),
            jax.ShapeDtypeStruct((BLK, GROUPS * D), F32),
            jax.ShapeDtypeStruct((BLK, GROUPS * D), F32),
        ),
        in_specs=[hbm] * 7,
        out_specs=(hbm, vmem, vmem),
        scratch_shapes=[*buffers.values(), *semaphores.values()],
        compiler_params=pltpu.CompilerParams(
            collective_id=0, has_side_effects=True, vmem_limit_bytes=VMEM_LIMIT
        ),
        name="attention_backward",
    )(
        file_starts, file_imports.T, header_lens, queries, keys, values, output_gradient
    )
    return dq.astype(F32), dk, dv


def solution(mesh):
    split = Mesh(mesh.devices.reshape(NX, NY, NZ, 2, 2), AXES)
    placed = P(AXES, None)
    return jax.shard_map(
        per_device,
        mesh=split,
        in_specs=(placed, placed, placed, placed, P(), P(), P()),
        out_specs=(placed, placed, placed),
        check_vma=False,
    )
```

```python
import math

import jax
import jax.numpy as jnp
from jax import lax
from jax.experimental import pallas as pl
from jax.experimental.pallas import tpu as pltpu
from jax.sharding import Mesh
from jax.sharding import PartitionSpec as P

WIN = 1024
HDR = 64
TOK = 256
BLK = 64
D = 128
HEADS = 12
GROUPS = 4
REACH = WIN // TOK
QB = TOK // BLK
IMPORTS = 4
FILES = 33
VMEM_LIMIT = 60 * 2**20
NX, NY, NZ = 2, 4, 8
NCTX = NX * NY * NZ
WROWS = WIN + BLK
HROWS = IMPORTS * HDR
ROWS = WROWS + HROWS
CHUNK_HEADS = 4
CHUNKS = HEADS // CHUNK_HEADS
CW = CHUNK_HEADS * BLK
COLS = HEADS * BLK
SCALE = 1.0 / math.sqrt(D)
LOG2E = 1.4426950408889634
HIDDEN = -1e30
MESH = pl.DeviceIdType.MESH
F32 = jnp.float32
BF16 = jnp.bfloat16
AXES = ("ctx_0", "ctx_1", "ctx_2", "head_0", "head_1")


def position():
    return tuple(lax.axis_index(a) for a in AXES)


def ctx_of(xh, y, z):
    return xh * (NY * NZ) + y * NZ + z


def ctx_shifted(xh, y, z, step):
    c = lax.rem(ctx_of(xh, y, z) + (NCTX + step), NCTX)
    return {
        "ctx_0": lax.div(c, NY * NZ),
        "ctx_1": lax.rem(lax.div(c, NZ), NY),
        "ctx_2": lax.rem(c, NZ),
    }


def head_peer(xl, co, d):
    pxl = 1 - xl if d & 2 else xl
    pco = 1 - co if d & 1 else co
    return {"head_0": pxl, "head_1": pco}, pxl * 2 + pco


def greet(peers):
    barrier = pltpu.get_barrier_semaphore()
    for peer in peers:
        pl.semaphore_signal(barrier, inc=1, device_id=peer, device_id_type=MESH)
    pl.semaphore_wait(barrier, len(peers))


def remote(src, dst, send, recv, peer):
    return pltpu.make_async_remote_copy(
        src_ref=src, dst_ref=dst, send_sem=send, recv_sem=recv, device_id=peer, device_id_type=MESH
    )


def all_peers(xh, y, z, xl, co):
    peers = [head_peer(xl, co, d)[0] for d in (1, 2, 3)]
    peers += [{"ctx_2": lax.rem(z + d, NZ)} for d in range(1, NZ)]
    peers += [{"ctx_1": n} for n in y_neighbours(y)]
    peers += [{"ctx_0": 1 - xh}]
    peers += [ctx_shifted(xh, y, z, 1), ctx_shifted(xh, y, z, -1)]
    return peers


def rows(start, size):
    return pl.ds(pl.multiple_of(start, size), size)


def y_neighbours(y):
    near = y + 1 - 2 * lax.rem(y, 2)
    return near, NY - 1 - y


def file_at(starts, place):
    count = jnp.int32(-1)
    for f in range(starts.shape[0]):
        count = count + jnp.where(starts[f] <= place, 1, 0)
    return count


def header_blocks(starts, imports, c):
    lower = file_at(starts, c * TOK)
    upper = file_at(starts, c * TOK + TOK - 1)
    blocks = []
    for file in (lower, upper):
        for m in range(IMPORTS):
            g = imports[m, file]
            blocks.append((g >= 0, lax.div(starts[jnp.maximum(g, 0)], TOK)))
    return lower, upper, blocks


def own_header_offset(starts, base):
    offset = jnp.int32(0)
    for f in range(starts.shape[0]):
        at = starts[f] - base
        offset = offset + jnp.where((at >= 0) & (at < TOK), at, 0)
    return offset


def fetch(pairs, sems):
    copies = [pltpu.make_async_copy(src, dst, sems.at[n]) for n, (src, dst) in enumerate(pairs)]
    for copy in copies:
        copy.start()
    return copies


def fold8(x, op):
    out = x[0:8]
    for r in range(8, x.shape[0], 8):
        out = op(out, x[r:r + 8])
    return out


def rows_at(start, size, multiple):
    return pl.ds(pl.multiple_of(start, multiple), size)


def receive_inputs(q, k, v, do, small, tables, b, sems):
    starts, imports = tables
    xh, y, z, xl, co = position()
    me = xl * 2 + co
    c = ctx_of(xh, y, z)
    width = HEADS * D
    own = REACH * TOK
    kvwin, slots = b["kvwin"], (b["slots_k"], b["slots_v"])
    here = fetch(
        (
            (k.at[:, rows(me * D, D)], kvwin.at[rows(own + me * BLK, BLK), pl.ds(0, D)]),
            (v.at[:, rows(me * D, D)], kvwin.at[rows(own + me * BLK, BLK), pl.ds(D, D)]),
            (q.at[:, rows(me * width, width)], b["q"].at[rows(me * BLK, BLK), :]),
            (do.at[:, rows(me * width, width)], b["do"].at[rows(me * BLK, BLK), :]),
        ),
        sems["here"],
    )
    greet(all_peers(xh, y, z, xl, co))
    kv_copies, q_copies = [], []
    for d in (2, 3, 1):
        peer, a = head_peer(xl, co, d)
        for n, src in enumerate((k, v)):
            kv_copies.append(remote(
                src.at[:, rows(a * D, D)],
                kvwin.at[rows(own + me * BLK, BLK), pl.ds(n * D, D)],
                sems["hsend"].at[d - 1, n], sems["hrecv"].at[d - 1, n], peer,
            ))
            kv_copies[-1].start()
    for d in (2, 3, 1):
        peer, a = head_peer(xl, co, d)
        for n, (src, dst) in enumerate(((q, b["q"]), (do, b["do"]))):
            q_copies.append(remote(
                src.at[:, rows(a * width, width)], dst.at[rows(me * BLK, BLK), :],
                sems["qsend"].at[d - 1, n], sems["qrecv"].at[d - 1, n], peer,
            ))
            q_copies[-1].start()
    for copy in small:
        copy.wait()
    offset = own_header_offset(starts, c * TOK)
    for copy in here[:2]:
        copy.wait()
    for copy in kv_copies:
        copy.wait_recv()

    forward = ctx_shifted(xh, y, z, 1)
    w_copies = [
        remote(
            kvwin.at[pl.ds((REACH - s) * TOK, TOK), :],
            kvwin.at[pl.ds((REACH - 1 - s) * TOK, TOK), :],
            sems["wsend"].at[s], sems["wrecv"].at[s], forward,
        )
        for s in range(REACH)
    ]
    w_copies[0].start()
    header = jnp.zeros((HDR, 2 * D), F32)
    for n in range(QB):
        keep = jnp.where(offset == n * BLK, 1.0, 0.0)
        header = header + kvwin[own + n * BLK:own + (n + 1) * BLK, :].astype(F32) * keep
    line = y * NZ + z
    for n in range(2):
        slots[n][line] = header[:, n * D:(n + 1) * D].astype(BF16)
    z_copies = ([], [])
    for n in range(2):
        for d in (1, 7, 2, 6, 3, 5, 4):
            part = slots[n].at[line]
            z_copies[n].append(remote(
                part, part, sems["zsend"].at[n, d - 1], sems["zrecv"].at[n, d - 1],
                {"ctx_2": lax.rem(z + d, NZ)},
            ))
            z_copies[n][-1].start()
    near, other = y_neighbours(y)
    near_copies, far_copies, x_copies = ([], []), ([], []), []

    def to_neighbours(n):
        for copy in z_copies[n]:
            copy.wait_recv()
        for d, to in enumerate((near, other)):
            part = slots[n].at[rows(y * NZ, NZ)]
            near_copies[n].append(remote(
                part, part, sems["ysend"].at[n, d], sems["yrecv"].at[n, d], {"ctx_1": to}
            ))
            near_copies[n][-1].start()

    def to_opposite(n):
        for d, (came, to) in enumerate(((near, other), (other, near))):
            near_copies[n][d].wait_recv()
            part = slots[n].at[rows(came * NZ + d * (NZ // 2), NZ // 2)]
            far_copies[n].append(remote(
                part, part, sems["ysend"].at[n, 2 + d], sems["yrecv"].at[n, 2 + d],
                {"ctx_1": to},
            ))
            far_copies[n][-1].start()

    def to_other_half(n):
        for copy in far_copies[n]:
            copy.wait_recv()
        for m, (_, shard) in enumerate(wanted):
            b["picked"][n, m] = slots[n][lax.rem(shard, NY * NZ)]
        x_copies.append(remote(
            b["picked"].at[n], b["far"].at[n], sems["xsend"].at[n], sems["xrecv"].at[n],
            {"ctx_0": 1 - xh},
        ))
        x_copies[-1].start()

    _, _, wanted = header_blocks(starts, imports, ctx_of(1 - xh, y, z))
    to_neighbours(0)
    w_copies[0].wait_recv()
    w_copies[1].start()
    to_neighbours(1)
    to_opposite(0)
    to_opposite(1)
    w_copies[1].wait_recv()
    w_copies[2].start()
    to_other_half(0)
    to_other_half(1)
    w_copies[2].wait_recv()
    w_copies[3].start()
    for copy in q_copies:
        copy.wait_recv()
    for copy in here[2:]:
        copy.wait()
    w_copies[3].wait_recv()
    for copy in x_copies:
        copy.wait_recv()
    y_copies = near_copies[0] + near_copies[1] + far_copies[0] + far_copies[1]
    return kv_copies + q_copies + z_copies[0] + z_copies[1] + w_copies + y_copies + x_copies


def attend_block(qb, starts, imports, lens, b):
    xh, y, z, _, _ = position()
    base = ctx_of(xh, y, z) * TOK
    place = base + qb * BLK
    lower = file_at(starts, base)
    file = file_at(starts, place)
    begin = starts[file]
    kc, vc, bias = b["kc"].at[qb], b["vc"], b["bias"]
    qs, dos = b["qs"].at[qb], b["dos"].at[qb]
    p_ref, ds_ref = b["hp"], b["hds"].at[qb]
    step = 64
    kc[0:WROWS, :] = b["kvwin"][rows_at(qb * BLK, WROWS, BLK), 0:D]
    vc[0:WROWS, :] = b["kvwin"][rows_at(qb * BLK, WROWS, BLK), D:2 * D]
    key_place = lax.broadcasted_iota(jnp.int32, (WROWS, D), 0) + (place - WIN)
    bias[0:WROWS, :] = jnp.where(key_place >= begin, 0.0, HIDDEN)
    offsets = lax.broadcasted_iota(jnp.int32, (HDR, D), 0)
    for m in range(IMPORTS):
        g = imports[m, file]
        known = jnp.maximum(g, 0)
        length = jnp.where(g >= 0, lens[known], 0)
        here = pl.ds(WROWS + m * HDR, HDR)
        shard = lax.div(starts[known], TOK)
        at = lax.rem(shard, NY * NZ)
        which = jnp.where(file == lower, 0, IMPORTS) + m
        same = jnp.full((HDR, D), lax.div(shard, NY * NZ)) == xh
        for n, (dst, slots) in enumerate(((kc, b["slots_k"]), (vc, b["slots_v"]))):
            near = slots[at].astype(F32)
            dst[here, :] = jnp.where(same, near, b["far"][n, which].astype(F32)).astype(BF16)
        bias[here, :] = jnp.where(offsets < length, 0.0, HIDDEN)
    for h in range(HEADS):
        qs[h * BLK:(h + 1) * BLK, :] = b["q"][rows(qb * BLK, BLK), h * D:(h + 1) * D]
        dos[h * BLK:(h + 1) * BLK, :] = b["do"][rows(qb * BLK, BLK), h * D:(h + 1) * D]

    t = lax.broadcasted_iota(jnp.int32, (BLK, CW), 0)
    p_at = lax.broadcasted_iota(jnp.int32, (BLK, CW), 1) % BLK
    nt = (((1,), (1,)), ((), ()))
    for chunk in range(CHUNKS):
        cols = slice(chunk * CW, (chunk + 1) * CW)
        s_ref, dp_ref = b["s"].at[qb, chunk], b["dp"].at[qb, chunk]
        s_ref[...] = lax.dot_general(kc[...], qs[cols, :], nt, preferred_element_type=F32)
        dp_ref[...] = lax.dot_general(vc[...], dos[cols, :], nt, preferred_element_type=F32)
        top = None
        for r in range(0, ROWS, step):
            s = s_ref[r:r + step, :] + jnp.concatenate([bias[r:r + step, :]] * (CW // D), axis=1)
            if r == 0:
                s = jnp.where(t > p_at, s, HIDDEN)
            if r == WIN:
                s = jnp.where(t <= p_at, s, HIDDEN)
            s_ref[r:r + step, :] = s
            part = fold8(s, jnp.maximum)
            top = part if top is None else jnp.maximum(top, part)
        top = jnp.max(top, axis=0, keepdims=True)
        total = jnp.zeros((8, CW), F32)
        centre = jnp.zeros((8, CW), F32)
        for r in range(0, ROWS, step):
            e = jnp.exp2((s_ref[r:r + step, :] - top) * (SCALE * LOG2E))
            s_ref[r:r + step, :] = e
            total = total + fold8(e, jnp.add)
            centre = centre + fold8(e * dp_ref[r:r + step, :], jnp.add)
        inverse = 1.0 / jnp.sum(total, axis=0, keepdims=True)
        centre = jnp.sum(centre, axis=0, keepdims=True) * inverse
        b["stat"][qb, chunk, 0:1, :] = inverse
        b["stat"][qb, chunk, 1:2, :] = centre
        for r in range(WROWS, ROWS, step):
            w = s_ref[r:r + step, :] * inverse
            here = slice(r - WROWS, r - WROWS + step)
            p_ref[here, cols] = w.astype(BF16)
            ds_ref[here, cols] = (w * (dp_ref[r:r + step, :] - centre)).astype(BF16)
    dv = jnp.dot(p_ref[...], dos[...], preferred_element_type=F32)
    dk = jnp.dot(ds_ref[...], qs[...], preferred_element_type=F32) * SCALE
    first = jnp.where(file == lower, 1.0, 0.0)
    for n, share in enumerate((first, 1.0 - first)):
        part = slice(n * HROWS, (n + 1) * HROWS)
        b["hacc"][part, 0:D] += dk * share
        b["hacc"][part, D:2 * D] += dv * share


def window_block(qb, b):
    p_ref, ds_ref = b["p"], b["ds"].at[qb]
    step = 64
    for chunk in range(CHUNKS):
        cols = slice(chunk * CW, (chunk + 1) * CW)
        s_ref, dp_ref = b["s"].at[qb, chunk], b["dp"].at[qb, chunk]
        inverse = b["stat"][qb, chunk, 0:1, :]
        centre = b["stat"][qb, chunk, 1:2, :]
        for r in range(0, WROWS, step):
            w = s_ref[r:r + step, :] * inverse
            p_ref[r:r + step, cols] = w.astype(BF16)
            ds_ref[r:r + step, cols] = (w * (dp_ref[r:r + step, :] - centre)).astype(BF16)
    window = rows_at(qb * BLK, WROWS, BLK)
    dkv = b["dkv"]
    dkv[window, 0:D] += jnp.dot(ds_ref[...], b["qs"][qb], preferred_element_type=F32) * SCALE
    dkv[window, D:2 * D] += jnp.dot(p_ref[...], b["dos"][qb], preferred_element_type=F32)


def query_block(qb, b):
    kc, ds_ref, hds = b["kc"].at[qb], b["ds"].at[qb], b["hds"].at[qb]
    tn = (((0,), (0,)), ((), ()))
    dqt = lax.dot_general(kc[0:WROWS, :], ds_ref[...], tn, preferred_element_type=F32)
    dqt = dqt + lax.dot_general(kc[WROWS:, :], hds[...], tn, preferred_element_type=F32)
    dq = (dqt.T * SCALE).astype(BF16)
    for h in range(HEADS):
        b["dq"][qb, :, h * D:(h + 1) * D] = dq[h * BLK:(h + 1) * BLK]


def fused_kernel(starts_hbm, imports_hbm, lens_hbm, q, k, v, do, dq_out, dk_out, dv_out, *scratch):
    b = dict(zip(BUFFERS, scratch))
    sems = dict(zip(SEMAPHORES, scratch[len(BUFFERS):]))
    starts, imports, lens = b["starts"], b["imports"], b["lens"]
    xh, y, z, xl, co = position()
    me = xl * 2 + co
    c = ctx_of(xh, y, z)
    width = HEADS * D
    slots = 2 * IMPORTS
    dkv, tab, hacc = b["dkv"], b["tab"], b["hacc"]
    mine, theirs = b["mine"], (b["theirs_k"], b["theirs_v"])
    small = fetch(
        ((starts_hbm, starts), (imports_hbm, imports), (lens_hbm, lens)), sems["small"]
    )
    for n in range(2):
        mine[n, slots] = jnp.zeros((HDR, D), BF16)
        theirs[n][slots] = jnp.zeros((HDR, D), BF16)
    dkv[...] = jnp.zeros_like(dkv)
    hacc[...] = jnp.zeros_like(hacc)
    sent = receive_inputs(q, k, v, do, small, (starts, imports), b, sems)
    offset = own_header_offset(starts, c * TOK)

    def dq_copy(to):
        return remote(
            b["dq"].at[to], dq_out.at[:, rows(me * width, width)],
            sems["dsend"].at[to], sems["drecv"].at[me],
            {"head_0": lax.div(to, 2), "head_1": lax.rem(to, 2)},
        )

    own_dq = pltpu.make_async_copy(
        b["dq"].at[me], dq_out.at[:, rows(me * width, width)], sems["dlocal"]
    )

    def block_of(i):
        turn = jnp.where(i == 3, 0, jnp.where(i == 2, 1, i + 2))
        return lax.rem(me + turn, QB)

    def first_half(i, carry):
        attend_block(i, starts, imports, lens, b)
        return carry

    def second_half(i, carry):
        window_block(i, b)
        return carry

    def third_part(i, carry):
        qb = block_of(i)
        query_block(qb, b)

        @pl.when(i < 3)
        def _():
            dq_copy(qb).start()

        return carry

    lax.fori_loop(0, QB, first_half, 0)
    halves = (slice(0, D), slice(D, 2 * D))
    x_copies = []
    for n, half in enumerate(halves):
        for m in range(slots):
            mine[n, m] = hacc[m * HDR:(m + 1) * HDR, half].astype(BF16)
        x_copies.append(remote(
            mine.at[n, pl.ds(0, slots)], theirs[n].at[pl.ds(0, slots)],
            sems["x2send"].at[n], sems["x2recv"].at[n], {"ctx_0": 1 - xh},
        ))
        x_copies[-1].start()

    back = ctx_shifted(xh, y, z, -1)
    wout, win = b["wout"], b["win"]
    w_copies = [
        remote(wout.at[s], win.at[s], sems["v2send"].at[s], sems["v2recv"].at[s], back)
        for s in range(REACH)
    ]

    def pass_on(s):
        w_copies[s - 1].wait_recv()
        wout[s] = (win[s - 1].astype(F32) + dkv[s * TOK:(s + 1) * TOK, :]).astype(BF16)
        w_copies[s].start()

    places = []
    for shard_at in (c, ctx_of(1 - xh, y, z)):
        _, _, blocks = header_blocks(starts, imports, shard_at)
        places += [blocks[0:IMPORTS], blocks[IMPORTS:]]

    def find(blocks, first, shard):
        at = jnp.int32(slots)
        for m, (used, block) in enumerate(blocks):
            at = jnp.where(used & (block == shard), first + m, at)
        return at

    near, other = y_neighbours(y)
    across = 2 * lax.rem(lax.div(y, 2) + 1, 2) + lax.rem(y, 2)
    y1out, y1in, y2out, y2in = b["y1out"], b["y1in"], b["y2out"], b["y2in"]
    acc, tz, rz, coll = b["acc"], b["tz"], b["rz"], b["coll"]
    near_copies, far_copies, z_copies = ([], []), ([], []), ([], [])
    middle = NZ // 2

    def to_opposite(n):
        x_copies[n].wait_recv()

        def one_slot(i, carry):
            shard = xh * (NY * NZ) + i
            total = None
            for buffer, lists in ((mine.at[n], places[0:2]), (theirs[n], places[2:4])):
                for side in range(2):
                    part = buffer[find(lists[side], side * IMPORTS, shard)].astype(F32)
                    total = part if total is None else total + part
            tab[n, i] = total
            return carry

        lax.fori_loop(0, NY * NZ, one_slot, 0)
        for d, to in enumerate((near, other)):
            y1out[n, d] = tab[n, rows(across * NZ + d * middle, middle)].astype(BF16)
            far_copies[n].append(remote(
                y1out.at[n, d], y1in.at[n, d],
                sems["y2send"].at[n, d], sems["y2recv"].at[n, d], {"ctx_1": to},
            ))
            far_copies[n][-1].start()

    def to_neighbours(n):
        for d, to in enumerate((other, near)):
            far_copies[n][d].wait_recv()
            add, rest = d * middle, (1 - d) * middle
            y2out[n, d, pl.ds(add, middle)] = (
                tab[n, rows(to * NZ + add, middle)] + y1in[n, d].astype(F32)
            ).astype(BF16)
            y2out[n, d, pl.ds(rest, middle)] = tab[n, rows(to * NZ + rest, middle)].astype(BF16)
            near_copies[n].append(remote(
                y2out.at[n, d], y2in.at[n, d],
                sems["y2send"].at[n, 2 + d], sems["y2recv"].at[n, 2 + d], {"ctx_1": to},
            ))
            near_copies[n][-1].start()

    def to_owners(n):
        for copy in near_copies[n]:
            copy.wait_recv()
        acc[n] = (
            tab[n, rows(y * NZ, NZ)] + y2in[n, 0].astype(F32) + y2in[n, 1].astype(F32)
        )
        tz[n] = acc[n].astype(BF16)
        for d in (4, 3, 5, 2, 6, 1, 7):
            to = lax.rem(z + d, NZ)
            z_copies[n].append(remote(
                tz.at[n, to], rz.at[n, d - 1],
                sems["z2send"].at[n, d - 1], sems["z2recv"].at[n, d - 1], {"ctx_2": to},
            ))
            z_copies[n][-1].start()

    lax.fori_loop(0, QB, second_half, 0)
    wout[0] = dkv[0:TOK, :].astype(BF16)
    w_copies[0].start()
    to_opposite(0)
    to_opposite(1)
    lax.fori_loop(0, QB // 2, third_part, 0)
    to_neighbours(0)
    pass_on(1)
    to_neighbours(1)
    lax.fori_loop(QB // 2, QB, third_part, 0)
    own_dq.start()
    to_owners(0)
    pass_on(2)
    to_owners(1)
    w_copies[2].wait_recv()
    last_copies = []
    for n, half in enumerate(halves):
        wout[3, :, half] = (
            win[2, :, half].astype(F32) + dkv[3 * TOK:4 * TOK, half]
        ).astype(BF16)
        lanes = pl.ds(n * D, D)
        last_copies.append(remote(
            wout.at[3, :, lanes], win.at[3, :, lanes],
            sems["v2send"].at[3 + n], sems["v2recv"].at[3 + n], back,
        ))
        last_copies[-1].start()
    h_copies = []
    for n, (half, dst) in enumerate(zip(halves, (dk_out, dv_out))):
        header = acc[n, z]
        for copy in z_copies[n]:
            copy.wait_recv()
        for d in range(NZ - 1):
            header = header + rz[n, d].astype(F32)
        last_copies[n].wait_recv()
        for block in range(QB):
            part = slice(block * BLK, (block + 1) * BLK)
            keep = jnp.where(offset == block * BLK, 1.0, 0.0)
            at = REACH * TOK + block * BLK
            coll[part, half] = (
                dkv[at:at + BLK, half] + win[3, part, half].astype(F32) + header * keep
            )
        for d in (2, 3, 1):
            peer, a = head_peer(xl, co, d)
            h_copies.append(remote(
                coll.at[rows(a * BLK, BLK), pl.ds(n * D, D)], dst.at[:, rows(me * D, D)],
                sems["h2send"].at[d - 1, n], sems["h2recv"].at[d - 1, n], peer,
            ))
            h_copies[-1].start()
        dst[:, rows(me * D, D)] = coll[rows(me * BLK, BLK), half]
    own_dq.wait()
    for d in (1, 2, 3):
        _, a = head_peer(xl, co, d)
        remote(
            b["dq"].at[a], dq_out.at[:, rows(a * width, width)],
            sems["dsend"].at[a], sems["drecv"].at[a],
            {"head_0": lax.div(a, 2), "head_1": lax.rem(a, 2)},
        ).wait()
    for copy in h_copies:
        copy.wait_recv()
    for pair in (near_copies, far_copies, z_copies):
        sent = sent + pair[0] + pair[1]
    for copy in sent + w_copies[:3] + last_copies + x_copies + h_copies:
        copy.wait_send()


def memory():
    vmem, smem = pltpu.VMEM, pltpu.SMEM
    dma = pltpu.SemaphoreType.DMA
    half = (HDR, D)
    buffers = dict(
        starts=smem((FILES,), jnp.int32), imports=smem((IMPORTS, FILES), jnp.int32),
        lens=smem((FILES,), jnp.int32),
        q=vmem((TOK, HEADS * D), BF16), do=vmem((TOK, HEADS * D), BF16),
        kvwin=vmem(((REACH + 1) * TOK, 2 * D), BF16),
        slots_k=vmem((NY * NZ, *half), BF16), slots_v=vmem((NY * NZ, *half), BF16),
        picked=vmem((2, 2 * IMPORTS, HDR, D), BF16), far=vmem((2, 2 * IMPORTS, HDR, D), BF16),
        kc=vmem((QB, ROWS, D), BF16), vc=vmem((ROWS, D), BF16), bias=vmem((ROWS, D), F32),
        qs=vmem((QB, COLS, D), BF16), dos=vmem((QB, COLS, D), BF16),
        s=vmem((QB, CHUNKS, ROWS, CW), F32), dp=vmem((QB, CHUNKS, ROWS, CW), F32),
        stat=vmem((QB, CHUNKS, 8, CW), F32),
        p=vmem((WROWS, COLS), BF16), ds=vmem((QB, WROWS, COLS), BF16),
        hp=vmem((HROWS, COLS), BF16), hds=vmem((QB, HROWS, COLS), BF16),
        hacc=vmem((2 * HROWS, 2 * D), F32),
        dq=vmem((QB, BLK, HEADS * D), BF16),
        dkv=vmem(((REACH + 1) * TOK, 2 * D), F32),
        mine=vmem((2, 2 * IMPORTS + 1, *half), BF16),
        theirs_k=vmem((2 * IMPORTS + 1, *half), BF16),
        theirs_v=vmem((2 * IMPORTS + 1, *half), BF16),
        tab=vmem((2, NY * NZ, *half), F32),
        y1out=vmem((2, 2, NZ // 2, *half), BF16), y1in=vmem((2, 2, NZ // 2, *half), BF16),
        y2out=vmem((2, 2, NZ, *half), BF16), y2in=vmem((2, 2, NZ, *half), BF16),
        acc=vmem((2, NZ, *half), F32), tz=vmem((2, NZ, *half), BF16),
        rz=vmem((2, NZ - 1, *half), BF16),
        wout=vmem((REACH, TOK, 2 * D), BF16), win=vmem((REACH, TOK, 2 * D), BF16),
        coll=vmem((TOK, 2 * D), F32),
    )
    four, window, line, pairs = dma((4,)), dma((REACH,)), dma((2, NZ - 1)), dma((3, 2))
    two, steps = dma((2,)), dma((2, 4))
    semaphores = dict(
        small=dma((3,)), here=four, hsend=pairs, hrecv=pairs, qsend=pairs, qrecv=pairs,
        wsend=window, wrecv=window, zsend=line, zrecv=line, xsend=two, xrecv=two,
        ysend=steps, yrecv=steps, dsend=four, drecv=four, dlocal=dma,
        v2send=dma((REACH + 1,)), v2recv=dma((REACH + 1,)), z2send=line, z2recv=line, x2send=two, x2recv=two,
        y2send=steps, y2recv=steps, h2send=pairs, h2recv=pairs,
    )
    return buffers, semaphores


BUFFERS, SEMAPHORES = (tuple(d) for d in memory())


def per_device(queries, keys, values, output_gradient, file_starts, file_imports, header_lens):
    hbm = pl.BlockSpec(memory_space=pl.ANY)
    vmem = pl.BlockSpec(memory_space=pltpu.VMEM)
    buffers, semaphores = memory()
    dq, dk, dv = pl.pallas_call(
        fused_kernel,
        out_shape=(
            jax.ShapeDtypeStruct((BLK, GROUPS * HEADS * D), BF16),
            jax.ShapeDtypeStruct((BLK, GROUPS * D), F32),
            jax.ShapeDtypeStruct((BLK, GROUPS * D), F32),
        ),
        in_specs=[hbm] * 7,
        out_specs=(hbm, vmem, vmem),
        scratch_shapes=[*buffers.values(), *semaphores.values()],
        compiler_params=pltpu.CompilerParams(
            collective_id=0, has_side_effects=True, vmem_limit_bytes=VMEM_LIMIT
        ),
        name="attention_backward",
    )(
        file_starts, file_imports.T, header_lens, queries, keys, values, output_gradient
    )
    return dq.astype(F32), dk, dv


def solution(mesh):
    split = Mesh(mesh.devices.reshape(NX, NY, NZ, 2, 2), AXES)
    placed = P(AXES, None)
    return jax.shard_map(
        per_device,
        mesh=split,
        in_specs=(placed, placed, placed, placed, P(), P(), P()),
        out_specs=(placed, placed, placed),
        check_vma=False,
    )
```
